32 devices in a mesh: mp: 2 (over core), dp: 16 (over z, y, x).
Axes of the slice: x: 2, y: 2, z: 4, core: 2. Of those that a mesh axis runs over, the one named last changes fastest.
Arguments:
- tokens: bfloat16 [131072, 512], P('dp'), may hold values from -6 to 6
- norm1_gain: float32 [512], replicated, may hold values from 0.5 to 1.5
- norm1_bias: float32 [512], replicated, may hold values from -1.5 to 1.5
- w_query: bfloat16 [512, 512], P(None, 'mp'), may hold values from -0.25 to 0.25
- b_query: float32 [512], P('mp'), may hold values from -2.5 to 2.5
- w_key: bfloat16 [512, 512], P(None, 'mp'), may hold values from -0.25 to 0.25
- b_key: float32 [512], P('mp'), may hold values from -2.5 to 2.5
- w_value: bfloat16 [512, 512], P(None, 'mp'), may hold values from -0.25 to 0.25
- b_value: float32 [512], P('mp'), may hold values from -2.5 to 2.5
- w_out: bfloat16 [512, 512], P('mp'), may hold values from -2 to 2
- b_out: float32 [512], replicated, may hold values from -1.5 to 1.5
- norm2_gain: float32 [512], replicated, may hold values from 0.5 to 1.5
- norm2_bias: float32 [512], replicated, may hold values from -1.5 to 1.5
- w_up: bfloat16 [512, 2048], P(None, 'mp'), may hold values from -0.25 to 0.25
- b_up: float32 [2048], P('mp'), may hold values from -2.5 to 2.5
- w_down: bfloat16 [2048, 512], P('mp'), may hold values from -0.125 to 0.125
- b_down: float32 [512], replicated, may hold values from -1.5 to 1.5
- cotangent: bfloat16 [131072, 512], P('dp'), may hold values from -6 to 6
Outputs:
- layer_out: bfloat16 [131072, 512], P('dp')
- tokens_grad: bfloat16 [131072, 512], P('dp')
- norm1_gain_grad: float32 [512], replicated
- norm1_bias_grad: float32 [512], replicated
- w_query_grad: float32 [512, 512], P(None, 'mp')
- b_query_grad: float32 [512], P('mp')
- w_key_grad: float32 [512, 512], P(None, 'mp')
- b_key_grad: float32 [512], P('mp')
- w_value_grad: float32 [512, 512], P(None, 'mp')
- b_value_grad: float32 [512], P('mp')
- w_out_grad: float32 [512, 512], P('mp')
- b_out_grad: float32 [512], replicated
- norm2_gain_grad: float32 [512], replicated
- norm2_bias_grad: float32 [512], replicated
- w_up_grad: float32 [512, 2048], P(None, 'mp')
- b_up_grad: float32 [2048], P('mp')
- w_down_grad: float32 [2048, 512], P('mp')
- b_down_grad: float32 [512], replicated
The draws below stay inside these ranges and needn't reach their ends.
All inputs are finite; a program needn't handle non-finite values.
Results may differ from the reference program's by a relative error of at most 0.025.
Values may be sent and summed in bfloat16 or wider, within the bound.
No kernel may reach another device: no remote copies, remote signals or barrier semaphores. Data moves between devices by JAX's collectives and lax.ppermute only.
A program may use at most 384 MiB of HBM per device.

```python
import math
import jax
import jax.numpy as jnp
from jax import lax

D = 512
HEADS = 8
HEAD_DIM = 64
FF = 2048
SEQ_LEN = 256
TOKENS = 131072


def block_levels(rng, shape, cuts, smallest, largest):
    def one(dim, blocks):
        draws = jax.random.uniform(jax.random.fold_in(jax.random.fold_in(rng, 6), dim), (blocks,), jnp.float32, smallest / len(cuts), largest / len(cuts))
        return jnp.repeat(jnp.exp(draws), shape[dim] // blocks).reshape((-1,) + (1,) * (len(shape) - dim - 1))

    level = one(*cuts[0])
    for cut in cuts[1:]:
        level = level * one(*cut)
    return level


def scatter_about(rng, dims, scale, bound, pieces=(), dtype=jnp.bfloat16):
    array = jax.random.normal(rng, dims, jnp.float32) * scale
    if len(pieces) > 0:
        array = block_levels(rng, dims, pieces, -0.22, 0.18) * array
    return jnp.clip(array, min=-bound, max=bound).astype(dtype)


def setup_inputs(seed: int = 0) -> dict:
    splits = jax.random.split(jax.random.key(seed), 19)
    tokens = scatter_about(splits[0], (TOKENS, D), 1.0, 6.0, ((0, 16),))
    norm1_gain = jnp.clip(1.0 + 0.1 * jax.random.normal(splits[1], (D,), jnp.float32), 0.5, 1.5)
    norm1_bias = scatter_about(splits[2], (D,), 0.3, 1.5, (), jnp.float32)
    w_query = scatter_about(splits[3], (D, D), D ** -0.5, 0.25, ((1, 2),))
    b_query = scatter_about(splits[4], (D,), 0.5, 2.5, ((0, 2),), jnp.float32)
    w_key = scatter_about(splits[5], (D, D), D ** -0.5, 0.25, ((1, 2),))
    b_key = scatter_about(splits[6], (D,), 0.5, 2.5, ((0, 2),), jnp.float32)
    w_value = scatter_about(splits[7], (D, D), D ** -0.5, 0.25, ((1, 2),))
    b_value = scatter_about(splits[8], (D,), 0.5, 2.5, ((0, 2),), jnp.float32)
    w_out = scatter_about(splits[9], (D, D), (D // 64) ** -0.5, 2.0, ((0, 2),))
    b_out = scatter_about(splits[10], (D,), 0.3, 1.5, (), jnp.float32)
    norm2_gain = jnp.clip(1.0 + 0.1 * jax.random.normal(splits[11], (D,), jnp.float32), 0.5, 1.5)
    norm2_bias = scatter_about(splits[12], (D,), 0.3, 1.5, (), jnp.float32)
    w_up = scatter_about(splits[13], (D, FF), D ** -0.5, 0.25, ((1, 2),))
    b_up = scatter_about(splits[14], (FF,), 0.5, 2.5, ((0, 2),), jnp.float32)
    w_down = scatter_about(splits[15], (FF, D), FF ** -0.5, 0.125, ((0, 2),))
    b_down = scatter_about(splits[16], (D,), 0.3, 1.5, (), jnp.float32)
    cotangent = scatter_about(splits[17], (TOKENS, D), 1.0, 6.0, ((0, 16),))
    return dict(tokens=tokens, norm1_gain=norm1_gain, norm1_bias=norm1_bias, w_query=w_query, b_query=b_query, w_key=w_key, b_key=b_key, w_value=w_value, b_value=b_value, w_out=w_out, b_out=b_out, norm2_gain=norm2_gain, norm2_bias=norm2_bias, w_up=w_up, b_up=b_up, w_down=w_down, b_down=b_down, cotangent=cotangent)


@jax.custom_vjp
def low(v):
    return lax.optimization_barrier(v.astype(jnp.bfloat16)).astype(jnp.float32)

@jax.custom_vjp
def low_back(v):
    return v

def low_keep(v):
    return (low(v), None)

def low_pass(kept, grad):
    return (grad,)

def back_keep(v):
    return (v, None)

def back_low(kept, grad):
    return (low(grad),)
low.defvjp(low_keep, low_pass)
low_back.defvjp(back_keep, back_low)

def matmul(left, right):
    return jnp.dot(left, right, precision=lax.Precision.HIGHEST)

def layer_norm(rows, gain, shift):
    center = rows - lax.optimization_barrier(jnp.mean(rows, axis=1, keepdims=True))
    factor = lax.rsqrt(lax.optimization_barrier(jnp.mean(center * center, axis=1, keepdims=True)) + 1e-05)
    return center * factor * gain + shift

def layer(rows, params):
    gain1, shift1, wquery, bquery, wkey, bkey, wvalue, bvalue, wout, bout, gain2, shift2, wup, bup, wdown, bdown = params
    count = rows.shape[0] // SEQ_LEN
    first = low(layer_norm(rows, gain1, shift1))

    def project(weight, shift):
        made = low(low_back(matmul(first, weight) + shift))
        return made.reshape(count, SEQ_LEN, HEADS, HEAD_DIM)
    query = project(wquery, bquery)
    keys = project(wkey, bkey)
    values = project(wvalue, bvalue)
    scale = 1.0 / math.sqrt(HEAD_DIM)
    scores = low_back(jnp.einsum('sihe,sjhe->shij', query, keys, precision=lax.Precision.HIGHEST) * scale)
    causal = lax.broadcasted_iota(jnp.int32, (SEQ_LEN, SEQ_LEN), 0) >= lax.broadcasted_iota(jnp.int32, (SEQ_LEN, SEQ_LEN), 1)
    root = jnp.sqrt(scores * scores + 1.0)
    magnitude = jnp.where(causal, root, -1e+30)
    top = lax.optimization_barrier(jnp.max(magnitude, axis=-1, keepdims=True))
    expo = jnp.where(causal, jnp.exp(magnitude - top), 0.0)
    probs = expo / lax.optimization_barrier(jnp.sum(expo, axis=-1, keepdims=True))
    signed = scores / root * probs
    mixed = jnp.einsum('shij,sjhe->sihe', low(signed), values, precision=lax.Precision.HIGHEST)
    mixed = low(low_back(mixed.reshape(rows.shape[0], D)))
    attn = low_back(matmul(mixed, wout))
    hidden1 = rows + attn + bout
    second = low(layer_norm(hidden1, gain2, shift2))
    upper = low_back(matmul(second, wup) + bup)
    act = low(jax.nn.gelu(upper, approximate=False))
    ffout = low_back(matmul(act, wdown))
    return hidden1 + ffout + bdown

def reference(tokens, norm1_gain, norm1_bias, w_query, b_query, w_key, b_key, w_value, b_value, w_out, b_out, norm2_gain, norm2_bias, w_up, b_up, w_down, b_down, cotangent):
    params = tuple((p.astype(jnp.float32) for p in (norm1_gain, norm1_bias, w_query, b_query, w_key, b_key, w_value, b_value, w_out, b_out, norm2_gain, norm2_bias, w_up, b_up, w_down, b_down)))
    nseq = TOKENS // SEQ_LEN
    group = math.gcd(nseq, max(1, 4096 // SEQ_LEN))
    blocks = nseq // group
    rows_in = tokens.astype(jnp.float32).reshape(blocks, group * SEQ_LEN, D)
    grads_in = cotangent.astype(jnp.float32).reshape(blocks, group * SEQ_LEN, D)

    def step(carry, pair):
        block_rows, block_grad = pair
        result, pullback = jax.vjp(layer, block_rows, params)
        grad_rows, grad_params = pullback(block_grad)
        carry = tuple((c + g for c, g in zip(carry, grad_params)))
        return (carry, (result, grad_rows))
    start = tuple((jnp.zeros_like(p) for p in params))
    totals, (outputs, input_grads) = lax.scan(step, start, (rows_in, grads_in))
    layer_out = outputs.reshape(TOKENS, D).astype(jnp.bfloat16)
    tokens_grad = input_grads.reshape(TOKENS, D).astype(jnp.bfloat16)
    return (layer_out, tokens_grad, totals[0], totals[1], totals[2], totals[3], totals[4], totals[5], totals[6], totals[7], totals[8], totals[9], totals[10], totals[11], totals[12], totals[13], totals[14], totals[15])
```

```python
import functools
import math

import jax
import jax.numpy as jnp
from jax import lax
from jax.experimental import pallas as pl
from jax.experimental.pallas import tpu as pltpu
from jax.sharding import PartitionSpec as P

HEAD_DIM = 64
SEQ = 256
HALF = SEQ // 2
LANES = 128
BF = jnp.bfloat16
F32 = jnp.float32
VMEM_LIMIT = 60 * 1024 * 1024


def dot(left, right):
    return jnp.dot(left, right, preferred_element_type=F32)


def tail_dot(left, right):
    return lax.dot_general(left, right, (((1,), (1,)), ((), ())), preferred_element_type=F32)


def turned(block):
    return block.astype(F32).T.astype(BF)


def wide(column, lanes):
    return jnp.concatenate([column] * (lanes // LANES), axis=1)


def lane_fold(rows):
    total = rows[:, :LANES]
    for start in range(LANES, rows.shape[1], LANES):
        total = total + rows[:, start : start + LANES]
    return total


def norm_plain(x):
    center = x - jnp.mean(x, axis=0, keepdims=True)
    factor = lax.rsqrt(jnp.mean(center * center, axis=0, keepdims=True) + 1e-05)
    return center * factor, factor


def norm_back(grad, plain, factor, gain):
    scaled = grad * gain
    return factor * (
        scaled
        - jnp.mean(scaled, axis=0, keepdims=True)
        - plain * jnp.mean(scaled * plain, axis=0, keepdims=True)
    )


def upper_mask():
    return lax.broadcasted_iota(jnp.int32, (HALF, HALF), 0) <= lax.broadcasted_iota(
        jnp.int32, (HALF, HALF), 1
    )


def head_scores(keys, query):
    full = dot(keys.astype(F32).T.astype(BF), query)
    return full[:HALF, :HALF], full[:, HALF:]


def smooth(scores):
    square = scores * scores + 1.0
    inverse = lax.rsqrt(square)
    return inverse, square * inverse


def attend(scores, mask):
    inverse, root = smooth(scores)
    if scores.shape[0] > HALF:
        diag = jnp.where(mask, root[HALF:], -1e30)
        magnitude = jnp.concatenate([root[:HALF], diag], axis=0)
    else:
        magnitude = jnp.where(mask, root, -1e30)
    top = jnp.max(magnitude, axis=0, keepdims=True)
    expo = jnp.exp(magnitude - top)
    total = jnp.sum(expo, axis=0, keepdims=True)
    signed = (scores * inverse) * (expo * (1.0 / total))
    return signed, top + jnp.log(total)


def attn_kernel(seqs, *refs):
    (tok, wq0, wq1, wk0, wk1, wv0, wv1, wo0, wo1, vec) = refs[:10]
    (query_o, keys_o, values_o, mixed_o, logsum_o, hidden_o) = refs[10:16]
    wqkv_t, wo_t = refs[16:18]
    dim = tok.shape[1]
    lanes = seqs * SEQ

    @pl.when(pl.program_id(0) == 0)
    def _():
        part = dim // 2
        for index, ref in enumerate((wq0, wq1, wk0, wk1, wv0, wv1)):
            wqkv_t[index * part : (index + 1) * part, :] = turned(ref[...])
        wo_t[:, :part] = turned(wo0[...])
        wo_t[:, part:] = turned(wo1[...])

    x = tok[...].astype(F32).T
    plain, _ = norm_plain(x)
    first = (plain * wide(vec[0:dim, :], lanes) + wide(vec[dim : 2 * dim, :], lanes)).astype(BF)
    outs = []
    for index in range(3):
        made = dot(wqkv_t[index * dim : (index + 1) * dim, :], first)
        made = made + wide(vec[(2 + index) * dim : (3 + index) * dim, :], lanes)
        made = made.astype(BF)
        if index == 0:
            made = made * jnp.asarray(1.0 / math.sqrt(HEAD_DIM), BF)
        outs.append(made)
    query, keys, values = outs
    mask = upper_mask()
    heads = dim // HEAD_DIM
    mixed_all = []
    for s in range(seqs):
        span = slice(s * SEQ, (s + 1) * SEQ)
        query_o[s], keys_o[s], values_o[s] = query[:, span], keys[:, span], values[:, span]
        parts = []
        logs = []
        for h in range(heads):
            rows = slice(h * HEAD_DIM, (h + 1) * HEAD_DIM)
            near, far = head_scores(keys[rows, span], query[rows, span])
            signed_a, log_a = attend(near, mask)
            signed_b, log_b = attend(far, mask)
            v = values[rows, span]
            mixed_a = dot(v[:, :HALF], signed_a.astype(BF))
            mixed_b = dot(v, signed_b.astype(BF))
            parts.append(jnp.concatenate([mixed_a, mixed_b], axis=1))
            logs.append(jnp.concatenate([log_a, log_b], axis=1))
        mixed = jnp.concatenate(parts, axis=0).astype(BF)
        mixed_o[s] = mixed
        logsum_o[s] = jnp.concatenate(logs, axis=0)
        mixed_all.append(mixed)
    mixed = jnp.concatenate(mixed_all, axis=1)
    hidden = x + dot(wo_t[...], mixed) + wide(vec[5 * dim : 6 * dim, :], lanes)
    for s in range(seqs):
        hidden_o[s] = hidden[:, s * SEQ : (s + 1) * SEQ]


def mlp_kernel(seqs, block, *refs):
    (hid, cot, wu0, wu1, wd0, wd1, vec, bup) = refs[:8]
    (out_o, dhid_o, gup_o, gdown_o, gvec_o, gbup_o) = refs[8:14]
    wu_t, wd_t, gup, gdown = refs[14:18]
    dim = hid.shape[1]
    units = wu0.shape[1]
    lanes = seqs * SEQ
    step = pl.program_id(0)

    @pl.when(step == 0)
    def _():
        for index, (up, down) in enumerate(((wu0, wd0), (wu1, wd1))):
            wu_t[index * units : (index + 1) * units, :] = turned(up[...])
            wd_t[:, index * units : (index + 1) * units] = turned(down[...])
        gup[...] = jnp.zeros_like(gup)
        gdown[...] = jnp.zeros_like(gdown)
        gvec_o[...] = jnp.zeros_like(gvec_o)
        gbup_o[...] = jnp.zeros_like(gbup_o)

    hidden = jnp.concatenate([hid[s] for s in range(seqs)], axis=1)
    grad_out = cot[...].astype(F32).T
    grad_low = grad_out.astype(BF)
    gain = wide(vec[0:dim, :], lanes)
    plain, factor = norm_plain(hidden)
    second = (plain * gain + wide(vec[dim : 2 * dim, :], lanes)).astype(BF)
    ffout = None
    dnorm = None
    for start in range(0, 2 * units, block):
        span = slice(start, start + block)
        half, inner = divmod(start, units)
        up_ref, down_ref = ((wu0, wd0), (wu1, wd1))[half]
        inner = slice(inner, inner + block)
        upper = dot(wu_t[span, :], second) + wide(bup[span, :], lanes)
        dact = dot(down_ref[inner, :], grad_low)
        cdf = 0.5 * lax.erf(upper * (1.0 / math.sqrt(2.0))) + 0.5
        density = jnp.exp(-0.5 * (upper * upper)) * (1.0 / math.sqrt(2.0 * math.pi))
        act = (upper * cdf).astype(BF)
        dup_wide = dact * (cdf + upper * density)
        dup = dup_wide.astype(BF)
        gbup_o[span, :] += lane_fold(dup.astype(F32))
        out_part = dot(wd_t[:, span], act)
        dn_part = dot(up_ref[:, inner], dup)
        ffout = out_part if ffout is None else ffout + out_part
        dnorm = dn_part if dnorm is None else dnorm + dn_part
        gup[:, span] += tail_dot(second, dup)
        gdown[span, :] += tail_dot(act, grad_low)
    out = hidden + ffout + wide(vec[2 * dim : 3 * dim, :], lanes)
    out_o[...] = out.T.astype(BF)
    gvec_o[0:dim, :] += lane_fold(dnorm * plain)
    gvec_o[dim : 2 * dim, :] += lane_fold(dnorm)
    gvec_o[2 * dim : 3 * dim, :] += lane_fold(grad_out)
    dhidden = grad_out + norm_back(dnorm, plain, factor, gain)
    gvec_o[3 * dim : 4 * dim, :] += lane_fold(dhidden)
    for s in range(seqs):
        dhid_o[s] = dhidden[:, s * SEQ : (s + 1) * SEQ]

    @pl.when(step == pl.num_programs(0) - 1)
    def _():
        for half in range(2):
            span = slice(half * units, (half + 1) * units)
            gup_o[half] = gup[:, span].astype(BF)
            gdown_o[half] = gdown[span, :].astype(BF)


def grad_kernel(seqs, *refs):
    (tok, dhid, query_i, keys_i, values_i, mixed_i, logsum_i) = refs[:7]
    (wq0, wq1, wk0, wk1, wv0, wv1, wo0, wo1, vec) = refs[7:16]
    (tgrad_o, gqkv_o, gout_o, gvec_o) = refs[16:20]
    gqkv, gout = refs[20:22]
    dim = tok.shape[1]
    part = dim // 2
    lanes = seqs * SEQ
    step = pl.program_id(0)
    scale = 1.0 / math.sqrt(HEAD_DIM)

    @pl.when(step == 0)
    def _():
        gqkv[...] = jnp.zeros_like(gqkv)
        gout[...] = jnp.zeros_like(gout)
        gvec_o[...] = jnp.zeros_like(gvec_o)

    dhidden = jnp.concatenate([dhid[s] for s in range(seqs)], axis=1)
    dattn = dhidden.astype(BF)
    mixed = jnp.concatenate([mixed_i[s] for s in range(seqs)], axis=1)
    gout[...] += tail_dot(mixed, dattn)
    dmixed = jnp.concatenate([dot(wo0[...], dattn), dot(wo1[...], dattn)], axis=0).astype(BF)
    mask = upper_mask()
    heads = dim // HEAD_DIM
    zero = jnp.zeros((HALF, HALF), BF)
    dq_all, dk_all, dv_all = [], [], []
    for s in range(seqs):
        span = slice(s * SEQ, (s + 1) * SEQ)
        dq, dk, dv = [], [], []
        for h in range(heads):
            rows = slice(h * HEAD_DIM, (h + 1) * HEAD_DIM)
            q, k, v = query_i[s, rows, :], keys_i[s, rows, :], values_i[s, rows, :]
            dm = dmixed[rows, span]
            score_pair = head_scores(k, q)
            dsigned_pair = head_scores(v, dm)
            signed_low, dscores_low = [], []
            for index in range(2):
                scores, dsigned = score_pair[index], dsigned_pair[index]
                lse = logsum_i[s, h : h + 1, index * HALF : (index + 1) * HALF]
                inverse, root = smooth(scores)
                if index == 1:
                    diag = jnp.where(mask, root[HALF:], -1e30)
                    magnitude = jnp.concatenate([root[:HALF], diag], axis=0)
                else:
                    magnitude = jnp.where(mask, root, -1e30)
                probs = jnp.exp(magnitude - lse)
                sign = scores * inverse
                signed = sign * probs
                row_dot = jnp.sum(signed * dsigned, axis=0, keepdims=True)
                slope = inverse * inverse * inverse + sign * sign
                dscores = probs * dsigned * slope - signed * row_dot
                signed_low.append(signed.astype(BF))
                dscores_low.append(dscores.astype(BF))
            dq_a = dot(k[:, :HALF], dscores_low[0])
            dq_b = dot(k, dscores_low[1])
            dq.append(jnp.concatenate([dq_a, dq_b], axis=1))
            full = jnp.concatenate(
                [jnp.concatenate([dscores_low[0], zero], axis=0), dscores_low[1]], axis=1
            )
            dk.append(tail_dot(q, full))
            full = jnp.concatenate(
                [jnp.concatenate([signed_low[0], zero], axis=0), signed_low[1]], axis=1
            )
            dv.append(tail_dot(dm, full))
        dq_all.append((jnp.concatenate(dq, axis=0) * scale).astype(BF))
        dk_all.append(jnp.concatenate(dk, axis=0).astype(BF))
        dv_all.append(jnp.concatenate(dv, axis=0).astype(BF))
    x = tok[...].astype(F32).T
    gain = wide(vec[0:dim, :], lanes)
    plain, factor = norm_plain(x)
    first = (plain * gain + wide(vec[dim : 2 * dim, :], lanes)).astype(BF)
    dnorm = None
    weights = ((wq0, wq1), (wk0, wk1), (wv0, wv1))
    for index, group in enumerate((dq_all, dk_all, dv_all)):
        grad = jnp.concatenate(group, axis=1)
        gqkv[:, index * dim : (index + 1) * dim] += tail_dot(first, grad)
        gvec_o[(2 + index) * dim : (3 + index) * dim, :] += lane_fold(grad.astype(F32))
        for half in range(2):
            made = dot(weights[index][half][...], grad[half * part : (half + 1) * part])
            dnorm = made if dnorm is None else dnorm + made
    gvec_o[0:dim, :] += lane_fold(dnorm * plain)
    gvec_o[dim : 2 * dim, :] += lane_fold(dnorm)
    tgrad = dhidden + norm_back(dnorm, plain, factor, gain)
    tgrad_o[...] = tgrad.T.astype(BF)

    @pl.when(step == pl.num_programs(0) - 1)
    def _():
        for half in range(2):
            for index in range(3):
                start = index * dim + half * part
                gqkv_o[half, index] = gqkv[:, start : start + part].astype(BF)
            gout_o[half] = gout[half * part : (half + 1) * part, :].astype(BF)


def whole_vmem():
    return pl.BlockSpec(memory_space=pltpu.VMEM)


def seq_block(seqs, *dims):
    return pl.BlockSpec((seqs,) + dims, lambda i: (i,) + (0,) * len(dims))


def params():
    return pltpu.CompilerParams(
        dimension_semantics=("arbitrary",), vmem_limit_bytes=VMEM_LIMIT
    )


def attn_call(tokens, weights, vec, seqs):
    rows, dim = tokens.shape
    count = rows // SEQ
    heads = dim // HEAD_DIM
    feat = jax.ShapeDtypeStruct((count, dim, SEQ), BF)
    return pl.pallas_call(
        functools.partial(attn_kernel, seqs),
        grid=(count // seqs,),
        in_specs=[pl.BlockSpec((seqs * SEQ, dim), lambda i: (i, 0))] + [whole_vmem()] * 9,
        out_specs=[seq_block(seqs, dim, SEQ)] * 4
        + [seq_block(seqs, heads, SEQ), seq_block(seqs, dim, SEQ)],
        out_shape=[feat] * 4
        + [
            jax.ShapeDtypeStruct((count, heads, SEQ), F32),
            jax.ShapeDtypeStruct((count, dim, SEQ), F32),
        ],
        scratch_shapes=[pltpu.VMEM((3 * dim, dim), BF), pltpu.VMEM((dim, dim), BF)],
        compiler_params=params(),
        name="attn_forward",
    )(tokens, *weights, vec)


def mlp_call(hidden, cotangent, weights, vec, bup, seqs, block):
    rows, dim = cotangent.shape
    count = rows // SEQ
    units = weights[0].shape[1]
    return pl.pallas_call(
        functools.partial(mlp_kernel, seqs, block),
        grid=(count // seqs,),
        in_specs=[
            seq_block(seqs, dim, SEQ),
            pl.BlockSpec((seqs * SEQ, dim), lambda i: (i, 0)),
        ]
        + [whole_vmem()] * 6,
        out_specs=[
            pl.BlockSpec((seqs * SEQ, dim), lambda i: (i, 0)),
            seq_block(seqs, dim, SEQ),
        ]
        + [whole_vmem()] * 4,
        out_shape=[
            jax.ShapeDtypeStruct((rows, dim), BF),
            jax.ShapeDtypeStruct((count, dim, SEQ), F32),
            jax.ShapeDtypeStruct((2, dim, units), BF),
            jax.ShapeDtypeStruct((2, units, dim), BF),
            jax.ShapeDtypeStruct((4 * dim, LANES), F32),
            jax.ShapeDtypeStruct((2 * units, LANES), F32),
        ],
        scratch_shapes=[
            pltpu.VMEM((2 * units, dim), BF),
            pltpu.VMEM((dim, 2 * units), BF),
            pltpu.VMEM((dim, 2 * units), F32),
            pltpu.VMEM((2 * units, dim), F32),
        ],
        compiler_params=params(),
        name="feed_forward",
    )(hidden, cotangent, *weights, vec, bup)


def grad_call(tokens, dhidden, saved, weights, vec, seqs):
    rows, dim = tokens.shape
    count = rows // SEQ
    part = dim // 2
    heads = dim // HEAD_DIM
    return pl.pallas_call(
        functools.partial(grad_kernel, seqs),
        grid=(count // seqs,),
        in_specs=[pl.BlockSpec((seqs * SEQ, dim), lambda i: (i, 0))]
        + [seq_block(seqs, dim, SEQ)] * 5
        + [seq_block(seqs, heads, SEQ)]
        + [whole_vmem()] * 9,
        out_specs=[pl.BlockSpec((seqs * SEQ, dim), lambda i: (i, 0))] + [whole_vmem()] * 3,
        out_shape=[
            jax.ShapeDtypeStruct((rows, dim), BF),
            jax.ShapeDtypeStruct((2, 3, dim, part), BF),
            jax.ShapeDtypeStruct((2, part, dim), BF),
            jax.ShapeDtypeStruct((5 * dim, LANES), F32),
        ],
        scratch_shapes=[pltpu.VMEM((dim, 3 * dim), F32), pltpu.VMEM((dim, dim), F32)],
        compiler_params=params(),
        name="attn_backward",
    )(tokens, dhidden, *saved, *weights, vec)


def shifted(value, axis, count, shift):
    return lax.ppermute(value, axis, [(i, (i + shift) % count) for i in range(count)])


def gathered(value, count, axis):
    blocks = [value] + [shifted(value, "mp", count, -r) for r in range(1, count)]
    half = count // 2
    return [
        blocks[g * half] if half == 1 else jnp.concatenate(blocks[g * half : (g + 1) * half], axis)
        for g in range(2)
    ]


def added(left, right):
    return (left.astype(F32) + right.astype(F32)).astype(BF)


def halve_double(value, order):
    me = lax.axis_index("dp")
    count = lax.axis_size("dp")
    swap = lambda block, bit: lax.ppermute(block, "dp", [(i, i ^ bit) for i in range(count)])
    for bit in order:
        half = value.shape[0] // 2
        low, high = value[:half], value[half:]
        upper = (me & bit) != 0
        keep, send = jnp.where(upper, high, low), jnp.where(upper, low, high)
        value = added(keep, swap(send, bit))
    for bit in reversed(order):
        other = swap(value, bit)
        upper = (me & bit) != 0
        value = jnp.concatenate(
            [jnp.where(upper, other, value), jnp.where(upper, value, other)], axis=0
        )
    return value


def dp_sum(value, count):
    bits = [1 << b for b in range(count.bit_length() - 1)]
    rows = value.shape[0]
    unit = 16 * count
    third = -(-rows // (3 * unit)) * unit
    value = jnp.pad(value, ((0, 3 * third - rows), (0, 0)))
    parts = []
    for index in range(3):
        order = bits[index:] + bits[:index]
        parts.append(halve_double(value[index * third : (index + 1) * third], order))
    return jnp.concatenate(parts, axis=0)[:rows]


def body(mp, dp, *args):
    (tokens, gain1, shift1, wq, bq, wk, bk, wv, bv, wo, bo) = args[:11]
    (gain2, shift2, wu, bu, wd, bd, cotangent) = args[11:]
    rows, dim = tokens.shape
    local = wq.shape[1]
    units = wu.shape[1]
    own = rows // mp
    me = lax.axis_index("mp")

    weights = []
    for w in (wq, wk, wv):
        weights += gathered(w, mp, 1)
    weights += gathered(wo, mp, 0)
    mlp_weights = gathered(wu, mp, 1) + gathered(wd, mp, 0)
    small = jnp.concatenate([bq, bk, bv, bu])
    blocks = [small] + [shifted(small, "mp", mp, -r) for r in range(1, mp)]
    spread = lambda lo, hi: jnp.concatenate([b[lo:hi] for b in blocks])
    over = lambda vector: jnp.broadcast_to(vector[:, None], (vector.shape[0], LANES))
    vec1 = over(
        jnp.concatenate(
            [gain1, shift1]
            + [spread(i * local, (i + 1) * local) for i in range(3)]
            + [bo]
        )
    )
    vec2 = over(jnp.concatenate([gain2, shift2, bd]))
    bup = over(spread(3 * local, 3 * local + units))

    tok = lax.dynamic_slice_in_dim(tokens, me * own, own)
    cot = lax.dynamic_slice_in_dim(cotangent, me * own, own)
    saved = attn_call(tok, weights, vec1, 1)
    out, dhidden, gup, gdown, gvec2, gbup = mlp_call(
        saved[-1], cot, mlp_weights, vec2, bup, 1, 512
    )
    tgrad, gqkv, gout, gvec1 = grad_call(tok, dhidden, saved[:-1], weights, vec1, 1)

    def whole(part):
        full = jnp.zeros((rows, dim), BF)
        for r in range(mp):
            block = part if r == 0 else shifted(part, "mp", mp, r)
            full = lax.dynamic_update_slice_in_dim(full, block, ((me - r) % mp) * own, 0)
        return full

    gvec1 = jnp.sum(gvec1, axis=1)
    gvec2 = jnp.sum(gvec2, axis=1)
    gbup = jnp.sum(gbup, axis=1)
    same = jnp.concatenate([gvec2, gvec1[: 2 * dim]])
    per = mp // 2

    def piece(r):
        g, j = divmod(r, per)
        cols = slice(j * units, (j + 1) * units)
        lanes = slice(j * local, (j + 1) * local)
        bias = [gvec1[(2 + i) * dim + r * local : (2 + i) * dim + (r + 1) * local] for i in range(3)]
        vector = jnp.concatenate([same] + bias + [gbup[r * units : (r + 1) * units]])
        size = -(-vector.shape[0] // dim) * dim
        vector = jnp.pad(vector, (0, size - vector.shape[0])).reshape(-1, dim).astype(BF)
        qkv = [gqkv[g, i][:, lanes].reshape(-1, dim) for i in range(3)]
        return jnp.concatenate(
            [gup[g][:, cols].reshape(-1, dim), gdown[g][cols]]
            + qkv
            + [gout[g][lanes], vector],
            axis=0,
        )

    total = piece(0).astype(F32)
    for r in range(1, mp):
        total = total + shifted(piece(r), "mp", mp, r).astype(F32)
    total = dp_sum(total.astype(BF), dp).astype(F32)
    at = 0

    def take(count, shape):
        nonlocal at
        block = total[at : at + count]
        at += count
        return block.reshape(shape)

    g_up = take(units, (dim, units))
    g_down = take(units, (units, dim))
    g_qkv = [take(local, (dim, local)) for _ in range(3)]
    g_out = take(local, (local, dim))
    vector = total[at:].reshape(-1)
    g_same = [vector[i * dim : (i + 1) * dim] for i in range(6)]
    base = 6 * dim
    g_bias = [vector[base + i * local : base + (i + 1) * local] for i in range(3)]
    g_bup = vector[base + 3 * local : base + 3 * local + units]
    return (
        whole(out),
        whole(tgrad),
        g_same[4],
        g_same[5],
        g_qkv[0],
        g_bias[0],
        g_qkv[1],
        g_bias[1],
        g_qkv[2],
        g_bias[2],
        g_out,
        g_same[3],
        g_same[0],
        g_same[1],
        g_up,
        g_bup,
        g_down,
        g_same[2],
    )


def solution(mesh):
    split = P("dp", None)
    columns, some, lines = P(None, "mp"), P("mp"), P("mp", None)
    return jax.shard_map(
        functools.partial(body, mesh.shape["mp"], mesh.shape["dp"]),
        mesh=mesh,
        in_specs=(split, P(), P(), columns, some, columns, some, columns, some, lines, P())
        + (P(), P(), columns, some, lines, P(), split),
        out_specs=(split, split, P(), P(), columns, some, columns, some, columns, some, lines)
        + (P(), P(), P(), columns, some, lines, P()),
        check_vma=False,
    )
```

```python
import functools
import math

import jax
import jax.numpy as jnp
from jax import lax
from jax.experimental import pallas as pl
from jax.experimental.pallas import tpu as pltpu
from jax.sharding import PartitionSpec as P

HEAD_DIM = 64
SEQ = 256
HALF = SEQ // 2
LANES = 128
BF = jnp.bfloat16
F32 = jnp.float32
VMEM_LIMIT = 60 * 1024 * 1024


def dot(left, right):
    return jnp.dot(left, right, preferred_element_type=F32)


def tail_dot(left, right):
    return lax.dot_general(left, right, (((1,), (1,)), ((), ())), preferred_element_type=F32)


def turned(block):
    return block.astype(F32).T.astype(BF)


def wide(column, lanes):
    return jnp.concatenate([column] * (lanes // LANES), axis=1)


def lane_fold(rows):
    total = rows[:, :LANES]
    for start in range(LANES, rows.shape[1], LANES):
        total = total + rows[:, start : start + LANES]
    return total


def as_row(sums):
    return jnp.sum(sums.T, axis=0, keepdims=True)


def norm_plain(x):
    center = x - jnp.mean(x, axis=0, keepdims=True)
    factor = lax.rsqrt(jnp.mean(center * center, axis=0, keepdims=True) + 1e-05)
    return center * factor, factor


def norm_back(grad, plain, factor, gain):
    scaled = grad * gain
    return factor * (
        scaled
        - jnp.mean(scaled, axis=0, keepdims=True)
        - plain * jnp.mean(scaled * plain, axis=0, keepdims=True)
    )


def upper_mask():
    return lax.broadcasted_iota(jnp.int32, (HALF, HALF), 0) <= lax.broadcasted_iota(
        jnp.int32, (HALF, HALF), 1
    )


def smooth(scores):
    square = scores * scores + 1.0
    inverse = lax.rsqrt(square)
    return inverse, square * inverse


def pair_diag(left, right):
    zero = jnp.zeros_like(left)
    return jnp.concatenate(
        [jnp.concatenate([left, zero], axis=1), jnp.concatenate([zero, right], axis=1)], axis=0
    )


def pair_near_far(rows):
    left, right = rows[:HEAD_DIM], rows[HEAD_DIM:]
    return (
        pair_diag(left[:, :HALF], right[:, :HALF]),
        pair_diag(left[:, HALF:], right[:, HALF:]),
    )


def attend(scores, mask):
    inverse, root = smooth(scores)
    if scores.shape[0] > HALF:
        diagonal = jnp.where(mask, root[HALF:], -1e30)
        magnitude = jnp.concatenate([root[:HALF], diagonal], axis=0)
    else:
        magnitude = jnp.where(mask, root, -1e30)
    top = jnp.max(magnitude, axis=0, keepdims=True)
    expo = jnp.exp(magnitude - top)
    probs = expo * (1.0 / jnp.sum(expo, axis=0, keepdims=True))
    sign = scores * inverse
    slope = inverse * inverse * inverse + sign * sign
    return (sign * probs).astype(BF), (probs * slope).astype(BF)


def attn_kernel(seqs, place, *refs):
    (tok, wq0, wq1, wk0, wk1, wv0, wv1, wo0, wo1, vec) = refs[:10]
    (query_o, keys_o, values_o, mixed_o, signed_o, slope_o, first_o, hidden_o) = refs[10:18]
    wqkv_t, wo_t = refs[18:20]
    dim = tok.shape[1]
    lanes = seqs * SEQ

    @pl.when(pl.program_id(0) == 0)
    def _():
        part = dim // 2
        for index, ref in enumerate((wq0, wq1, wk0, wk1, wv0, wv1)):
            wqkv_t[index * part : (index + 1) * part, :] = turned(ref[...])
        wo_t[:, :part] = turned(wo0[...])
        wo_t[:, part:] = turned(wo1[...])

    half = lax.broadcasted_iota(jnp.int32, (HALF, SEQ), 1)
    mask = lax.broadcasted_iota(jnp.int32, (HALF, SEQ), 0) <= jnp.where(half < HALF, half, half - HALF)
    pairs = dim // LANES
    x = tok[...].astype(F32).T
    plain, _ = norm_plain(x)
    first = (plain * wide(vec[0:dim, :], lanes) + wide(vec[dim : 2 * dim, :], lanes)).astype(BF)
    outs = []
    for index in range(3):
        made = dot(wqkv_t[index * dim : (index + 1) * dim, :], first)
        made = made + wide(vec[(2 + index) * dim : (3 + index) * dim, :], lanes)
        made = made.astype(BF)
        if index == 0:
            made = made * jnp.asarray(1.0 / math.sqrt(HEAD_DIM), BF)
        outs.append(made)
    query, keys, values = outs
    mixed_all = []
    for s in range(seqs):
        span = slice(s * SEQ, (s + 1) * SEQ)
        first_o[s] = first[:, span]
        k_nat = turned(keys[:, span])
        parts = []
        for p in range(pairs):
            rows = slice(p * LANES, (p + 1) * LANES)
            c, g = divmod(p, 2)
            query_o[s, c, g], keys_o[s, c, g] = query[rows, span], keys[rows, span]
            values_o[s, c, g] = values[rows, span]
            near_q, far_q = pair_near_far(query[rows, span])
            kp = k_nat[:, rows]
            near, near_g = attend(dot(kp[:HALF], near_q), mask)
            far, far_g = attend(dot(kp, far_q), mask)
            signed_o[s, c, g, :HALF], signed_o[s, c, g, HALF:] = near, far
            slope_o[s, c, g, :HALF], slope_o[s, c, g, HALF:] = near_g, far_g
            v = values[rows, span]
            near_m, far_m = dot(v[:, :HALF], near), dot(v, far)
            made = jnp.concatenate(
                [
                    jnp.concatenate([near_m[:HEAD_DIM, :HALF], far_m[:HEAD_DIM, :HALF]], axis=1),
                    jnp.concatenate([near_m[HEAD_DIM:, HALF:], far_m[HEAD_DIM:, HALF:]], axis=1),
                ],
                axis=0,
            ).astype(BF)
            mixed_o[s, c, g] = made
            parts.append(made)
        mixed_all.append(jnp.concatenate(parts, axis=0))
    mixed = jnp.concatenate(mixed_all, axis=1)
    hidden = x + dot(wo_t[...], mixed) + wide(vec[5 * dim : 6 * dim, :], lanes)
    for s in range(seqs):
        hidden_o[s] = hidden[:, s * SEQ : (s + 1) * SEQ]


def mlp_kernel(seqs, block, place, *refs):
    (hid, cot, wu0, wu1, wd0, wd1, vec, bup) = refs[:8]
    (out_o, low_o, grad_o, gvec_o) = refs[8:12]
    wu_t, wd_t, gup, gdown, gvec, gbup = refs[12:18]
    dim = hid.shape[1]
    units = wu0.shape[1]
    lanes = seqs * SEQ
    step = pl.program_id(0)

    @pl.when(step == 0)
    def _():
        for index, (up, down) in enumerate(((wu0, wd0), (wu1, wd1))):
            wu_t[index * units : (index + 1) * units, :] = turned(up[...])
            wd_t[:, index * units : (index + 1) * units] = turned(down[...])
        gup[...] = jnp.zeros_like(gup)
        gdown[...] = jnp.zeros_like(gdown)
        gvec[...] = jnp.zeros_like(gvec)
        gbup[...] = jnp.zeros_like(gbup)

    hidden = jnp.concatenate([hid[s] for s in range(seqs)], axis=1)
    grad_out = cot[...].astype(F32).T
    grad_low = grad_out.astype(BF)
    gain = wide(vec[0:dim, :], lanes)
    plain, factor = norm_plain(hidden)
    second = (plain * gain + wide(vec[dim : 2 * dim, :], lanes)).astype(BF)
    ffout = None
    dnorm = None
    for start in range(0, 2 * units, block):
        span = slice(start, start + block)
        half, inner = divmod(start, units)
        up_ref, down_ref = ((wu0, wd0), (wu1, wd1))[half]
        inner = slice(inner, inner + block)
        upper = dot(wu_t[span, :], second) + wide(bup[span, :], lanes)
        dact = dot(down_ref[inner, :], grad_low)
        cdf = 0.5 * lax.erf(upper * (1.0 / math.sqrt(2.0))) + 0.5
        density = jnp.exp(-0.5 * (upper * upper)) * (1.0 / math.sqrt(2.0 * math.pi))
        act = (upper * cdf).astype(BF)
        dup_wide = dact * (cdf + upper * density)
        dup = dup_wide.astype(BF)
        gbup[span, :] += lane_fold(dup.astype(F32))
        out_part = dot(wd_t[:, span], act)
        dn_part = dot(up_ref[:, inner], dup)
        ffout = out_part if ffout is None else ffout + out_part
        dnorm = dn_part if dnorm is None else dnorm + dn_part
        gup[:, span] += tail_dot(second, dup)
        gdown[span, :] += tail_dot(act, grad_low)
    out = hidden + ffout + wide(vec[2 * dim : 3 * dim, :], lanes)
    out_o[...] = out.T.astype(BF)
    gvec[0:dim, :] += lane_fold(dnorm * plain)
    gvec[dim : 2 * dim, :] += lane_fold(dnorm)
    gvec[2 * dim : 3 * dim, :] += lane_fold(grad_out)
    dhidden = grad_out + norm_back(dnorm, plain, factor, gain)
    gvec[3 * dim :, :] += lane_fold(dhidden)
    for s in range(seqs):
        low_o[s] = dhidden[:, s * SEQ : (s + 1) * SEQ].astype(BF)

    @pl.when(step == pl.num_programs(0) - 1)
    def _():
        for half in range(2):
            for index in range(units // dim):
                start = half * units + index * dim
                grad_o[half, index * dim : (index + 1) * dim, :] = gup[:, start : start + dim].astype(BF)
            grad_o[half, units:, :] = gdown[half * units : (half + 1) * units, :].astype(BF)
        for index in range(4):
            gvec_o[index : index + 1, :] = as_row(gvec[index * dim : (index + 1) * dim, :])
        for index in range(2 * units // dim):
            gvec_o[4 + index : 5 + index, :] = as_row(gbup[index * dim : (index + 1) * dim, :])


def grad_kernel(seqs, group, *refs):
    (low_i, first_i, query_i, keys_i, values_i, mixed_i, signed_i, slope_i) = refs[:8]
    wo0, wo1 = refs[8:10]
    (dq_o, dk_o, dv_o, grad_o, gvec_o) = refs[10:15]
    gqkv, gout, gb = refs[15:18]
    dim = low_i.shape[1]
    part = 2 * LANES
    step = pl.program_id(0)
    scale = 1.0 / math.sqrt(HEAD_DIM)

    @pl.when(step == 0)
    def _():
        gqkv[...] = jnp.zeros_like(gqkv)
        gout[...] = jnp.zeros_like(gout)
        gb[...] = jnp.zeros_like(gb)

    place = slice(group * LANES, (group + 1) * LANES)
    first = jnp.concatenate([first_i[s] for s in range(seqs)], axis=1)
    low = jnp.concatenate([low_i[s] for s in range(seqs)], axis=1)
    dmixed = jnp.concatenate([dot(wo0[place, :], low), dot(wo1[place, :], low)], axis=0).astype(BF)
    mixed = jnp.concatenate(
        [
            jnp.concatenate([mixed_i[s, 0, 0], mixed_i[s, 1, 0]], axis=0)
            for s in range(seqs)
        ],
        axis=1,
    )
    dq_all, dk_all, dv_all = [], [], []
    for s in range(seqs):
        span = slice(s * SEQ, (s + 1) * SEQ)
        dq, dk, dv = [], [], []
        for c in range(2):
            rows = slice(c * LANES, (c + 1) * LANES)
            q, k = query_i[s, c, 0], keys_i[s, c, 0]
            dm = dmixed[rows, span]
            v_nat = turned(values_i[s, c, 0])
            near_q, far_q = pair_near_far(q)
            near_m, far_m = pair_near_far(dm)
            low_pair = []
            for index in range(2):
                keys = slice(0, HALF) if index == 0 else slice(0, SEQ)
                block = slice(0, HALF) if index == 0 else slice(HALF, HALF + SEQ)
                dsigned = dot(v_nat[keys], (near_m, far_m)[index])
                signed = signed_i[s, c, 0, block].astype(F32)
                row_dot = jnp.sum(signed * dsigned, axis=0, keepdims=True)
                dscores = slope_i[s, c, 0, block].astype(F32) * dsigned - signed * row_dot
                low_pair.append(dscores.astype(BF))
            near, far = low_pair
            near_p, far_p = dot(k[:, :HALF], near), dot(k, far)
            dq.append(
                jnp.concatenate(
                    [
                        jnp.concatenate([near_p[:HEAD_DIM, :HALF], far_p[:HEAD_DIM, :HALF]], axis=1),
                        jnp.concatenate([near_p[HEAD_DIM:, HALF:], far_p[HEAD_DIM:, HALF:]], axis=1),
                    ],
                    axis=0,
                )
            )
            near_p, far_p = tail_dot(near, near_q), tail_dot(far, far_q)
            dk.append(jnp.concatenate([far_p[:HALF] + near_p, far_p[HALF:]], axis=0))
            near_p = tail_dot(signed_i[s, c, 0, :HALF], near_m)
            far_p = tail_dot(signed_i[s, c, 0, HALF:], far_m)
            dv.append(jnp.concatenate([far_p[:HALF] + near_p, far_p[HALF:]], axis=0))
        dq_all.append((jnp.concatenate(dq, axis=0) * scale).astype(BF))
        dk_all.append(jnp.concatenate(dk, axis=1).astype(BF))
        dv_all.append(jnp.concatenate(dv, axis=1).astype(BF))
        dq_o[s], dk_o[s], dv_o[s] = dq_all[s], dk_all[s], dv_all[s]
    gout[...] += tail_dot(mixed, low)
    dq, dk, dv = jnp.concatenate(dq_all, axis=1), jnp.concatenate(dk_all, axis=0), jnp.concatenate(dv_all, axis=0)
    gqkv[:, :part] += tail_dot(first, dq)
    gqkv[:, part : 2 * part] += dot(first, dk)
    gqkv[:, 2 * part :] += dot(first, dv)
    gb[:part, :] += lane_fold(dq.astype(F32))
    for index, block in ((2, dk), (3, dv)):
        total = jnp.sum(block.astype(F32).reshape(-1, 8, part), axis=0)
        gb[index * LANES : index * LANES + 8, :] += total[:, :LANES]
        gb[index * LANES + 8 : index * LANES + 16, :] += total[:, LANES:]

    @pl.when(step == pl.num_programs(0) - 1)
    def _():
        for c in range(2):
            for index in range(3):
                start = index * part + c * LANES
                grad_o[c, index * dim : (index + 1) * dim, :] = gqkv[:, start : start + LANES].astype(BF)
            for index in range(dim // LANES):
                start = 3 * dim + index * LANES
                grad_o[c, start : start + LANES, :] = gout[
                    c * LANES : (c + 1) * LANES, index * LANES : (index + 1) * LANES
                ].astype(BF)
            gvec_o[c : c + 1, :] = as_row(gb[c * LANES : (c + 1) * LANES, :])
            for index in (2, 3):
                rows = slice(index * LANES + 8 * c, index * LANES + 8 * c + 8)
                gvec_o[2 * index - 2 + c : 2 * index - 1 + c, :] = jnp.sum(gb[rows, :], axis=0, keepdims=True)


def input_kernel(seqs, place, *refs):
    tok, dhid, dq0, dk0, dv0, dq1, dk1, dv1 = refs[:8]
    wq0, wq1, wk0, wk1, wv0, wv1, vec = refs[8:15]
    tgrad_o, gvec_o = refs[15:17]
    gvec = refs[17]
    dim = tok.shape[1]

    @pl.when(pl.program_id(0) == 0)
    def _():
        gvec[...] = jnp.zeros_like(gvec)

    gain = wide(vec[0:dim, :], SEQ)
    for s in range(seqs):
        rows = slice(s * SEQ, (s + 1) * SEQ)
        dnorm = None
        for c, (wq, wk, wv) in enumerate(((wq0, wk0, wv0), (wq1, wk1, wv1))):
            lanes = slice(c * LANES, (c + 1) * LANES)
            dq = jnp.concatenate([dq0[s, lanes, :], dq1[s, lanes, :]], axis=0)
            dk = jnp.concatenate([dk0[s, :, lanes], dk1[s, :, lanes]], axis=1)
            dv = jnp.concatenate([dv0[s, :, lanes], dv1[s, :, lanes]], axis=1)
            made = dot(wq[...], dq) + tail_dot(wk[...], dk) + tail_dot(wv[...], dv)
            dnorm = made if dnorm is None else dnorm + made
        plain, factor = norm_plain(tok[rows, :].astype(F32).T)
        gvec[0:dim, :] += lane_fold(dnorm * plain)
        gvec[dim : 2 * dim, :] += lane_fold(dnorm)
        tgrad = dhid[s].astype(F32) + norm_back(dnorm, plain, factor, gain)
        tgrad_o[rows, :] = tgrad.T.astype(BF)

    @pl.when(pl.program_id(0) == pl.num_programs(0) - 1)
    def _():
        for index in range(2):
            gvec_o[index : index + 1, :] = as_row(gvec[index * dim : (index + 1) * dim, :])


def whole_vmem():
    return pl.BlockSpec(memory_space=pltpu.VMEM)


def seq_block(seqs, *dims):
    return pl.BlockSpec((seqs,) + dims, lambda i: (i,) + (0,) * len(dims))


def params():
    return pltpu.CompilerParams(
        dimension_semantics=("arbitrary",), vmem_limit_bytes=VMEM_LIMIT
    )


def prefetch(grid, in_specs, out_specs, scratch=()):
    return pltpu.PrefetchScalarGridSpec(
        num_scalar_prefetch=1, grid=grid, in_specs=in_specs, out_specs=out_specs, scratch_shapes=scratch
    )


def row_block(seqs, dim, steps):
    return pl.BlockSpec((seqs * SEQ, dim), lambda i, place: (place[0] * steps + i, 0))


def placed_seq_block(seqs, *dims):
    return pl.BlockSpec((seqs,) + dims, lambda i, place: (i,) + (0,) * len(dims))


def attn_call(place, tokens, own, weights, vec, seqs):
    dim = tokens.shape[1]
    count = own // SEQ
    steps = count // seqs
    feat = (2, 2, LANES, SEQ)
    wide_block = (2, 2, HALF + SEQ, SEQ)
    shape = jax.ShapeDtypeStruct
    return pl.pallas_call(
        functools.partial(attn_kernel, seqs),
        grid_spec=prefetch(
            (steps,),
            [row_block(seqs, dim, steps)] + [whole_vmem()] * 9,
            [placed_seq_block(seqs, *feat)] * 4
            + [placed_seq_block(seqs, *wide_block)] * 2
            + [placed_seq_block(seqs, dim, SEQ)] * 2,
            [pltpu.VMEM((3 * dim, dim), BF), pltpu.VMEM((dim, dim), BF)],
        ),
        out_shape=[shape((count,) + feat, BF)] * 4
        + [shape((count,) + wide_block, BF)] * 2
        + [shape((count, dim, SEQ), BF), shape((count, dim, SEQ), F32)],
        compiler_params=params(),
        name="attn_forward",
    )(place, tokens, *weights, vec)


def grad_call(group, low, first, saved, weights, seqs):
    count, dim = low.shape[:2]
    steps = count // seqs
    one = lambda *dims: pl.BlockSpec((seqs, 2, 1) + dims, lambda i: (i, 0, group, 0, 0))
    shape = jax.ShapeDtypeStruct
    part = 2 * LANES
    return pl.pallas_call(
        functools.partial(grad_kernel, seqs, group),
        grid=(steps,),
        in_specs=[seq_block(seqs, dim, SEQ)] * 2
        + [one(LANES, SEQ)] * 4
        + [one(HALF + SEQ, SEQ)] * 2
        + [whole_vmem()] * 2,
        out_specs=[seq_block(seqs, part, SEQ), seq_block(seqs, SEQ, part), seq_block(seqs, SEQ, part)]
        + [whole_vmem()] * 2,
        out_shape=[
            shape((count, part, SEQ), BF),
            shape((count, SEQ, part), BF),
            shape((count, SEQ, part), BF),
            shape((2, 4 * dim, LANES), BF),
            shape((8, LANES), F32),
        ],
        scratch_shapes=[
            pltpu.VMEM((dim, 3 * part), F32),
            pltpu.VMEM((part, dim), F32),
            pltpu.VMEM((4 * LANES, LANES), F32),
        ],
        compiler_params=params(),
        name="attn_backward",
    )(low, first, *saved, *weights)


def input_call(place, tokens, dhidden, pieces, weights, vec, seqs):
    dim = tokens.shape[1]
    count = dhidden.shape[0]
    steps = count // seqs
    part = 2 * LANES
    trio = [
        placed_seq_block(seqs, part, SEQ),
        placed_seq_block(seqs, SEQ, part),
        placed_seq_block(seqs, SEQ, part),
    ]
    return pl.pallas_call(
        functools.partial(input_kernel, seqs),
        grid_spec=prefetch(
            (steps,),
            [row_block(seqs, dim, steps), placed_seq_block(seqs, dim, SEQ)]
            + trio * 2
            + [whole_vmem()] * 7,
            [
                pl.BlockSpec((seqs * SEQ, dim), lambda i, place: (i, 0)),
                whole_vmem(),
            ],
            [pltpu.VMEM((2 * dim, LANES), F32)],
        ),
        out_shape=[
            jax.ShapeDtypeStruct((count * SEQ, dim), BF),
            jax.ShapeDtypeStruct((8, dim), F32),
        ],
        compiler_params=params(),
        name="input_grad",
    )(place, tokens, dhidden, *pieces, *weights, vec)


def mlp_call(place, hidden, cotangent, weights, vec, bup, seqs, block):
    count, dim = hidden.shape[:2]
    steps = count // seqs
    units = weights[0].shape[1]
    shape = jax.ShapeDtypeStruct
    return pl.pallas_call(
        functools.partial(mlp_kernel, seqs, block),
        grid_spec=prefetch(
            (steps,),
            [placed_seq_block(seqs, dim, SEQ), row_block(seqs, dim, steps)] + [whole_vmem()] * 6,
            [
                pl.BlockSpec((seqs * SEQ, dim), lambda i, place: (i, 0)),
                placed_seq_block(seqs, dim, SEQ),
            ]
            + [whole_vmem()] * 2,
            [
                pltpu.VMEM((2 * units, dim), BF),
                pltpu.VMEM((dim, 2 * units), BF),
                pltpu.VMEM((dim, 2 * units), F32),
                pltpu.VMEM((2 * units, dim), F32),
                pltpu.VMEM((4 * dim, LANES), F32),
                pltpu.VMEM((2 * units, LANES), F32),
            ],
        ),
        out_shape=[
            shape((count * SEQ, dim), BF),
            shape((count, dim, SEQ), BF),
            shape((2, 2 * units, dim), BF),
            shape((8, dim), F32),
        ],
        compiler_params=params(),
        name="feed_forward",
    )(place, hidden, cotangent, *weights, vec, bup)


def shifted(value, axis, count, shift):
    return lax.ppermute(value, axis, [(i, (i + shift) % count) for i in range(count)])


def gathered(value, count, axis):
    blocks = [value] + [shifted(value, "mp", count, -r) for r in range(1, count)]
    half = count // 2
    return [
        blocks[g * half] if half == 1 else jnp.concatenate(blocks[g * half : (g + 1) * half], axis)
        for g in range(2)
    ]


def total_of(blocks):
    total = blocks[0].astype(F32)
    for block in blocks[1:]:
        total = total + block.astype(F32)
    return total.astype(BF)


class DpSum:
    def __init__(self, count):
        self.count = count
        self.groups = []
        bit = 1
        while bit < count:
            size = min(4, count // bit)
            self.groups.append((bit, size))
            bit *= size

    def swap(self, value, distance):
        return lax.ppermute(value, "dp", [(i, i ^ distance) for i in range(self.count)])

    def place(self, bit, size):
        return (lax.axis_index("dp") // bit) % size

    def scatter(self, value, stage):
        bit, size = self.groups[stage]
        here = self.place(bit, size)
        parts = value.reshape(size, value.shape[0] // size, value.shape[1])
        pick = lambda m: lax.dynamic_index_in_dim(parts, here ^ m, 0, keepdims=False)
        return [pick(0)] + [self.swap(pick(m), m * bit) for m in range(1, size)]

    def gather(self, value, stage):
        bit, size = self.groups[stage]
        return [value] + [self.swap(value, m * bit) for m in range(1, size)]

    def join(self, blocks, stage):
        bit, size = self.groups[stage]
        here = self.place(bit, size)
        whole = jnp.zeros((size,) + blocks[0].shape, blocks[0].dtype)
        for m, block in enumerate(blocks):
            whole = lax.dynamic_update_index_in_dim(whole, block, here ^ m, 0)
        return whole.reshape(-1, blocks[0].shape[1])


def body(mp, dp, *args):
    (tokens, gain1, shift1, wq, bq, wk, bk, wv, bv, wo, bo) = args[:11]
    (gain2, shift2, wu, bu, wd, bd, cotangent) = args[11:]
    rows, dim = tokens.shape
    local = wq.shape[1]
    units = wu.shape[1]
    own = rows // mp
    per = mp // 2
    me = lax.axis_index("mp")
    place = me.astype(jnp.int32).reshape(1)
    tie = lax.optimization_barrier
    dp_sum = DpSum(dp)

    weights = []
    for w in (wq, wk, wv):
        weights += gathered(w, mp, 1)
    weights += gathered(wo, mp, 0)
    small = jnp.concatenate([bq, bk, bv, bu])
    blocks = [small] + [shifted(small, "mp", mp, -r) for r in range(1, mp)]
    mlp_weights = gathered(wu, mp, 1) + gathered(wd, mp, 0)
    spread = lambda lo, hi: jnp.concatenate([b[lo:hi] for b in blocks])
    over = lambda vector: jnp.broadcast_to(vector[:, None], (vector.shape[0], LANES))
    vec1 = over(
        jnp.concatenate(
            [gain1, shift1] + [spread(i * local, (i + 1) * local) for i in range(3)] + [bo]
        )
    )
    vec2 = over(jnp.concatenate([gain2, shift2, bd]))
    bup = over(spread(3 * local, 3 * local + units))

    def whole(part, others):
        full = jnp.zeros((rows, dim), BF)
        for r, block in enumerate([part] + others):
            full = lax.dynamic_update_slice_in_dim(full, block, ((me - r) % mp) * own, 0)
        return full

    def spread_out(part):
        return [shifted(part, "mp", mp, r) for r in range(1, mp)]

    def ff_piece(grad, r):
        g, j = divmod(r, per)
        if per == 1:
            return grad[g]
        up = grad[g, : per * units].reshape(-1, dim, dim)
        up = jnp.concatenate(list(up), axis=1)[:, j * units : (j + 1) * units]
        down = grad[g, per * units + j * units : per * units + (j + 1) * units]
        return jnp.concatenate([up.reshape(-1, dim), down], axis=0)

    def at_piece(grads, r):
        g, j = divmod(r, per)
        if per == 1:
            return jnp.concatenate([grad[g] for grad in grads], axis=0)
        parts = []
        for index in range(3):
            block = [grad[g, index * dim : (index + 1) * dim] for grad in grads]
            block = jnp.concatenate(block, axis=1)[:, j * local : (j + 1) * local]
            parts.append(block.reshape(-1, LANES))
        block = [grad[g, 3 * dim :].reshape(-1, LANES, LANES) for grad in grads]
        block = jnp.concatenate([jnp.concatenate(list(b), axis=1) for b in block], axis=0)
        parts.append(block[j * local : (j + 1) * local].reshape(-1, LANES))
        return jnp.concatenate(parts, axis=0)

    def mp_send(piece):
        return [piece(0)] + [shifted(piece(r), "mp", mp, r) for r in range(1, mp)]

    *saved, first, hidden = attn_call(place, tokens, own, weights, vec1, 2)
    hidden, mlp_weights = tie((hidden, mlp_weights))
    out, low, grad_ff, vec_ff = mlp_call(place, hidden, cotangent, mlp_weights, vec2, bup, 2, 512)

    ff = mp_send(lambda r: ff_piece(grad_ff, r))
    outs = spread_out(out)
    low, ff[0], out = tie((low, ff[0], out))
    dq0, dk0, dv0, grad0, vec_at0 = grad_call(0, low, first, saved, weights[6:], 2)
    ff, outs, dq0 = tie((ff, outs, dq0))
    ff = dp_sum.scatter(total_of(ff), 0)
    out_full = whole(out, outs)
    if per == 1:
        at0 = mp_send(lambda r: at_piece([grad0], r))
    low, ff[0] = tie((low, ff[0]))
    dq1, dk1, dv1, grad1, vec_at1 = grad_call(1, low, first, saved, weights[6:], 2)
    ff, dq1 = tie((ff, dq1))
    ff = dp_sum.scatter(total_of(ff), 1)
    if per == 1:
        at1 = mp_send(lambda r: at_piece([grad1], r))
    low, ff[0] = tie((low, ff[0]))
    tgrad, vec_in = input_call(
        place, tokens, low, [dq0, dk0, dv0, dq1, dk1, dv1], weights[:6], vec1, 2
    )
    tgrads = spread_out(tgrad)

    same = jnp.concatenate([vec_ff[:4].reshape(-1), vec_in[:2].reshape(-1)])
    gbup = vec_ff[4:].reshape(-1)
    bias = []
    for index in range(3):
        chunks = [v[2 * index + c] for c in range(2) for v in (vec_at0, vec_at1)]
        bias.append(jnp.concatenate(chunks))

    def vec_piece(r):
        vector = jnp.concatenate(
            [same] + [b[r * local : (r + 1) * local] for b in bias] + [gbup[r * units : (r + 1) * units]]
        )
        size = -(-vector.shape[0] // (16 * dp * LANES)) * (16 * dp * LANES)
        return jnp.pad(vector, (0, size - vector.shape[0])).reshape(-1, LANES).astype(BF)

    ff, tgrad = tie((ff, tgrad))
    if per == 1:
        vecs = mp_send(vec_piece)
        at = jnp.concatenate([total_of(at0), total_of(at1), total_of(vecs)], axis=0)
    else:
        at = total_of(
            mp_send(lambda r: jnp.concatenate([at_piece([grad0, grad1], r), vec_piece(r)], axis=0))
        )
    stages = len(dp_sum.groups)
    for stage in range(2, stages):
        ff = dp_sum.scatter(total_of(ff), stage)
    ff = total_of(ff)
    for stage in range(stages):
        at = total_of(dp_sum.scatter(at, stage))
    for stage in reversed(range(stages)):
        ff = dp_sum.join(dp_sum.gather(ff, stage), stage)
        at = dp_sum.join(dp_sum.gather(at, stage), stage)
    ff, at = ff.astype(F32), at.astype(F32)

    if per == 1:
        g_up = jnp.concatenate(list(ff[:units].reshape(-1, dim, dim)), axis=1)
        tall = 4 * dim
        halves = [at[:tall], at[tall : 2 * tall]]
        g_qkv = [
            jnp.concatenate([h[i * dim : (i + 1) * dim] for h in halves], axis=1) for i in range(3)
        ]
        g_out = jnp.concatenate(
            [
                jnp.concatenate(list(h[3 * dim :].reshape(-1, LANES, LANES)), axis=1)
                for h in halves
            ],
            axis=0,
        )
        used = 2 * tall
    else:
        g_up = ff[:units].reshape(dim, units)
        each = dim * local // LANES
        g_qkv = [at[i * each : (i + 1) * each].reshape(dim, local) for i in range(3)]
        g_out = at[3 * each : 4 * each].reshape(local, dim)
        used = 4 * each
    g_down = ff[units:]
    vector = at[used:].reshape(-1)
    g_same = [vector[i * dim : (i + 1) * dim] for i in range(6)]
    base = 6 * dim
    g_bias = [vector[base + i * local : base + (i + 1) * local] for i in range(3)]
    g_bup = vector[base + 3 * local : base + 3 * local + units]
    return (
        out_full,
        whole(tgrad, tgrads),
        g_same[4],
        g_same[5],
        g_qkv[0],
        g_bias[0],
        g_qkv[1],
        g_bias[1],
        g_qkv[2],
        g_bias[2],
        g_out,
        g_same[3],
        g_same[0],
        g_same[1],
        g_up,
        g_bup,
        g_down,
        g_same[2],
    )


def solution(mesh):
    split = P("dp", None)
    columns, some, lines = P(None, "mp"), P("mp"), P("mp", None)
    return jax.shard_map(
        functools.partial(body, mesh.shape["mp"], mesh.shape["dp"]),
        mesh=mesh,
        in_specs=(split, P(), P(), columns, some, columns, some, columns, some, lines, P())
        + (P(), P(), columns, some, lines, P(), split),
        out_specs=(split, split, P(), P(), columns, some, columns, some, columns, some, lines)
        + (P(), P(), P(), columns, some, lines, P()),
        check_vma=False,
    )
```

```python
import functools
import math

import jax
import jax.numpy as jnp
from jax import lax
from jax.experimental import pallas as pl
from jax.experimental.pallas import tpu as pltpu
from jax.sharding import PartitionSpec as P

HEAD_DIM = 64
SEQ = 256
HALF = SEQ // 2
LANES = 128
BF = jnp.bfloat16
F32 = jnp.float32
VMEM_LIMIT = 60 * 1024 * 1024


def dot(left, right):
    return jnp.dot(left, right, preferred_element_type=F32)


def tail_dot(left, right):
    return lax.dot_general(left, right, (((1,), (1,)), ((), ())), preferred_element_type=F32)


def turned(block):
    return block.astype(F32).T.astype(BF)


def wide(column, lanes):
    return jnp.concatenate([column] * (lanes // LANES), axis=1)


def lane_fold(rows):
    total = rows[:, :LANES]
    for start in range(LANES, rows.shape[1], LANES):
        total = total + rows[:, start : start + LANES]
    return total


def as_column(row):
    return jnp.broadcast_to(row, (LANES, row.shape[1])).T


def as_row(sums):
    return jnp.sum(sums.T, axis=0, keepdims=True)


def norm_plain(x):
    center = x - jnp.mean(x, axis=0, keepdims=True)
    factor = lax.rsqrt(jnp.mean(center * center, axis=0, keepdims=True) + 1e-05)
    return center * factor, factor


def norm_back(grad, plain, factor, gain):
    scaled = grad * gain
    return factor * (
        scaled
        - jnp.mean(scaled, axis=0, keepdims=True)
        - plain * jnp.mean(scaled * plain, axis=0, keepdims=True)
    )


def upper_mask():
    return lax.broadcasted_iota(jnp.int32, (HALF, HALF), 0) <= lax.broadcasted_iota(
        jnp.int32, (HALF, HALF), 1
    )


def smooth(scores):
    square = scores * scores + 1.0
    inverse = lax.rsqrt(square)
    return inverse, square * inverse


def pair_diag(left, right):
    zero = jnp.zeros_like(left)
    return jnp.concatenate(
        [jnp.concatenate([left, zero], axis=1), jnp.concatenate([zero, right], axis=1)], axis=0
    )


def pair_near_far(rows):
    left, right = rows[:HEAD_DIM], rows[HEAD_DIM:]
    return (
        pair_diag(left[:, :HALF], right[:, :HALF]),
        pair_diag(left[:, HALF:], right[:, HALF:]),
    )


def attend(scores, mask):
    inverse, root = smooth(scores)
    if scores.shape[0] > HALF:
        diagonal = jnp.where(mask, root[HALF:], -1e30)
        magnitude = jnp.concatenate([root[:HALF], diagonal], axis=0)
    else:
        magnitude = jnp.where(mask, root, -1e30)
    top = jnp.max(magnitude, axis=0, keepdims=True)
    expo = jnp.exp(magnitude - top)
    probs = expo * (1.0 / jnp.sum(expo, axis=0, keepdims=True))
    sign = scores * inverse
    slope = inverse * inverse * inverse + sign * sign
    return (sign * probs).astype(BF), (probs * slope).astype(BF)


def attn_kernel(seqs, place, *refs):
    (tok, wq0, wq1, wk0, wk1, wv0, wv1, wo0, wo1) = refs[:9]
    gain1, shift1, bout, small0, small1 = refs[9:14]
    (query_o, keys_o, values_o, mixed_o, signed_o, slope_o, first_o, hidden_o) = refs[14:22]
    wqkv_t, wo_t, vec = refs[22:25]
    dim = tok.shape[1]
    lanes = seqs * SEQ

    @pl.when(pl.program_id(0) == 0)
    def _():
        part = dim // 2
        for index, ref in enumerate((wq0, wq1, wk0, wk1, wv0, wv1)):
            wqkv_t[index * part : (index + 1) * part, :] = turned(ref[...])
        wo_t[:, :part] = turned(wo0[...])
        wo_t[:, part:] = turned(wo1[...])
        for index, ref in ((0, gain1), (1, shift1), (5, bout)):
            vec[index * dim : (index + 1) * dim, :] = as_column(ref[...])
        for index in range(3):
            for c, ref in enumerate((small0, small1)):
                start = (2 + index) * dim + c * part
                vec[start : start + part, :] = as_column(ref[:, index * part : (index + 1) * part])

    half = lax.broadcasted_iota(jnp.int32, (HALF, SEQ), 1)
    mask = lax.broadcasted_iota(jnp.int32, (HALF, SEQ), 0) <= jnp.where(half < HALF, half, half - HALF)
    pairs = dim // LANES
    x = tok[...].astype(F32).T
    plain, _ = norm_plain(x)
    first = (plain * wide(vec[0:dim, :], lanes) + wide(vec[dim : 2 * dim, :], lanes)).astype(BF)
    outs = []
    for index in range(3):
        made = dot(wqkv_t[index * dim : (index + 1) * dim, :], first)
        made = made + wide(vec[(2 + index) * dim : (3 + index) * dim, :], lanes)
        made = made.astype(BF)
        if index == 0:
            made = made * jnp.asarray(1.0 / math.sqrt(HEAD_DIM), BF)
        outs.append(made)
    query, keys, values = outs
    mixed_all = []
    for s in range(seqs):
        span = slice(s * SEQ, (s + 1) * SEQ)
        first_o[s] = first[:, span]
        k_nat = turned(keys[:, span])
        parts = []
        for p in range(pairs):
            rows = slice(p * LANES, (p + 1) * LANES)
            c, g = divmod(p, 2)
            query_o[s, c, g], keys_o[s, c, g] = query[rows, span], keys[rows, span]
            values_o[s, c, g] = values[rows, span]
            near_q, far_q = pair_near_far(query[rows, span])
            kp = k_nat[:, rows]
            near, near_g = attend(dot(kp[:HALF], near_q), mask)
            far, far_g = attend(dot(kp, far_q), mask)
            signed_o[s, c, g, :HALF], signed_o[s, c, g, HALF:] = near, far
            slope_o[s, c, g, :HALF], slope_o[s, c, g, HALF:] = near_g, far_g
            v = values[rows, span]
            near_m, far_m = dot(v[:, :HALF], near), dot(v, far)
            made = jnp.concatenate(
                [
                    jnp.concatenate([near_m[:HEAD_DIM, :HALF], far_m[:HEAD_DIM, :HALF]], axis=1),
                    jnp.concatenate([near_m[HEAD_DIM:, HALF:], far_m[HEAD_DIM:, HALF:]], axis=1),
                ],
                axis=0,
            ).astype(BF)
            mixed_o[s, c, g] = made
            parts.append(made)
        mixed_all.append(jnp.concatenate(parts, axis=0))
    mixed = jnp.concatenate(mixed_all, axis=1)
    hidden = x + dot(wo_t[...], mixed) + wide(vec[5 * dim : 6 * dim, :], lanes)
    for s in range(seqs):
        hidden_o[s] = hidden[:, s * SEQ : (s + 1) * SEQ]


def mlp_kernel(seqs, block, place, *refs):
    (hid, cot, wu0, wu1, wd0, wd1, gain2, shift2, small0, small1) = refs[:10]
    (act_o, low_o, own_o, other_o, gvec_o) = refs[10:15]
    wu_t, gup, gdown, gvec, gbup, vec, bup = refs[15:22]
    dim = hid.shape[1]
    units = wu0.shape[1]
    lanes = seqs * SEQ
    step = pl.program_id(0)

    @pl.when(step == 0)
    def _():
        for index, (up, small) in enumerate(((wu0, small0), (wu1, small1))):
            rows = slice(index * units, (index + 1) * units)
            wu_t[rows, :] = turned(up[...])
            bup[rows, :] = as_column(small[:, small.shape[1] - units :])
        for index, ref in enumerate((gain2, shift2)):
            vec[index * dim : (index + 1) * dim, :] = as_column(ref[...])
        gup[...] = jnp.zeros_like(gup)
        gdown[...] = jnp.zeros_like(gdown)
        gvec[...] = jnp.zeros_like(gvec)
        gbup[...] = jnp.zeros_like(gbup)

    hidden = jnp.concatenate([hid[s] for s in range(seqs)], axis=1)
    grad_out = cot[...].astype(F32).T
    grad_low = grad_out.astype(BF)
    gain = wide(vec[0:dim, :], lanes)
    plain, factor = norm_plain(hidden)
    second = (plain * gain + wide(vec[dim : 2 * dim, :], lanes)).astype(BF)
    dnorm = None
    for start in range(0, 2 * units, block):
        span = slice(start, start + block)
        half, inner = divmod(start, units)
        up_ref, down_ref = ((wu0, wd0), (wu1, wd1))[half]
        inner = slice(inner, inner + block)
        upper = dot(wu_t[span, :], second) + wide(bup[span, :], lanes)
        dact = dot(down_ref[inner, :], grad_low)
        cdf = 0.5 * lax.erf(upper * (1.0 / math.sqrt(2.0))) + 0.5
        density = jnp.exp(-0.5 * (upper * upper)) * (1.0 / math.sqrt(2.0 * math.pi))
        act = (upper * cdf).astype(BF)
        dup = (dact * (cdf + upper * density)).astype(BF)
        for s in range(seqs):
            act_o[s, span, :] = act[:, s * SEQ : (s + 1) * SEQ]
        gbup[span, :] += lane_fold(dup.astype(F32))
        dn_part = dot(up_ref[:, inner], dup)
        dnorm = dn_part if dnorm is None else dnorm + dn_part
        gup[:, span] += tail_dot(second, dup)
        gdown[span, :] += tail_dot(act, grad_low)
    gvec[0:dim, :] += lane_fold(dnorm * plain)
    gvec[dim : 2 * dim, :] += lane_fold(dnorm)
    gvec[2 * dim : 3 * dim, :] += lane_fold(grad_out)
    dhidden = grad_out + norm_back(dnorm, plain, factor, gain)
    gvec[3 * dim :, :] += lane_fold(dhidden)
    for s in range(seqs):
        low_o[s] = dhidden[:, s * SEQ : (s + 1) * SEQ].astype(BF)

    @pl.when(step == pl.num_programs(0) - 1)
    def _():
        for half, grad_o in enumerate((own_o, other_o)):
            for index in range(units // dim):
                start = half * units + index * dim
                grad_o[index * dim : (index + 1) * dim, :] = gup[:, start : start + dim].astype(BF)
            grad_o[units:, :] = gdown[half * units : (half + 1) * units, :].astype(BF)
        for index in range(4):
            gvec_o[index : index + 1, :] = as_row(gvec[index * dim : (index + 1) * dim, :])
        for index in range(2 * units // dim):
            gvec_o[4 + index : 5 + index, :] = as_row(gbup[index * dim : (index + 1) * dim, :])


def out_kernel(seqs, place, hid, act, wd0, wd1, bdown, out_o, whole_o, wd_t, vec):
    units = wd0.shape[0]

    @pl.when(pl.program_id(0) == 0)
    def _():
        wd_t[:, :units] = turned(wd0[...])
        wd_t[:, units:] = turned(wd1[...])
        vec[...] = as_column(bdown[...])

    for s in range(seqs):
        rows = slice(s * SEQ, (s + 1) * SEQ)
        out = hid[s] + dot(wd_t[...], act[s]) + wide(vec[...], SEQ)
        made = out.T.astype(BF)
        out_o[rows, :] = made
        whole_o[rows, :] = made


def ff_unpack_kernel(total, up_o, down_o):
    dim, units = up_o.shape
    for start in range(0, units, dim):
        up_o[:, start : start + dim] = total[start : start + dim, :].astype(F32)
    down_o[...] = total[units:, :].astype(F32)


def at_unpack_kernel(here, b0, b1, b2, b3, *refs):
    outs, hold = refs[:-1], refs[-1]
    size = b0.shape[0]
    for m, block in enumerate((b0, b1, b2, b3)):
        hold[here[m]] = block[...]
    rows = lambda start, count: [
        hold[k, max(start - k * size, 0) : min(start + count - k * size, size), :].astype(F32)
        for k in range(4)
        if start < (k + 1) * size and start + count > k * size
    ]
    get = lambda start, count: jnp.concatenate(rows(start, count), axis=0)
    dim = outs[0].shape[0]
    for g in range(2):
        base = g * 4 * dim
        for index in range(3):
            outs[index][:, g * LANES : (g + 1) * LANES] = get(base + index * dim, dim)
        for index in range(dim // LANES):
            outs[3][g * LANES : (g + 1) * LANES, index * LANES : (index + 1) * LANES] = get(
                base + 3 * dim + index * LANES, LANES
            )
    at = 8 * dim
    for out in outs[4:]:
        for start in range(0, out.shape[1], LANES):
            out[:, start : start + LANES] = get(at // 16 * 16, 16)[at % 16 : at % 16 + 1]
            at += 1


def grad_kernel(seqs, group, *refs):
    (low_i, first_i, query_i, keys_i, values_i, mixed_i, signed_i, slope_i) = refs[:8]
    wo0, wo1 = refs[8:10]
    (dq_o, dk_o, dv_o, own_o, other_o, gvec_o) = refs[10:16]
    gqkv, gout, gb = refs[16:19]
    dim = low_i.shape[1]
    part = 2 * LANES
    step = pl.program_id(0)
    scale = 1.0 / math.sqrt(HEAD_DIM)

    @pl.when(step == 0)
    def _():
        gqkv[...] = jnp.zeros_like(gqkv)
        gout[...] = jnp.zeros_like(gout)
        gb[...] = jnp.zeros_like(gb)

    place = slice(group * LANES, (group + 1) * LANES)
    first = jnp.concatenate([first_i[s] for s in range(seqs)], axis=1)
    low = jnp.concatenate([low_i[s] for s in range(seqs)], axis=1)
    dmixed = jnp.concatenate([dot(wo0[place, :], low), dot(wo1[place, :], low)], axis=0).astype(BF)
    mixed = jnp.concatenate(
        [
            jnp.concatenate([mixed_i[s, 0, 0], mixed_i[s, 1, 0]], axis=0)
            for s in range(seqs)
        ],
        axis=1,
    )
    dq_all, dk_all, dv_all = [], [], []
    for s in range(seqs):
        span = slice(s * SEQ, (s + 1) * SEQ)
        dq, dk, dv = [], [], []
        for c in range(2):
            rows = slice(c * LANES, (c + 1) * LANES)
            q, k = query_i[s, c, 0], keys_i[s, c, 0]
            dm = dmixed[rows, span]
            v_nat = turned(values_i[s, c, 0])
            near_q, far_q = pair_near_far(q)
            near_m, far_m = pair_near_far(dm)
            low_pair = []
            for index in range(2):
                keys = slice(0, HALF) if index == 0 else slice(0, SEQ)
                block = slice(0, HALF) if index == 0 else slice(HALF, HALF + SEQ)
                dsigned = dot(v_nat[keys], (near_m, far_m)[index])
                signed = signed_i[s, c, 0, block].astype(F32)
                row_dot = jnp.sum(signed * dsigned, axis=0, keepdims=True)
                dscores = slope_i[s, c, 0, block].astype(F32) * dsigned - signed * row_dot
                low_pair.append(dscores.astype(BF))
            near, far = low_pair
            near_p, far_p = dot(k[:, :HALF], near), dot(k, far)
            dq.append(
                jnp.concatenate(
                    [
                        jnp.concatenate([near_p[:HEAD_DIM, :HALF], far_p[:HEAD_DIM, :HALF]], axis=1),
                        jnp.concatenate([near_p[HEAD_DIM:, HALF:], far_p[HEAD_DIM:, HALF:]], axis=1),
                    ],
                    axis=0,
                )
            )
            near_p, far_p = tail_dot(near, near_q), tail_dot(far, far_q)
            dk.append(jnp.concatenate([far_p[:HALF] + near_p, far_p[HALF:]], axis=0))
            near_p = tail_dot(signed_i[s, c, 0, :HALF], near_m)
            far_p = tail_dot(signed_i[s, c, 0, HALF:], far_m)
            dv.append(jnp.concatenate([far_p[:HALF] + near_p, far_p[HALF:]], axis=0))
        dq_all.append((jnp.concatenate(dq, axis=0) * scale).astype(BF))
        dk_all.append(jnp.concatenate(dk, axis=1).astype(BF))
        dv_all.append(jnp.concatenate(dv, axis=1).astype(BF))
        dq_o[s], dk_o[s], dv_o[s] = dq_all[s], dk_all[s], dv_all[s]
    gout[...] += tail_dot(mixed, low)
    dq, dk, dv = jnp.concatenate(dq_all, axis=1), jnp.concatenate(dk_all, axis=0), jnp.concatenate(dv_all, axis=0)
    gqkv[:, :part] += tail_dot(first, dq)
    gqkv[:, part : 2 * part] += dot(first, dk)
    gqkv[:, 2 * part :] += dot(first, dv)
    gb[:part, :] += lane_fold(dq.astype(F32))
    for index, block in ((2, dk), (3, dv)):
        total = jnp.sum(block.astype(F32).reshape(-1, 8, part), axis=0)
        gb[index * LANES : index * LANES + 8, :] += total[:, :LANES]
        gb[index * LANES + 8 : index * LANES + 16, :] += total[:, LANES:]

    @pl.when(step == pl.num_programs(0) - 1)
    def _():
        for c, grad_o in enumerate((own_o, other_o)):
            for index in range(3):
                start = index * part + c * LANES
                grad_o[index * dim : (index + 1) * dim, :] = gqkv[:, start : start + LANES].astype(BF)
            for index in range(dim // LANES):
                start = 3 * dim + index * LANES
                grad_o[start : start + LANES, :] = gout[
                    c * LANES : (c + 1) * LANES, index * LANES : (index + 1) * LANES
                ].astype(BF)
            gvec_o[c : c + 1, :] = as_row(gb[c * LANES : (c + 1) * LANES, :])
            for index in (2, 3):
                rows = slice(index * LANES + 8 * c, index * LANES + 8 * c + 8)
                gvec_o[2 * index - 2 + c : 2 * index - 1 + c, :] = jnp.sum(gb[rows, :], axis=0, keepdims=True)


def input_kernel(seqs, place, *refs):
    tok, dhid, dq0, dk0, dv0, dq1, dk1, dv1 = refs[:8]
    wq0, wq1, wk0, wk1, wv0, wv1, gain1 = refs[8:15]
    tgrad_o, whole_o, gvec_o = refs[15:18]
    gvec, vec = refs[18:20]
    dim = tok.shape[1]

    @pl.when(pl.program_id(0) == 0)
    def _():
        gvec[...] = jnp.zeros_like(gvec)
        vec[...] = as_column(gain1[...])

    gain = wide(vec[...], SEQ)
    for s in range(seqs):
        rows = slice(s * SEQ, (s + 1) * SEQ)
        dnorm = None
        for c, (wq, wk, wv) in enumerate(((wq0, wk0, wv0), (wq1, wk1, wv1))):
            lanes = slice(c * LANES, (c + 1) * LANES)
            dq = jnp.concatenate([dq0[s, lanes, :], dq1[s, lanes, :]], axis=0)
            dk = jnp.concatenate([dk0[s, :, lanes], dk1[s, :, lanes]], axis=1)
            dv = jnp.concatenate([dv0[s, :, lanes], dv1[s, :, lanes]], axis=1)
            made = dot(wq[...], dq) + tail_dot(wk[...], dk) + tail_dot(wv[...], dv)
            dnorm = made if dnorm is None else dnorm + made
        plain, factor = norm_plain(tok[rows, :].astype(F32).T)
        gvec[0:dim, :] += lane_fold(dnorm * plain)
        gvec[dim : 2 * dim, :] += lane_fold(dnorm)
        tgrad = dhid[s].astype(F32) + norm_back(dnorm, plain, factor, gain)
        made = tgrad.T.astype(BF)
        tgrad_o[rows, :] = made
        whole_o[rows, :] = made

    @pl.when(pl.program_id(0) == pl.num_programs(0) - 1)
    def _():
        for index in range(2):
            gvec_o[index : index + 1, :] = as_row(gvec[index * dim : (index + 1) * dim, :])


def whole_vmem():
    return pl.BlockSpec(memory_space=pltpu.VMEM)


def seq_block(seqs, *dims):
    return pl.BlockSpec((seqs,) + dims, lambda i: (i,) + (0,) * len(dims))


def params():
    return pltpu.CompilerParams(
        dimension_semantics=("arbitrary",), vmem_limit_bytes=VMEM_LIMIT
    )


def prefetch(grid, in_specs, out_specs, scratch=()):
    return pltpu.PrefetchScalarGridSpec(
        num_scalar_prefetch=1, grid=grid, in_specs=in_specs, out_specs=out_specs, scratch_shapes=scratch
    )


def row_block(seqs, dim, steps):
    return pl.BlockSpec((seqs * SEQ, dim), lambda i, place: (place[0] * steps + i, 0))


def placed_seq_block(seqs, *dims):
    return pl.BlockSpec((seqs,) + dims, lambda i, place: (i,) + (0,) * len(dims))


def attn_call(place, tokens, own, weights, vectors, seqs):
    dim = tokens.shape[1]
    count = own // SEQ
    steps = count // seqs
    feat = (2, 2, LANES, SEQ)
    wide_block = (2, 2, HALF + SEQ, SEQ)
    shape = jax.ShapeDtypeStruct
    return pl.pallas_call(
        functools.partial(attn_kernel, seqs),
        grid_spec=prefetch(
            (steps,),
            [row_block(seqs, dim, steps)] + [whole_vmem()] * 13,
            [placed_seq_block(seqs, *feat)] * 4
            + [placed_seq_block(seqs, *wide_block)] * 2
            + [placed_seq_block(seqs, dim, SEQ)] * 2,
            [
                pltpu.VMEM((3 * dim, dim), BF),
                pltpu.VMEM((dim, dim), BF),
                pltpu.VMEM((6 * dim, LANES), F32),
            ],
        ),
        out_shape=[shape((count,) + feat, BF)] * 4
        + [shape((count,) + wide_block, BF)] * 2
        + [shape((count, dim, SEQ), BF), shape((count, dim, SEQ), F32)],
        compiler_params=params(),
        cost_estimate=pl.CostEstimate(flops=1, bytes_accessed=1, transcendentals=0),
        name="attn_forward",
    )(place, tokens, *weights, *vectors)


def grad_call(group, low, first, saved, weights, seqs):
    count, dim = low.shape[:2]
    steps = count // seqs
    one = lambda *dims: pl.BlockSpec((seqs, 2, 1) + dims, lambda i: (i, 0, group, 0, 0))
    shape = jax.ShapeDtypeStruct
    part = 2 * LANES
    return pl.pallas_call(
        functools.partial(grad_kernel, seqs, group),
        grid=(steps,),
        in_specs=[seq_block(seqs, dim, SEQ)] * 2
        + [one(LANES, SEQ)] * 4
        + [one(HALF + SEQ, SEQ)] * 2
        + [whole_vmem()] * 2,
        out_specs=[seq_block(seqs, part, SEQ), seq_block(seqs, SEQ, part), seq_block(seqs, SEQ, part)]
        + [whole_vmem()] * 3,
        out_shape=[
            shape((count, part, SEQ), BF),
            shape((count, SEQ, part), BF),
            shape((count, SEQ, part), BF),
            shape((4 * dim, LANES), BF),
            shape((4 * dim, LANES), BF),
            shape((8, LANES), F32),
        ],
        scratch_shapes=[
            pltpu.VMEM((dim, 3 * part), F32),
            pltpu.VMEM((part, dim), F32),
            pltpu.VMEM((4 * LANES, LANES), F32),
        ],
        compiler_params=params(),
        cost_estimate=pl.CostEstimate(flops=1, bytes_accessed=1, transcendentals=0),
        name="attn_backward",
    )(low, first, *saved, *weights)


def input_call(place, tokens, dhidden, pieces, weights, gain1, seqs):
    dim = tokens.shape[1]
    count = dhidden.shape[0]
    steps = count // seqs
    part = 2 * LANES
    trio = [
        placed_seq_block(seqs, part, SEQ),
        placed_seq_block(seqs, SEQ, part),
        placed_seq_block(seqs, SEQ, part),
    ]
    return pl.pallas_call(
        functools.partial(input_kernel, seqs),
        grid_spec=prefetch(
            (steps,),
            [row_block(seqs, dim, steps), placed_seq_block(seqs, dim, SEQ)]
            + trio * 2
            + [whole_vmem()] * 7,
            [
                pl.BlockSpec((seqs * SEQ, dim), lambda i, place: (i, 0)),
                row_block(seqs, dim, steps),
                whole_vmem(),
            ],
            [pltpu.VMEM((2 * dim, LANES), F32), pltpu.VMEM((dim, LANES), F32)],
        ),
        out_shape=[
            jax.ShapeDtypeStruct((count * SEQ, dim), BF),
            jax.ShapeDtypeStruct(tokens.shape, BF),
            jax.ShapeDtypeStruct((8, dim), F32),
        ],
        compiler_params=params(),
        cost_estimate=pl.CostEstimate(flops=1, bytes_accessed=1, transcendentals=0),
        name="input_grad",
    )(place, tokens, dhidden, *pieces, *weights, gain1)


def mlp_call(place, hidden, cotangent, weights, vectors, seqs, block):
    count, dim = hidden.shape[:2]
    steps = count // seqs
    units = weights[0].shape[1]
    shape = jax.ShapeDtypeStruct
    return pl.pallas_call(
        functools.partial(mlp_kernel, seqs, block),
        grid_spec=prefetch(
            (steps,),
            [placed_seq_block(seqs, dim, SEQ), row_block(seqs, dim, steps)] + [whole_vmem()] * 8,
            [placed_seq_block(seqs, 2 * units, SEQ), placed_seq_block(seqs, dim, SEQ)]
            + [whole_vmem()] * 3,
            [
                pltpu.VMEM((2 * units, dim), BF),
                pltpu.VMEM((dim, 2 * units), F32),
                pltpu.VMEM((2 * units, dim), F32),
                pltpu.VMEM((4 * dim, LANES), F32),
                pltpu.VMEM((2 * units, LANES), F32),
                pltpu.VMEM((2 * dim, LANES), F32),
                pltpu.VMEM((2 * units, LANES), F32),
            ],
        ),
        out_shape=[
            shape((count, 2 * units, SEQ), BF),
            shape((count, dim, SEQ), BF),
            shape((2 * units, dim), BF),
            shape((2 * units, dim), BF),
            shape((8, dim), F32),
        ],
        compiler_params=params(),
        cost_estimate=pl.CostEstimate(flops=1, bytes_accessed=1, transcendentals=0),
        name="feed_forward",
    )(place, hidden, cotangent, *weights, *vectors)


def out_call(place, hidden, act, weights, bdown, rows, seqs):
    count, dim = hidden.shape[:2]
    units = act.shape[1]
    steps = count // seqs
    return pl.pallas_call(
        functools.partial(out_kernel, seqs),
        grid_spec=prefetch(
            (steps,),
            [placed_seq_block(seqs, dim, SEQ), placed_seq_block(seqs, units, SEQ)] + [whole_vmem()] * 3,
            [
                pl.BlockSpec((seqs * SEQ, dim), lambda i, place: (i, 0)),
                row_block(seqs, dim, steps),
            ],
            [pltpu.VMEM((dim, units), BF), pltpu.VMEM((dim, LANES), F32)],
        ),
        out_shape=[
            jax.ShapeDtypeStruct((count * SEQ, dim), BF),
            jax.ShapeDtypeStruct((rows, dim), BF),
        ],
        compiler_params=params(),
        cost_estimate=pl.CostEstimate(flops=1, bytes_accessed=1, transcendentals=0),
        name="layer_out",
    )(place, hidden, act, *weights, bdown)


def ff_unpack_call(total, units):
    dim = total.shape[1]
    return pl.pallas_call(
        ff_unpack_kernel,
        in_specs=[whole_vmem()],
        out_specs=[whole_vmem()] * 2,
        out_shape=[
            jax.ShapeDtypeStruct((dim, units), F32),
            jax.ShapeDtypeStruct((units, dim), F32),
        ],
        compiler_params=pltpu.CompilerParams(vmem_limit_bytes=VMEM_LIMIT),
        name="ff_unpack",
    )(total)


def at_unpack_call(here, blocks, dim, local, sizes):
    shape = jax.ShapeDtypeStruct
    outs = [shape((dim, local), F32)] * 3 + [shape((local, dim), F32)]
    outs += [shape((1, n), F32) for n in sizes]
    return pl.pallas_call(
        at_unpack_kernel,
        in_specs=[pl.BlockSpec(memory_space=pltpu.SMEM)] + [whole_vmem()] * 4,
        out_specs=[whole_vmem()] * len(outs),
        out_shape=outs,
        scratch_shapes=[pltpu.VMEM((4,) + blocks[0].shape, BF)],
        compiler_params=pltpu.CompilerParams(vmem_limit_bytes=VMEM_LIMIT),
        name="at_unpack",
    )(here, *blocks)


def shifted(value, axis, count, shift):
    return lax.ppermute(value, axis, [(i, (i + shift) % count) for i in range(count)])


def gathered(value, count, axis):
    blocks = [value] + [shifted(value, "mp", count, -r) for r in range(1, count)]
    half = count // 2
    return [
        blocks[g * half] if half == 1 else jnp.concatenate(blocks[g * half : (g + 1) * half], axis)
        for g in range(2)
    ]


def total_of(blocks):
    total = blocks[0].astype(F32)
    for block in blocks[1:]:
        total = total + block.astype(F32)
    return total.astype(BF)


class DpSum:
    def __init__(self, count):
        self.count = count
        self.groups = []
        bit = 1
        while bit < count:
            size = min(4, count // bit)
            self.groups.append((bit, size))
            bit *= size

    def swap(self, value, distance):
        return lax.ppermute(value, "dp", [(i, i ^ distance) for i in range(self.count)])

    def place(self, bit, size):
        return (lax.axis_index("dp") // bit) % size

    def scatter(self, value, stage):
        bit, size = self.groups[stage]
        here = self.place(bit, size)
        parts = value.reshape(size, value.shape[0] // size, value.shape[1])
        pick = lambda m: lax.dynamic_index_in_dim(parts, here ^ m, 0, keepdims=False)
        return [pick(0)] + [self.swap(pick(m), m * bit) for m in range(1, size)]

    def gather(self, value, stage):
        bit, size = self.groups[stage]
        return [value] + [self.swap(value, m * bit) for m in range(1, size)]

    def join(self, blocks, stage):
        bit, size = self.groups[stage]
        here = self.place(bit, size)
        whole = jnp.zeros((size,) + blocks[0].shape, blocks[0].dtype)
        for m, block in enumerate(blocks):
            whole = lax.dynamic_update_index_in_dim(whole, block, here ^ m, 0)
        return whole.reshape(-1, blocks[0].shape[1])


def body(mp, dp, *args):
    (tokens, gain1, shift1, wq, bq, wk, bk, wv, bv, wo, bo) = args[:11]
    (gain2, shift2, wu, bu, wd, bd, cotangent) = args[11:]
    rows, dim = tokens.shape
    local = wq.shape[1]
    units = wu.shape[1]
    own = rows // mp
    per = mp // 2
    me = lax.axis_index("mp")
    place = me.astype(jnp.int32).reshape(1)
    tie = lax.optimization_barrier
    dp_sum = DpSum(dp)

    weights = []
    for w in (wq, wk, wv):
        weights += gathered(w, mp, 1)
    weights += gathered(wo, mp, 0)
    small = jnp.concatenate([bq, bk, bv, bu]).reshape(1, -1)
    smalls = [small] + [shifted(small, "mp", mp, -r) for r in range(1, mp)]
    if per > 1:
        cuts = [0, local, 2 * local, 3 * local, 3 * local + units]
        smalls = [
            jnp.concatenate(
                [
                    block[:, lo:hi]
                    for lo, hi in zip(cuts, cuts[1:])
                    for block in smalls[c * per : (c + 1) * per]
                ],
                axis=1,
            )
            for c in range(2)
        ]
    mlp_weights = gathered(wu, mp, 1) + gathered(wd, mp, 0)
    gain1, shift1, bo, gain2, shift2, bd = (
        v.reshape(1, -1) for v in (gain1, shift1, bo, gain2, shift2, bd)
    )

    def filled(full, others):
        for r, block in enumerate(others, 1):
            full = lax.dynamic_update_slice_in_dim(full, block, ((me - r) % mp) * own, 0)
        return full

    def spread_out(part):
        return [shifted(part, "mp", mp, r) for r in range(1, mp)]

    def ff_piece(grad, r):
        g, j = divmod(r, per)
        if per == 1:
            return grad[g]
        up = grad[g][: per * units].reshape(-1, dim, dim)
        up = jnp.concatenate(list(up), axis=1)[:, j * units : (j + 1) * units]
        down = grad[g][per * units + j * units : per * units + (j + 1) * units]
        return jnp.concatenate([up.reshape(-1, dim), down], axis=0)

    def at_piece(grads, r):
        g, j = divmod(r, per)
        if per == 1:
            return jnp.concatenate([grad[g] for grad in grads], axis=0)
        parts = []
        for index in range(3):
            block = [grad[g][index * dim : (index + 1) * dim] for grad in grads]
            block = jnp.concatenate(block, axis=1)[:, j * local : (j + 1) * local]
            parts.append(block.reshape(-1, LANES))
        block = [grad[g][3 * dim :].reshape(-1, LANES, LANES) for grad in grads]
        block = jnp.concatenate([jnp.concatenate(list(b), axis=1) for b in block], axis=0)
        parts.append(block[j * local : (j + 1) * local].reshape(-1, LANES))
        return jnp.concatenate(parts, axis=0)

    def mp_send(piece):
        return [piece(0)] + [shifted(piece(r), "mp", mp, r) for r in range(1, mp)]

    *saved, first, hidden = attn_call(
        place, tokens, own, weights, [gain1, shift1, bo] + smalls, 2
    )
    hidden, mlp_weights = tie((hidden, mlp_weights))
    act, low, *grad_ff, vec_ff = mlp_call(
        place, hidden, cotangent, mlp_weights, [gain2, shift2] + smalls, 2, 512
    )
    ff = total_of(mp_send(lambda r: ff_piece(grad_ff, r)))
    low, ff = tie((low, ff))
    ff = lax.psum(ff, "dp")
    dq0, dk0, dv0, *grad0, vec_at0 = grad_call(0, low, first, saved, weights[6:], 2)
    at0 = mp_send(lambda r: at_piece([grad0], r)) if per == 1 else []
    low, at0 = tie((low, at0))
    dq1, dk1, dv1, *grad1, vec_at1 = grad_call(1, low, first, saved, weights[6:], 2)
    at0, dq1 = tie((at0, dq1))
    def finish(low, dq1, at0, act):
        at1 = mp_send(lambda r: at_piece([grad1], r)) if per == 1 else []
        low, at1, dq1 = tie((low, at1, dq1))
        pieces = [dq0, dk0, dv0, dq1, dk1, dv1]
        tgrad, tgrad_full, vec_in = input_call(place, tokens, low, pieces, weights[:6], gain1, 2)
        at1, tgrad = tie((at1, tgrad))

        vecs = [vec_ff[:4].reshape(-1, LANES), vec_in[:2].reshape(-1, LANES)]
        if per == 1:
            grow = -(-(6 * dim + 3 * local + units) // (16 * dp * LANES)) * 16 * dp

            def vec_piece(r):
                gb = vec_ff[4 + r * units // dim : 4 + (r + 1) * units // dim].reshape(-1, LANES)
                bias = [v[2 * i + r : 2 * i + r + 1] for i in range(3) for v in (vec_at0, vec_at1)]
                made = jnp.concatenate(vecs + bias + [gb], axis=0)
                return jnp.pad(made, ((0, grow - made.shape[0]), (0, 0))).astype(BF)

            at = jnp.concatenate(
                [total_of(at0), total_of(at1), total_of(mp_send(vec_piece))], axis=0
            )
        else:
            same = jnp.concatenate([v.reshape(-1) for v in vecs])
            gbup = vec_ff[4:].reshape(-1)
            bias = [
                jnp.concatenate([v[2 * i + c] for c in range(2) for v in (vec_at0, vec_at1)])
                for i in range(3)
            ]

            def all_piece(r):
                vector = jnp.concatenate(
                    [same]
                    + [b[r * local : (r + 1) * local] for b in bias]
                    + [gbup[r * units : (r + 1) * units]]
                )
                size = -(-vector.shape[0] // (16 * dp * LANES)) * (16 * dp * LANES)
                vector = jnp.pad(vector, (0, size - vector.shape[0])).reshape(-1, LANES).astype(BF)
                return jnp.concatenate([at_piece([grad0, grad1], r), vector], axis=0)

            at = total_of(mp_send(all_piece))
        at = dp_sum.scatter(at, 0)
        tgrads = spread_out(tgrad)
        act, at[0], tgrad = tie((act, at[0], tgrad))
        out, out_full = out_call(place, hidden, act, mlp_weights[2:], bd, rows, 2)
        at, out, tgrads = tie((at, out, tgrads))
        at = total_of(at)
        stages = len(dp_sum.groups)
        for stage in range(1, stages):
            at = total_of(dp_sum.scatter(at, stage))
        outs = spread_out(out)
        tgrad_full = filled(tgrad_full, tgrads)
        for stage in reversed(range(1, stages)):
            at = dp_sum.join(dp_sum.gather(at, stage), stage)
        at = dp_sum.gather(at, 0)

        sizes = [dim] * 6 + [local] * 3 + [units]
        if per == 1 and len(at) == 4:
            here = dp_sum.place(*dp_sum.groups[0]).astype(jnp.int32) ^ jnp.arange(4, dtype=jnp.int32)
            *g_at, g0, g1, g2, g3, g4, g5, q0, q1, q2, g_bup = at_unpack_call(
                here, at, dim, local, sizes
            )
            g_qkv, g_out = g_at[:3], g_at[3]
            g_same = [v.reshape(-1) for v in (g0, g1, g2, g3, g4, g5)]
            g_bias = [v.reshape(-1) for v in (q0, q1, q2)]
            g_bup = g_bup.reshape(-1)
        else:
            at = dp_sum.join(at, 0).astype(F32)
            each = dim * local // LANES
            g_qkv = [at[i * each : (i + 1) * each].reshape(dim, local) for i in range(3)]
            g_out = at[3 * each : 4 * each].reshape(local, dim)
            vector = at[4 * each :].reshape(-1)
            parts = []
            for size in sizes:
                parts.append(vector[:size])
                vector = vector[size:]
            g_same, g_bias, g_bup = parts[:6], parts[6:9], parts[9]
        out_full = filled(out_full, outs)
        return (out_full, tgrad_full, list(g_same), list(g_qkv), list(g_bias), g_out, g_bup)

    blank = jax.eval_shape(finish, low, dq1, at0, act)
    out_full, tgrad_full, g_same, g_qkv, g_bias, g_out, g_bup = lax.cond(
        lax.axis_index("dp") != dp,
        finish,
        lambda *_: jax.tree.map(lambda v: jnp.zeros(v.shape, v.dtype), blank),
        low,
        dq1,
        at0,
        act,
    )
    if per == 1:
        g_up, g_down = ff_unpack_call(ff, units)
    else:
        ff = ff.astype(F32)
        g_up = ff[:units].reshape(dim, units)
        g_down = ff[units:]
    return (
        out_full,
        tgrad_full,
        g_same[4],
        g_same[5],
        g_qkv[0],
        g_bias[0],
        g_qkv[1],
        g_bias[1],
        g_qkv[2],
        g_bias[2],
        g_out,
        g_same[3],
        g_same[0],
        g_same[1],
        g_up,
        g_bup,
        g_down,
        g_same[2],
    )


def solution(mesh):
    split = P("dp", None)
    columns, some, lines = P(None, "mp"), P("mp"), P("mp", None)
    return jax.shard_map(
        functools.partial(body, mesh.shape["mp"], mesh.shape["dp"]),
        mesh=mesh,
        in_specs=(split, P(), P(), columns, some, columns, some, columns, some, lines, P())
        + (P(), P(), columns, some, lines, P(), split),
        out_specs=(split, split, P(), P(), columns, some, columns, some, columns, some, lines)
        + (P(), P(), P(), columns, some, lines, P()),
        check_vma=False,
    )
```

```python
import functools
import math

import jax
import jax.numpy as jnp
from jax import lax
from jax.experimental import pallas as pl
from jax.experimental.pallas import tpu as pltpu
from jax.sharding import PartitionSpec as P

HEAD_DIM = 64
SEQ = 256
HALF = SEQ // 2
LANES = 128
BF = jnp.bfloat16
F32 = jnp.float32
VMEM_LIMIT = 60 * 1024 * 1024
SEQS = {"attn": 4, "mlp": 2, "grad": 2, "input": 4, "out": 4}


def dot(left, right):
    return jnp.dot(left, right, preferred_element_type=F32)


def tail_dot(left, right):
    return lax.dot_general(left, right, (((1,), (1,)), ((), ())), preferred_element_type=F32)


def turned(block):
    return block.astype(F32).T.astype(BF)


def wide(column, lanes):
    return jnp.concatenate([column] * (lanes // LANES), axis=1)


def lane_fold(rows):
    total = rows[:, :LANES]
    for start in range(LANES, rows.shape[1], LANES):
        total = total + rows[:, start : start + LANES]
    return total


def as_column(row):
    return jnp.broadcast_to(row, (LANES, row.shape[1])).T


def as_row(sums):
    return jnp.sum(sums.T, axis=0, keepdims=True)


def norm_plain(x):
    center = x - jnp.mean(x, axis=0, keepdims=True)
    factor = lax.rsqrt(jnp.mean(center * center, axis=0, keepdims=True) + 1e-05)
    return center * factor, factor


def norm_back(grad, plain, factor, gain):
    scaled = grad * gain
    return factor * (
        scaled
        - jnp.mean(scaled, axis=0, keepdims=True)
        - plain * jnp.mean(scaled * plain, axis=0, keepdims=True)
    )


def upper_mask():
    return lax.broadcasted_iota(jnp.int32, (HALF, HALF), 0) <= lax.broadcasted_iota(
        jnp.int32, (HALF, HALF), 1
    )


def smooth(scores):
    square = scores * scores + 1.0
    inverse = lax.rsqrt(square)
    return inverse, square * inverse


def pair_diag(left, right):
    zero = jnp.zeros_like(left)
    return jnp.concatenate(
        [jnp.concatenate([left, zero], axis=1), jnp.concatenate([zero, right], axis=1)], axis=0
    )


def pair_near_far(rows):
    left, right = rows[:HEAD_DIM], rows[HEAD_DIM:]
    return (
        pair_diag(left[:, :HALF], right[:, :HALF]),
        pair_diag(left[:, HALF:], right[:, HALF:]),
    )


def attend(scores, mask):
    inverse, root = smooth(scores)
    if scores.shape[0] > HALF:
        diagonal = jnp.where(mask, root[HALF:], -1e30)
        magnitude = jnp.concatenate([root[:HALF], diagonal], axis=0)
    else:
        magnitude = jnp.where(mask, root, -1e30)
    top = jnp.max(magnitude, axis=0, keepdims=True)
    expo = jnp.exp(magnitude - top)
    norm = 1.0 / jnp.sum(expo, axis=0, keepdims=True)
    low_expo, sign, low = expo.astype(BF), (scores * inverse).astype(BF), inverse.astype(BF)
    return sign * low_expo, (low * low * low + sign * sign) * low_expo, norm


def attn_kernel(seqs, place, *refs):
    (tok, wq0, wq1, wk0, wk1, wv0, wv1, wo0, wo1) = refs[:9]
    gain1, shift1, bout, small0, small1 = refs[9:14]
    (query_o, keys_o, values_o, mixed_o, signed_o, slope_o, norm_o, first_o, hidden_o) = refs[14:23]
    wqkv_t, wo_t, vec = refs[23:26]
    dim = tok.shape[1]
    lanes = seqs * SEQ

    @pl.when(pl.program_id(0) == 0)
    def _():
        part = dim // 2
        for index, ref in enumerate((wq0, wq1, wk0, wk1, wv0, wv1)):
            wqkv_t[index * part : (index + 1) * part, :] = turned(ref[...])
        wo_t[:, :part] = turned(wo0[...])
        wo_t[:, part:] = turned(wo1[...])
        for index, ref in ((0, gain1), (1, shift1), (5, bout)):
            vec[index * dim : (index + 1) * dim, :] = as_column(ref[...])
        for index in range(3):
            for c, ref in enumerate((small0, small1)):
                start = (2 + index) * dim + c * part
                vec[start : start + part, :] = as_column(ref[:, index * part : (index + 1) * part])

    half = lax.broadcasted_iota(jnp.int32, (HALF, SEQ), 1)
    mask = lax.broadcasted_iota(jnp.int32, (HALF, SEQ), 0) <= jnp.where(half < HALF, half, half - HALF)
    pairs = dim // LANES
    scale = jnp.asarray(1.0 / math.sqrt(HEAD_DIM), BF)

    def prepare(s):
        x = tok[s * SEQ : (s + 1) * SEQ, :].astype(F32).T
        plain, _ = norm_plain(x)
        first = (plain * wide(vec[0:dim, :], SEQ) + wide(vec[dim : 2 * dim, :], SEQ)).astype(BF)
        first_o[s] = first
        return first

    def project(s, p, first):
        c, g = divmod(p, 2)
        made = []
        for index in range(3):
            rows = slice(index * dim + p * LANES, index * dim + (p + 1) * LANES)
            bias = slice(2 * dim + rows.start, 2 * dim + rows.stop)
            made.append((dot(wqkv_t[rows, :], first) + wide(vec[bias, :], SEQ)).astype(BF))
        query, keys, values = made[0] * scale, made[1], made[2]
        query_o[s, c, g], keys_o[s, c, g], values_o[s, c, g] = query, keys, values
        near_q, far_q = pair_near_far(query)
        kp = turned(keys)
        return dot(kp[:HALF], near_q), dot(kp, far_q), values

    def mix(s, p, near_s, far_s, values):
        c, g = divmod(p, 2)
        near, near_g, near_n = attend(near_s, mask)
        far, far_g, far_n = attend(far_s, mask)
        norms = [
            jnp.concatenate([near_n[:, lanes], far_n[:, lanes]], axis=1)
            for lanes in (slice(0, HALF), slice(HALF, SEQ))
        ]
        signed_o[s, c, g, :HALF], signed_o[s, c, g, HALF:] = near, far
        slope_o[s, c, g, :HALF], slope_o[s, c, g, HALF:] = near_g, far_g
        near_m, far_m = dot(values[:, :HALF], near), dot(values, far)
        made = jnp.concatenate(
            [
                jnp.concatenate([near_m[:HEAD_DIM, :HALF], far_m[:HEAD_DIM, :HALF]], axis=1) * norms[0],
                jnp.concatenate([near_m[HEAD_DIM:, HALF:], far_m[HEAD_DIM:, HALF:]], axis=1) * norms[1],
            ],
            axis=0,
        ).astype(BF)
        mixed_o[s, c, g] = made
        for e in range(2):
            norm_o[s, c, g, e : e + 1, :] = norms[e]
        return made

    def finish(s, mixed):
        x = tok[s * SEQ : (s + 1) * SEQ, :].astype(F32).T
        hidden_o[s] = x + dot(wo_t[...], jnp.concatenate(mixed, axis=0)) + wide(vec[5 * dim : 6 * dim, :], SEQ)

    first = prepare(0)
    ready = project(0, 0, first)
    mixed = []
    for s in range(seqs):
        done, mixed = mixed, []
        for p in range(pairs):
            current = ready
            if p == pairs // 2 and s + 1 < seqs:
                following = prepare(s + 1)
            if p + 1 < pairs:
                ready = project(s, p + 1, first)
            elif s + 1 < seqs:
                first = following
                ready = project(s + 1, 0, first)
            mixed.append(mix(s, p, *current))
            if p == 0 and s > 0:
                finish(s - 1, done)
    finish(seqs - 1, mixed)


def mlp_kernel(seqs, block, place, *refs):
    (hid, cot, wu0, wu1, wd0, wd1, gain2, shift2, small0, small1) = refs[:10]
    (act_o, low_o, own_o, other_o, gvec_o) = refs[10:15]
    wu_t, gup, gdown, gvec, vec, bup = refs[15:21]
    dim = hid.shape[1]
    units = wu0.shape[1]
    lanes = seqs * SEQ
    step = pl.program_id(0)

    @pl.when(step == 0)
    def _():
        for index, (up, small) in enumerate(((wu0, small0), (wu1, small1))):
            rows = slice(index * units, (index + 1) * units)
            wu_t[rows, :] = turned(up[...])
            bup[rows, :] = as_column(small[:, small.shape[1] - units :])
        for index, ref in enumerate((gain2, shift2)):
            vec[index * dim : (index + 1) * dim, :] = as_column(ref[...])
        gup[...] = jnp.zeros_like(gup)
        gdown[...] = jnp.zeros_like(gdown)
        gvec[...] = jnp.zeros_like(gvec)

    hidden = jnp.concatenate([hid[s] for s in range(seqs)], axis=1)
    grad_out = cot[...].astype(F32).T
    grad_low = grad_out.astype(BF)
    gain = wide(vec[0:dim, :], lanes)
    plain, factor = norm_plain(hidden)
    second = (plain * gain + wide(vec[dim : 2 * dim, :], lanes)).astype(BF)
    ones = jnp.ones((16, lanes), BF)
    second_ones = jnp.concatenate([second, ones], axis=0)
    dnorm = None
    for start in range(0, 2 * units, block):
        span = slice(start, start + block)
        half, inner = divmod(start, units)
        up_ref, down_ref = ((wu0, wd0), (wu1, wd1))[half]
        inner = slice(inner, inner + block)
        upper = dot(wu_t[span, :], second) + wide(bup[span, :], lanes)
        dact = dot(down_ref[inner, :], grad_low)
        part = upper * (1.0 / math.sqrt(2.0))
        cdf = 0.5 * lax.erf(part) + 0.5
        density = jnp.exp2((part * part) * (-1.0 / math.log(2.0)))
        act = (upper * cdf).astype(BF)
        dup = (dact * (cdf + part * density * (1.0 / math.sqrt(math.pi)))).astype(BF)
        for s in range(seqs):
            act_o[s, span, :] = act[:, s * SEQ : (s + 1) * SEQ]
        dn_part = dot(up_ref[:, inner], dup)
        dnorm = dn_part if dnorm is None else dnorm + dn_part
        gup[:, span] += tail_dot(second_ones, dup)
        if start == 0:
            act = jnp.concatenate([ones, act], axis=0)
            gdown[: 16 + block, :] += tail_dot(act, grad_low)
        else:
            gdown[16 + start : 16 + start + block, :] += tail_dot(act, grad_low)
    gvec[0:dim, :] += lane_fold(dnorm * plain)
    gvec[dim : 2 * dim, :] += lane_fold(dnorm)
    dhidden = grad_out + norm_back(dnorm, plain, factor, gain)
    gvec[2 * dim :, :] += lane_fold(dhidden)
    for s in range(seqs):
        low_o[s] = dhidden[:, s * SEQ : (s + 1) * SEQ].astype(BF)

    @pl.when(step == pl.num_programs(0) - 1)
    def _():
        for half, grad_o in enumerate((own_o, other_o)):
            for index in range(units // dim):
                start = half * units + index * dim
                grad_o[index * dim : (index + 1) * dim, :] = gup[:dim, start : start + dim].astype(BF)
            grad_o[units:, :] = gdown[16 + half * units : 16 + (half + 1) * units, :].astype(BF)
        for index, row in ((0, 0), (1, 1), (2, 3)):
            gvec_o[row : row + 1, :] = as_row(gvec[index * dim : (index + 1) * dim, :])
        gvec_o[2:3, :] = gdown[:1, :]
        for index in range(2 * units // dim):
            gvec_o[4 + index : 5 + index, :] = gup[dim : dim + 1, index * dim : (index + 1) * dim]


def out_kernel(seqs, place, hid, act, wd0, wd1, bdown, out_o, whole_o, wd_t, vec):
    units = wd0.shape[0]

    @pl.when(pl.program_id(0) == 0)
    def _():
        wd_t[:, :units] = turned(wd0[...])
        wd_t[:, units:] = turned(wd1[...])
        vec[...] = as_column(bdown[...])

    for s in range(seqs):
        rows = slice(s * SEQ, (s + 1) * SEQ)
        out = hid[s] + dot(wd_t[...], act[s]) + wide(vec[...], SEQ)
        made = out.T.astype(BF)
        out_o[rows, :] = made
        whole_o[rows, :] = made


def ff_unpack_kernel(total, up_o, down_o):
    dim, units = up_o.shape
    for start in range(0, units, dim):
        up_o[:, start : start + dim] = total[start : start + dim, :].astype(F32)
    down_o[...] = total[units:, :].astype(F32)


def at_unpack_kernel(here, b0, b1, b2, b3, *refs):
    outs, hold = refs[:-1], refs[-1]
    size = b0.shape[0]
    for m, block in enumerate((b0, b1, b2, b3)):
        hold[here[m]] = block[...]
    rows = lambda start, count: [
        hold[k, max(start - k * size, 0) : min(start + count - k * size, size), :].astype(F32)
        for k in range(4)
        if start < (k + 1) * size and start + count > k * size
    ]
    get = lambda start, count: jnp.concatenate(rows(start, count), axis=0)
    dim = outs[0].shape[0]
    for g in range(2):
        base = g * 4 * dim
        for index in range(3):
            outs[index][:, g * LANES : (g + 1) * LANES] = get(base + index * dim, dim)
        for index in range(dim // LANES):
            outs[3][g * LANES : (g + 1) * LANES, index * LANES : (index + 1) * LANES] = get(
                base + 3 * dim + index * LANES, LANES
            )
    at = 8 * dim
    for out in outs[4:]:
        for start in range(0, out.shape[1], LANES):
            out[:, start : start + LANES] = get(at // 16 * 16, 16)[at % 16 : at % 16 + 1]
            at += 1


def grad_kernel(seqs, *refs):
    (low_i, first_i, query_i, keys_i, values_i, mixed_i, signed_i, slope_i, norm_i) = refs[:9]
    wo0, wo1 = refs[9:11]
    outs = refs[11:17]
    own_o, other_o, gvec_o = refs[17:20]
    gqkv, gout, gb = refs[20:23]
    dim = low_i.shape[1]
    part = 2 * LANES
    step = pl.program_id(0)
    scale = 1.0 / math.sqrt(HEAD_DIM)

    @pl.when(step == 0)
    def _():
        gqkv[...] = jnp.zeros_like(gqkv)
        gout[...] = jnp.zeros_like(gout)
        gb[...] = jnp.zeros_like(gb)

    first = jnp.concatenate([first_i[s] for s in range(seqs)], axis=1)
    low = jnp.concatenate([low_i[s] for s in range(seqs)], axis=1)

    def pair(s, c, g, dm):
        q, k = query_i[s, c, g], keys_i[s, c, g]
        v_nat = turned(values_i[s, c, g])
        near_q, far_q = pair_near_far(q)
        near_m, far_m = pair_near_far(dm)
        low_pair = []
        for index in range(2):
            keys = slice(0, HALF) if index == 0 else slice(0, SEQ)
            block = slice(0, HALF) if index == 0 else slice(HALF, HALF + SEQ)
            lanes = slice(index * HALF, (index + 1) * HALF)
            dsigned = dot(v_nat[keys], (near_m, far_m)[index])
            signed = signed_i[s, c, g, block].astype(F32)
            row_dot = jnp.sum(signed * dsigned, axis=0, keepdims=True)
            row_dot = row_dot * jnp.concatenate(
                [norm_i[s, c, g, e : e + 1, lanes] for e in range(2)], axis=1
            )
            dscores = slope_i[s, c, g, block].astype(F32) * dsigned - signed * row_dot
            low_pair.append(dscores.astype(BF))
        near, far = low_pair
        near_p, far_p = dot(k[:, :HALF], near), dot(k, far)
        dq = jnp.concatenate(
            [
                jnp.concatenate([near_p[:HEAD_DIM, :HALF], far_p[:HEAD_DIM, :HALF]], axis=1),
                jnp.concatenate([near_p[HEAD_DIM:, HALF:], far_p[HEAD_DIM:, HALF:]], axis=1),
            ],
            axis=0,
        )
        near_p, far_p = tail_dot(near, near_q), tail_dot(far, far_q)
        dk = jnp.concatenate([far_p[:HALF] + near_p, far_p[HALF:]], axis=0)
        near_p = tail_dot(signed_i[s, c, g, :HALF], near_m)
        far_p = tail_dot(signed_i[s, c, g, HALF:], far_m)
        dv = jnp.concatenate([far_p[:HALF] + near_p, far_p[HALF:]], axis=0)
        return dq, dk, dv

    for g in range(2):
        place = slice(g * LANES, (g + 1) * LANES)
        spread = lambda s, c, e: jnp.broadcast_to(norm_i[s, c, g, e : e + 1, :], (HEAD_DIM, SEQ))
        norms = jnp.concatenate(
            [
                jnp.concatenate([spread(s, c, e) for c in range(2) for e in range(2)], axis=0)
                for s in range(seqs)
            ],
            axis=1,
        )
        dmixed = jnp.concatenate([dot(wo0[place, :], low), dot(wo1[place, :], low)], axis=0)
        dmixed = (dmixed * norms).astype(BF)
        mixed = jnp.concatenate(
            [
                jnp.concatenate([mixed_i[s, 0, g], mixed_i[s, 1, g]], axis=0)
                for s in range(seqs)
            ],
            axis=1,
        )
        dq_o, dk_o, dv_o = outs[3 * g : 3 * g + 3]
        dq_all, dk_all, dv_all = [], [], []
        for s in range(seqs):
            span = slice(s * SEQ, (s + 1) * SEQ)
            dq, dk, dv = zip(
                *[pair(s, c, g, dmixed[c * LANES : (c + 1) * LANES, span]) for c in range(2)]
            )
            dq_all.append((jnp.concatenate(dq, axis=0) * scale).astype(BF))
            dk_all.append(jnp.concatenate(dk, axis=1).astype(BF))
            dv_all.append(jnp.concatenate(dv, axis=1).astype(BF))
            dq_o[s], dk_o[s], dv_o[s] = dq_all[s], dk_all[s], dv_all[s]
        gout[g * part : (g + 1) * part, :] += tail_dot(mixed, low)
        dq = jnp.concatenate(dq_all, axis=1)
        dk, dv = jnp.concatenate(dk_all, axis=0), jnp.concatenate(dv_all, axis=0)
        at = 3 * g * part
        gqkv[:, at : at + part] += tail_dot(first, dq)
        gqkv[:, at + part : at + 2 * part] += dot(first, dk)
        gqkv[:, at + 2 * part : at + 3 * part] += dot(first, dv)
        base = g * 4 * LANES
        gb[base : base + part, :] += lane_fold(dq.astype(F32))
        for index, block in ((2, dk), (3, dv)):
            total = jnp.sum(block.astype(F32).reshape(-1, 8, part), axis=0)
            rows = base + index * LANES
            gb[rows : rows + 8, :] += total[:, :LANES]
            gb[rows + 8 : rows + 16, :] += total[:, LANES:]

    @pl.when(step == pl.num_programs(0) - 1)
    def _():
        for g in range(2):
            base = g * 4 * LANES
            tall = g * 4 * dim
            for c, grad_o in enumerate((own_o, other_o)):
                for index in range(3):
                    start = 3 * g * part + index * part + c * LANES
                    grad_o[tall + index * dim : tall + (index + 1) * dim, :] = gqkv[
                        :, start : start + LANES
                    ].astype(BF)
                for index in range(dim // LANES):
                    start = tall + 3 * dim + index * LANES
                    grad_o[start : start + LANES, :] = gout[
                        g * part + c * LANES : g * part + (c + 1) * LANES,
                        index * LANES : (index + 1) * LANES,
                    ].astype(BF)
                gvec_o[8 * g + c : 8 * g + c + 1, :] = as_row(
                    gb[base + c * LANES : base + (c + 1) * LANES, :]
                )
                for index in (2, 3):
                    rows = slice(base + index * LANES + 8 * c, base + index * LANES + 8 * c + 8)
                    at = 8 * g + 2 * index - 2 + c
                    gvec_o[at : at + 1, :] = jnp.sum(gb[rows, :], axis=0, keepdims=True)


def input_kernel(seqs, place, *refs):
    tok, dhid, dq0, dk0, dv0, dq1, dk1, dv1 = refs[:8]
    wq0, wq1, wk0, wk1, wv0, wv1, gain1 = refs[8:15]
    vec_ff, vec_at = refs[15:17]
    tgrad_o, whole_o, gvec_o, own_o, other_o = refs[17:22]
    gvec, vec, pack = refs[22:25]
    dim = tok.shape[1]

    @pl.when(pl.program_id(0) == 0)
    def _():
        gvec[...] = jnp.zeros_like(gvec)
        vec[...] = as_column(gain1[...])

    gain = wide(vec[...], SEQ)
    for s in range(seqs):
        rows = slice(s * SEQ, (s + 1) * SEQ)
        dnorm = None
        for c, (wq, wk, wv) in enumerate(((wq0, wk0, wv0), (wq1, wk1, wv1))):
            lanes = slice(c * LANES, (c + 1) * LANES)
            dq = jnp.concatenate([dq0[s, lanes, :], dq1[s, lanes, :]], axis=0)
            dk = jnp.concatenate([dk0[s, :, lanes], dk1[s, :, lanes]], axis=1)
            dv = jnp.concatenate([dv0[s, :, lanes], dv1[s, :, lanes]], axis=1)
            made = dot(wq[...], dq) + tail_dot(wk[...], dk) + tail_dot(wv[...], dv)
            dnorm = made if dnorm is None else dnorm + made
        plain, factor = norm_plain(tok[rows, :].astype(F32).T)
        gvec[0:dim, :] += lane_fold(dnorm * plain)
        gvec[dim : 2 * dim, :] += lane_fold(dnorm)
        tgrad = dhid[s].astype(F32) + norm_back(dnorm, plain, factor, gain)
        made = tgrad.T.astype(BF)
        tgrad_o[rows, :] = made
        whole_o[rows, :] = made

    @pl.when(pl.program_id(0) == pl.num_programs(0) - 1)
    def _():
        for index in range(2):
            gvec_o[index : index + 1, :] = as_row(gvec[index * dim : (index + 1) * dim, :])
        same = [(vec_ff, r) for r in range(4)] + [(gvec_o, 0), (gvec_o, 1)]
        units = 2 * dim
        pack[...] = jnp.zeros_like(pack)
        for c, out in enumerate((own_o, other_o)):
            rows = [ref[r : r + 1, k : k + LANES] for ref, r in same for k in range(0, dim, LANES)]
            rows += [vec_at[r : r + 1, :] for i in range(3) for r in (2 * i + c, 8 + 2 * i + c)]
            rows += [
                vec_ff[4 + r : 5 + r, k : k + LANES]
                for r in range(c * units // dim, (c + 1) * units // dim)
                for k in range(0, dim, LANES)
            ]
            for index, row in enumerate(rows):
                pack[index : index + 1, :] = row
            out[...] = pack[...].astype(BF)


def whole_vmem():
    return pl.BlockSpec(memory_space=pltpu.VMEM)


def seq_block(seqs, *dims):
    return pl.BlockSpec((seqs,) + dims, lambda i: (i,) + (0,) * len(dims))


def params():
    return pltpu.CompilerParams(
        dimension_semantics=("arbitrary",), vmem_limit_bytes=VMEM_LIMIT
    )


def prefetch(grid, in_specs, out_specs, scratch=()):
    return pltpu.PrefetchScalarGridSpec(
        num_scalar_prefetch=1, grid=grid, in_specs=in_specs, out_specs=out_specs, scratch_shapes=scratch
    )


def row_block(seqs, dim, steps):
    return pl.BlockSpec((seqs * SEQ, dim), lambda i, place: (place[0] * steps + i, 0))


def placed_seq_block(seqs, *dims):
    return pl.BlockSpec((seqs,) + dims, lambda i, place: (i,) + (0,) * len(dims))


def attn_call(place, tokens, own, weights, vectors, seqs):
    dim = tokens.shape[1]
    count = own // SEQ
    steps = count // seqs
    feat = (2, 2, LANES, SEQ)
    wide_block = (2, 2, HALF + SEQ, SEQ)
    shape = jax.ShapeDtypeStruct
    return pl.pallas_call(
        functools.partial(attn_kernel, seqs),
        grid_spec=prefetch(
            (steps,),
            [row_block(seqs, dim, steps)] + [whole_vmem()] * 13,
            [placed_seq_block(seqs, *feat)] * 4
            + [placed_seq_block(seqs, *wide_block)] * 2
            + [placed_seq_block(seqs, 2, 2, 8, SEQ)]
            + [placed_seq_block(seqs, dim, SEQ)] * 2,
            [
                pltpu.VMEM((3 * dim, dim), BF),
                pltpu.VMEM((dim, dim), BF),
                pltpu.VMEM((6 * dim, LANES), F32),
            ],
        ),
        out_shape=[shape((count,) + feat, BF)] * 4
        + [shape((count,) + wide_block, BF)] * 2
        + [shape((count, 2, 2, 8, SEQ), F32)]
        + [shape((count, dim, SEQ), BF), shape((count, dim, SEQ), F32)],
        compiler_params=params(),
        cost_estimate=pl.CostEstimate(flops=1, bytes_accessed=1, transcendentals=0),
        name="attn_forward",
    )(place, tokens, *weights, *vectors)


def grad_call(low, first, saved, weights, seqs):
    count, dim = low.shape[:2]
    steps = count // seqs
    every = lambda *dims: seq_block(seqs, 2, 2, *dims)
    shape = jax.ShapeDtypeStruct
    part = 2 * LANES
    trio = [seq_block(seqs, part, SEQ), seq_block(seqs, SEQ, part), seq_block(seqs, SEQ, part)]
    return pl.pallas_call(
        functools.partial(grad_kernel, seqs),
        grid=(steps,),
        in_specs=[seq_block(seqs, dim, SEQ)] * 2
        + [every(LANES, SEQ)] * 4
        + [every(HALF + SEQ, SEQ)] * 2
        + [every(8, SEQ)]
        + [whole_vmem()] * 2,
        out_specs=trio * 2 + [whole_vmem()] * 3,
        out_shape=[
            shape((count, part, SEQ), BF),
            shape((count, SEQ, part), BF),
            shape((count, SEQ, part), BF),
        ]
        * 2
        + [
            shape((8 * dim, LANES), BF),
            shape((8 * dim, LANES), BF),
            shape((16, LANES), F32),
        ],
        scratch_shapes=[
            pltpu.VMEM((dim, 6 * part), F32),
            pltpu.VMEM((2 * part, dim), F32),
            pltpu.VMEM((8 * LANES, LANES), F32),
        ],
        compiler_params=params(),
        cost_estimate=pl.CostEstimate(flops=1, bytes_accessed=1, transcendentals=0),
        name="attn_backward",
    )(low, first, *saved, *weights)


def input_call(place, tokens, dhidden, pieces, weights, gain1, vectors, grow, seqs):
    dim = tokens.shape[1]
    count = dhidden.shape[0]
    steps = count // seqs
    part = 2 * LANES
    trio = [
        placed_seq_block(seqs, part, SEQ),
        placed_seq_block(seqs, SEQ, part),
        placed_seq_block(seqs, SEQ, part),
    ]
    return pl.pallas_call(
        functools.partial(input_kernel, seqs),
        grid_spec=prefetch(
            (steps,),
            [row_block(seqs, dim, steps), placed_seq_block(seqs, dim, SEQ)]
            + trio * 2
            + [whole_vmem()] * 9,
            [
                pl.BlockSpec((seqs * SEQ, dim), lambda i, place: (i, 0)),
                row_block(seqs, dim, steps),
            ]
            + [whole_vmem()] * 3,
            [
                pltpu.VMEM((2 * dim, LANES), F32),
                pltpu.VMEM((dim, LANES), F32),
                pltpu.VMEM((grow, LANES), F32),
            ],
        ),
        out_shape=[
            jax.ShapeDtypeStruct((count * SEQ, dim), BF),
            jax.ShapeDtypeStruct(tokens.shape, BF),
            jax.ShapeDtypeStruct((8, dim), F32),
            jax.ShapeDtypeStruct((grow, LANES), BF),
            jax.ShapeDtypeStruct((grow, LANES), BF),
        ],
        compiler_params=params(),
        cost_estimate=pl.CostEstimate(flops=1, bytes_accessed=1, transcendentals=0),
        name="input_grad",
    )(place, tokens, dhidden, *pieces, *weights, gain1, *vectors)


def mlp_call(place, hidden, cotangent, weights, vectors, seqs, block):
    count, dim = hidden.shape[:2]
    steps = count // seqs
    units = weights[0].shape[1]
    shape = jax.ShapeDtypeStruct
    return pl.pallas_call(
        functools.partial(mlp_kernel, seqs, block),
        grid_spec=prefetch(
            (steps,),
            [placed_seq_block(seqs, dim, SEQ), row_block(seqs, dim, steps)] + [whole_vmem()] * 8,
            [placed_seq_block(seqs, 2 * units, SEQ), placed_seq_block(seqs, dim, SEQ)]
            + [whole_vmem()] * 3,
            [
                pltpu.VMEM((2 * units, dim), BF),
                pltpu.VMEM((dim + 16, 2 * units), F32),
                pltpu.VMEM((2 * units + 16, dim), F32),
                pltpu.VMEM((3 * dim, LANES), F32),
                pltpu.VMEM((2 * dim, LANES), F32),
                pltpu.VMEM((2 * units, LANES), F32),
            ],
        ),
        out_shape=[
            shape((count, 2 * units, SEQ), BF),
            shape((count, dim, SEQ), BF),
            shape((2 * units, dim), BF),
            shape((2 * units, dim), BF),
            shape((8, dim), F32),
        ],
        compiler_params=params(),
        cost_estimate=pl.CostEstimate(flops=1, bytes_accessed=1, transcendentals=0),
        name="feed_forward",
    )(place, hidden, cotangent, *weights, *vectors)


def out_call(place, hidden, act, weights, bdown, rows, seqs):
    count, dim = hidden.shape[:2]
    units = act.shape[1]
    steps = count // seqs
    return pl.pallas_call(
        functools.partial(out_kernel, seqs),
        grid_spec=prefetch(
            (steps,),
            [placed_seq_block(seqs, dim, SEQ), placed_seq_block(seqs, units, SEQ)] + [whole_vmem()] * 3,
            [
                pl.BlockSpec((seqs * SEQ, dim), lambda i, place: (i, 0)),
                row_block(seqs, dim, steps),
            ],
            [pltpu.VMEM((dim, units), BF), pltpu.VMEM((dim, LANES), F32)],
        ),
        out_shape=[
            jax.ShapeDtypeStruct((count * SEQ, dim), BF),
            jax.ShapeDtypeStruct((rows, dim), BF),
        ],
        compiler_params=params(),
        cost_estimate=pl.CostEstimate(flops=1, bytes_accessed=1, transcendentals=0),
        name="layer_out",
    )(place, hidden, act, *weights, bdown)


def ff_unpack_call(total, units):
    dim = total.shape[1]
    return pl.pallas_call(
        ff_unpack_kernel,
        in_specs=[whole_vmem()],
        out_specs=[whole_vmem()] * 2,
        out_shape=[
            jax.ShapeDtypeStruct((dim, units), F32),
            jax.ShapeDtypeStruct((units, dim), F32),
        ],
        compiler_params=pltpu.CompilerParams(vmem_limit_bytes=VMEM_LIMIT),
        name="ff_unpack",
    )(total)


def at_unpack_call(here, blocks, dim, local, sizes):
    shape = jax.ShapeDtypeStruct
    outs = [shape((dim, local), F32)] * 3 + [shape((local, dim), F32)]
    outs += [shape((1, n), F32) for n in sizes]
    return pl.pallas_call(
        at_unpack_kernel,
        in_specs=[pl.BlockSpec(memory_space=pltpu.SMEM)] + [whole_vmem()] * 4,
        out_specs=[whole_vmem()] * len(outs),
        out_shape=outs,
        scratch_shapes=[pltpu.VMEM((4,) + blocks[0].shape, BF)],
        compiler_params=pltpu.CompilerParams(vmem_limit_bytes=VMEM_LIMIT),
        name="at_unpack",
    )(here, *blocks)


def shifted(value, axis, count, shift):
    return lax.ppermute(value, axis, [(i, (i + shift) % count) for i in range(count)])


def gathered(value, count, axis):
    blocks = [value] + [shifted(value, "mp", count, -r) for r in range(1, count)]
    half = count // 2
    return [
        blocks[g * half] if half == 1 else jnp.concatenate(blocks[g * half : (g + 1) * half], axis)
        for g in range(2)
    ]


def total_of(blocks):
    total = blocks[0].astype(F32)
    for block in blocks[1:]:
        total = total + block.astype(F32)
    return total.astype(BF)


class DpSum:
    def __init__(self, count):
        self.count = count
        self.groups = []
        bit = 1
        while bit < count:
            size = min(4, count // bit)
            self.groups.append((bit, size))
            bit *= size

    def swap(self, value, distance):
        return lax.ppermute(value, "dp", [(i, i ^ distance) for i in range(self.count)])

    def place(self, bit, size):
        return (lax.axis_index("dp") // bit) % size

    def scatter(self, value, stage):
        bit, size = self.groups[stage]
        here = self.place(bit, size)
        parts = value.reshape(size, value.shape[0] // size, value.shape[1])
        pick = lambda m: lax.dynamic_index_in_dim(parts, here ^ m, 0, keepdims=False)
        return [pick(0)] + [self.swap(pick(m), m * bit) for m in range(1, size)]

    def gather(self, value, stage):
        bit, size = self.groups[stage]
        return [value] + [self.swap(value, m * bit) for m in range(1, size)]

    def join(self, blocks, stage):
        bit, size = self.groups[stage]
        here = self.place(bit, size)
        whole = jnp.zeros((size,) + blocks[0].shape, blocks[0].dtype)
        for m, block in enumerate(blocks):
            whole = lax.dynamic_update_index_in_dim(whole, block, here ^ m, 0)
        return whole.reshape(-1, blocks[0].shape[1])


def body(mp, dp, *args):
    (tokens, gain1, shift1, wq, bq, wk, bk, wv, bv, wo, bo) = args[:11]
    (gain2, shift2, wu, bu, wd, bd, cotangent) = args[11:]
    rows, dim = tokens.shape
    local = wq.shape[1]
    units = wu.shape[1]
    own = rows // mp
    per = mp // 2
    me = lax.axis_index("mp")
    place = me.astype(jnp.int32).reshape(1)
    tie = lax.optimization_barrier
    dp_sum = DpSum(dp)

    weights = []
    for w in (wq, wk, wv):
        weights += gathered(w, mp, 1)
    weights += gathered(wo, mp, 0)
    small = jnp.concatenate([bq, bk, bv, bu]).reshape(1, -1)
    smalls = [small] + [shifted(small, "mp", mp, -r) for r in range(1, mp)]
    if per > 1:
        cuts = [0, local, 2 * local, 3 * local, 3 * local + units]
        smalls = [
            jnp.concatenate(
                [
                    block[:, lo:hi]
                    for lo, hi in zip(cuts, cuts[1:])
                    for block in smalls[c * per : (c + 1) * per]
                ],
                axis=1,
            )
            for c in range(2)
        ]
    mlp_weights = gathered(wu, mp, 1) + gathered(wd, mp, 0)
    gain1, shift1, bo, gain2, shift2, bd = (
        v.reshape(1, -1) for v in (gain1, shift1, bo, gain2, shift2, bd)
    )

    def filled(full, others):
        for r, block in enumerate(others, 1):
            full = lax.dynamic_update_slice_in_dim(full, block, ((me - r) % mp) * own, 0)
        return full

    def spread_out(part):
        return [shifted(part, "mp", mp, r) for r in range(1, mp)]

    def ff_piece(grad, r):
        g, j = divmod(r, per)
        if per == 1:
            return grad[g]
        up = grad[g][: per * units].reshape(-1, dim, dim)
        up = jnp.concatenate(list(up), axis=1)[:, j * units : (j + 1) * units]
        down = grad[g][per * units + j * units : per * units + (j + 1) * units]
        return jnp.concatenate([up.reshape(-1, dim), down], axis=0)

    def at_piece(grads, r):
        g, j = divmod(r, per)
        if per == 1:
            return jnp.concatenate([grad[g] for grad in grads], axis=0)
        parts = []
        for index in range(3):
            block = [grad[g][index * dim : (index + 1) * dim] for grad in grads]
            block = jnp.concatenate(block, axis=1)[:, j * local : (j + 1) * local]
            parts.append(block.reshape(-1, LANES))
        block = [grad[g][3 * dim :].reshape(-1, LANES, LANES) for grad in grads]
        block = jnp.concatenate([jnp.concatenate(list(b), axis=1) for b in block], axis=0)
        parts.append(block[j * local : (j + 1) * local].reshape(-1, LANES))
        return jnp.concatenate(parts, axis=0)

    def mp_send(piece):
        return [piece(0)] + [shifted(piece(r), "mp", mp, r) for r in range(1, mp)]

    *saved, first, hidden = attn_call(
        place, tokens, own, weights, [gain1, shift1, bo] + smalls, SEQS["attn"]
    )
    hidden, mlp_weights = tie((hidden, mlp_weights))
    act, low, *grad_ff, vec_ff = mlp_call(
        place, hidden, cotangent, mlp_weights, [gain2, shift2] + smalls, SEQS["mlp"], 512
    )
    ff = total_of(mp_send(lambda r: ff_piece(grad_ff, r)))
    low, ff = tie((low, ff))
    ff = lax.psum(ff, "dp")
    *pieces, grad_own, grad_other, vec_at = grad_call(low, first, saved, weights[6:], SEQS["grad"])
    grad_at = [grad_own, grad_other]

    def finish(low, act, grad_at):
        at = mp_send(lambda r: grad_at[r]) if per == 1 else []
        low, at = tie((low, at))
        grow = -(-(6 * dim + 3 * local + units) // (16 * dp * LANES)) * 16 * dp
        tgrad, tgrad_full, vec_in, *vec_low = input_call(
            place,
            tokens,
            low,
            pieces,
            weights[:6],
            gain1,
            [vec_ff, vec_at],
            max(grow, -(-(6 * dim + 6 * LANES + 2 * dim) // LANES)),
            SEQS["input"],
        )
        at, tgrad = tie((at, tgrad))

        if per == 1:
            at = jnp.concatenate([total_of(at), total_of(mp_send(lambda r: vec_low[r]))], axis=0)
        else:
            same = jnp.concatenate([vec_ff[:4].reshape(-1), vec_in[:2].reshape(-1)])
            vec_at0, vec_at1 = vec_at[:8], vec_at[8:]
            grads = [[v[: 4 * dim] for v in grad_at], [v[4 * dim :] for v in grad_at]]
            gbup = vec_ff[4:].reshape(-1)
            bias = [
                jnp.concatenate([v[2 * i + c] for c in range(2) for v in (vec_at0, vec_at1)])
                for i in range(3)
            ]

            def all_piece(r):
                vector = jnp.concatenate(
                    [same]
                    + [b[r * local : (r + 1) * local] for b in bias]
                    + [gbup[r * units : (r + 1) * units]]
                )
                size = -(-vector.shape[0] // (16 * dp * LANES)) * (16 * dp * LANES)
                vector = jnp.pad(vector, (0, size - vector.shape[0])).reshape(-1, LANES).astype(BF)
                return jnp.concatenate([at_piece(grads, r), vector], axis=0)

            at = total_of(mp_send(all_piece))
        at = dp_sum.scatter(at, 0)
        tgrads = spread_out(tgrad)
        act, at[0], tgrad = tie((act, at[0], tgrad))
        out, out_full = out_call(
            place, hidden, act, mlp_weights[2:], bd, rows, SEQS["out"]
        )
        at, out, tgrads = tie((at, out, tgrads))
        at = total_of(at)
        stages = len(dp_sum.groups)
        for stage in range(1, stages):
            at = total_of(dp_sum.scatter(at, stage))
        outs = spread_out(out)
        tgrad_full = filled(tgrad_full, tgrads)
        at, tgrad_full = tie((at, tgrad_full))
        for stage in reversed(range(1, stages)):
            at = dp_sum.join(dp_sum.gather(at, stage), stage)
        at = dp_sum.gather(at, 0)
        out_full = filled(out_full, outs)
        at, out_full = tie((at, out_full))

        sizes = [dim] * 6 + [local] * 3 + [units]
        if per == 1 and len(at) == 4:
            here = dp_sum.place(*dp_sum.groups[0]).astype(jnp.int32) ^ jnp.arange(4, dtype=jnp.int32)
            *g_at, g0, g1, g2, g3, g4, g5, q0, q1, q2, g_bup = at_unpack_call(
                here, at, dim, local, sizes
            )
            g_qkv, g_out = g_at[:3], g_at[3]
            g_same = [v.reshape(-1) for v in (g0, g1, g2, g3, g4, g5)]
            g_bias = [v.reshape(-1) for v in (q0, q1, q2)]
            g_bup = g_bup.reshape(-1)
        else:
            at = dp_sum.join(at, 0).astype(F32)
            each = dim * local // LANES
            g_qkv = [at[i * each : (i + 1) * each].reshape(dim, local) for i in range(3)]
            g_out = at[3 * each : 4 * each].reshape(local, dim)
            vector = at[4 * each :].reshape(-1)
            parts = []
            for size in sizes:
                parts.append(vector[:size])
                vector = vector[size:]
            g_same, g_bias, g_bup = parts[:6], parts[6:9], parts[9]
        return (out_full, tgrad_full, list(g_same), list(g_qkv), list(g_bias), g_out, g_bup)

    blank = jax.eval_shape(finish, low, act, grad_at)
    out_full, tgrad_full, g_same, g_qkv, g_bias, g_out, g_bup = lax.cond(
        lax.axis_index("dp") != dp,
        finish,
        lambda *_: jax.tree.map(lambda v: jnp.zeros(v.shape, v.dtype), blank),
        low,
        act,
        grad_at,
    )
    if per == 1:
        g_up, g_down = ff_unpack_call(ff, units)
    else:
        ff = ff.astype(F32)
        g_up = ff[:units].reshape(dim, units)
        g_down = ff[units:]
    return (
        out_full,
        tgrad_full,
        g_same[4],
        g_same[5],
        g_qkv[0],
        g_bias[0],
        g_qkv[1],
        g_bias[1],
        g_qkv[2],
        g_bias[2],
        g_out,
        g_same[3],
        g_same[0],
        g_same[1],
        g_up,
        g_bup,
        g_down,
        g_same[2],
    )


def solution(mesh):
    split = P("dp", None)
    columns, some, lines = P(None, "mp"), P("mp"), P("mp", None)
    return jax.shard_map(
        functools.partial(body, mesh.shape["mp"], mesh.shape["dp"]),
        mesh=mesh,
        in_specs=(split, P(), P(), columns, some, columns, some, columns, some, lines, P())
        + (P(), P(), columns, some, lines, P(), split),
        out_specs=(split, split, P(), P(), columns, some, columns, some, columns, some, lines)
        + (P(), P(), P(), columns, some, lines, P()),
        check_vma=False,
    )
```

```python
import functools
import math

import jax
import jax.numpy as jnp
from jax import lax
from jax.experimental import pallas as pl
from jax.experimental.pallas import tpu as pltpu
from jax.sharding import PartitionSpec as P

HEAD_DIM = 64
SEQ = 256
HALF = SEQ // 2
LANES = 128
BF = jnp.bfloat16
F32 = jnp.float32
VMEM_LIMIT = 60 * 1024 * 1024
SEQS = {"attn": 4, "mlp": 2, "grad": 2, "input": 4, "out": 4}


def dot(left, right):
    return jnp.dot(left, right, preferred_element_type=F32)


def tail_dot(left, right):
    return lax.dot_general(left, right, (((1,), (1,)), ((), ())), preferred_element_type=F32)


def turned(block):
    return block.astype(F32).T.astype(BF)


def wide(column, lanes):
    return jnp.concatenate([column] * (lanes // LANES), axis=1)


def lane_fold(rows):
    total = rows[:, :LANES]
    for start in range(LANES, rows.shape[1], LANES):
        total = total + rows[:, start : start + LANES]
    return total


def as_column(row):
    return jnp.broadcast_to(row, (LANES, row.shape[1])).T


def as_row(sums):
    return jnp.sum(sums.T, axis=0, keepdims=True)


def norm_plain(x):
    center = x - jnp.mean(x, axis=0, keepdims=True)
    factor = lax.rsqrt(jnp.mean(center * center, axis=0, keepdims=True) + 1e-05)
    return center * factor, factor


def norm_back(grad, plain, factor, gain):
    scaled = grad * gain
    return factor * (
        scaled
        - jnp.mean(scaled, axis=0, keepdims=True)
        - plain * jnp.mean(scaled * plain, axis=0, keepdims=True)
    )


def upper_mask():
    return lax.broadcasted_iota(jnp.int32, (HALF, HALF), 0) <= lax.broadcasted_iota(
        jnp.int32, (HALF, HALF), 1
    )


def smooth(scores):
    square = scores * scores + 1.0
    inverse = lax.rsqrt(square)
    return inverse, square * inverse


def pair_diag(left, right):
    zero = jnp.zeros_like(left)
    return jnp.concatenate(
        [jnp.concatenate([left, zero], axis=1), jnp.concatenate([zero, right], axis=1)], axis=0
    )


def pair_near_far(rows):
    left, right = rows[:HEAD_DIM], rows[HEAD_DIM:]
    return (
        pair_diag(left[:, :HALF], right[:, :HALF]),
        pair_diag(left[:, HALF:], right[:, HALF:]),
    )


def attend(scores, mask):
    inverse, root = smooth(scores)
    if scores.shape[0] > HALF:
        diagonal = jnp.where(mask, root[HALF:], -1e30)
        magnitude = jnp.concatenate([root[:HALF], diagonal], axis=0)
    else:
        magnitude = jnp.where(mask, root, -1e30)
    top = jnp.max(magnitude, axis=0, keepdims=True)
    expo = jnp.exp(magnitude - top)
    norm = 1.0 / jnp.sum(expo, axis=0, keepdims=True)
    low_expo, sign, low = expo.astype(BF), (scores * inverse).astype(BF), inverse.astype(BF)
    return sign * low_expo, (low * low * low + sign * sign) * low_expo, norm


def attn_kernel(seqs, place, *refs):
    (tok, wq0, wq1, wk0, wk1, wv0, wv1, wo0, wo1) = refs[:9]
    gain1, shift1, bout, small0, small1 = refs[9:14]
    (query_o, keys_o, values_o, mixed_o, signed_o, slope_o, norm_o, first_o, hidden_o) = refs[14:23]
    wqkv_t, wo_t, vec = refs[23:26]
    dim = tok.shape[1]
    lanes = seqs * SEQ

    @pl.when(pl.program_id(0) == 0)
    def _():
        part = dim // 2
        for index, ref in enumerate((wq0, wq1, wk0, wk1, wv0, wv1)):
            wqkv_t[index * part : (index + 1) * part, :] = turned(ref[...])
        wo_t[:, :part] = turned(wo0[...])
        wo_t[:, part:] = turned(wo1[...])
        for index, ref in ((0, gain1), (1, shift1), (5, bout)):
            vec[index * dim : (index + 1) * dim, :] = as_column(ref[...])
        for index in range(3):
            for c, ref in enumerate((small0, small1)):
                start = (2 + index) * dim + c * part
                vec[start : start + part, :] = as_column(ref[:, index * part : (index + 1) * part])

    half = lax.broadcasted_iota(jnp.int32, (HALF, SEQ), 1)
    mask = lax.broadcasted_iota(jnp.int32, (HALF, SEQ), 0) <= jnp.where(half < HALF, half, half - HALF)
    pairs = dim // LANES
    scale = jnp.asarray(1.0 / math.sqrt(HEAD_DIM), BF)

    def prepare(s):
        x = tok[s * SEQ : (s + 1) * SEQ, :].astype(F32).T
        plain, _ = norm_plain(x)
        first = (plain * wide(vec[0:dim, :], SEQ) + wide(vec[dim : 2 * dim, :], SEQ)).astype(BF)
        first_o[s] = first
        return first

    def project(s, p, first):
        c, g = divmod(p, 2)
        made = []
        for index in range(3):
            rows = slice(index * dim + p * LANES, index * dim + (p + 1) * LANES)
            bias = slice(2 * dim + rows.start, 2 * dim + rows.stop)
            made.append((dot(wqkv_t[rows, :], first) + wide(vec[bias, :], SEQ)).astype(BF))
        query, keys, values = made[0] * scale, made[1], made[2]
        query_o[s, c, g], keys_o[s, c, g], values_o[s, c, g] = query, keys, values
        near_q, far_q = pair_near_far(query)
        kp = turned(keys)
        return dot(kp[:HALF], near_q), dot(kp, far_q), values

    def mix(s, p, near_s, far_s, values):
        c, g = divmod(p, 2)
        near, near_g, near_n = attend(near_s, mask)
        far, far_g, far_n = attend(far_s, mask)
        norms = [
            jnp.concatenate([near_n[:, lanes], far_n[:, lanes]], axis=1)
            for lanes in (slice(0, HALF), slice(HALF, SEQ))
        ]
        signed_o[s, c, g, :HALF], signed_o[s, c, g, HALF:] = near, far
        slope_o[s, c, g, :HALF], slope_o[s, c, g, HALF:] = near_g, far_g
        near_m, far_m = dot(values[:, :HALF], near), dot(values, far)
        made = jnp.concatenate(
            [
                jnp.concatenate([near_m[:HEAD_DIM, :HALF], far_m[:HEAD_DIM, :HALF]], axis=1) * norms[0],
                jnp.concatenate([near_m[HEAD_DIM:, HALF:], far_m[HEAD_DIM:, HALF:]], axis=1) * norms[1],
            ],
            axis=0,
        ).astype(BF)
        mixed_o[s, c, g] = made
        for e in range(2):
            norm_o[s, c, g, e : e + 1, :] = norms[e]
        return made

    def finish(s, mixed):
        x = tok[s * SEQ : (s + 1) * SEQ, :].astype(F32).T
        made = x + dot(wo_t[...], jnp.concatenate(mixed, axis=0)) + wide(vec[5 * dim : 6 * dim, :], SEQ)
        hidden_o[s] = made.astype(BF)

    first = prepare(0)
    ready = project(0, 0, first)
    mixed = []
    for s in range(seqs):
        done, mixed = mixed, []
        for p in range(pairs):
            current = ready
            if p == pairs // 2 and s + 1 < seqs:
                following = prepare(s + 1)
            if p + 1 < pairs:
                ready = project(s, p + 1, first)
            elif s + 1 < seqs:
                first = following
                ready = project(s + 1, 0, first)
            mixed.append(mix(s, p, *current))
            if p == 0 and s > 0:
                finish(s - 1, done)
    finish(seqs - 1, mixed)


def mlp_kernel(seqs, block, place, *refs):
    (hid, cot, wu0, wu1, wd0, wd1, gain2, shift2, small0, small1) = refs[:10]
    (act_o, dup_o, own_o, other_o, gvec_o) = refs[10:15]
    wu_t, gup, gdown, vec, bup = refs[15:20]
    dim = hid.shape[1]
    units = wu0.shape[1]
    lanes = seqs * SEQ
    step = pl.program_id(0)

    @pl.when(step == 0)
    def _():
        for index, (up, small) in enumerate(((wu0, small0), (wu1, small1))):
            rows = slice(index * units, (index + 1) * units)
            wu_t[rows, :] = turned(up[...])
            bup[rows, :] = as_column(small[:, small.shape[1] - units :])
        for index, ref in enumerate((gain2, shift2)):
            vec[index * dim : (index + 1) * dim, :] = as_column(ref[...])
        gup[...] = jnp.zeros_like(gup)
        gdown[...] = jnp.zeros_like(gdown)

    hidden = jnp.concatenate([hid[s] for s in range(seqs)], axis=1).astype(F32)
    grad_low = cot[...].astype(F32).T.astype(BF)
    plain, _ = norm_plain(hidden)
    second = plain * wide(vec[0:dim, :], lanes) + wide(vec[dim : 2 * dim, :], lanes)
    second = second.astype(BF)
    ones = jnp.ones((16, lanes), BF)
    second_ones = jnp.concatenate([second, ones], axis=0)
    for start in range(0, 2 * units, block):
        span = slice(start, start + block)
        half, inner = divmod(start, units)
        upper = dot(wu_t[span, :], second) + wide(bup[span, :], lanes)
        dact = dot((wd0, wd1)[half][inner : inner + block, :], grad_low)
        part = upper * (1.0 / math.sqrt(2.0))
        cdf = 0.5 * lax.erf(part) + 0.5
        density = jnp.exp2((part * part) * (-1.0 / math.log(2.0)))
        act = (upper * cdf).astype(BF)
        dup = (dact * (cdf + part * density * (1.0 / math.sqrt(math.pi)))).astype(BF)
        for s in range(seqs):
            act_o[s, span, :] = act[:, s * SEQ : (s + 1) * SEQ]
            dup_o[s, span, :] = dup[:, s * SEQ : (s + 1) * SEQ]
        gup[:, span] += tail_dot(second_ones, dup)
        if start == 0:
            act = jnp.concatenate([ones, act], axis=0)
            gdown[: 16 + block, :] += tail_dot(act, grad_low)
        else:
            gdown[16 + start : 16 + start + block, :] += tail_dot(act, grad_low)

    @pl.when(step == pl.num_programs(0) - 1)
    def _():
        for half, grad_o in enumerate((own_o, other_o)):
            for index in range(units // dim):
                start = half * units + index * dim
                grad_o[index * dim : (index + 1) * dim, :] = gup[:dim, start : start + dim].astype(BF)
            grad_o[units:, :] = gdown[16 + half * units : 16 + (half + 1) * units, :].astype(BF)
        gvec_o[0:1, :] = gdown[:1, :]
        for index in range(2 * units // dim):
            gvec_o[4 + index : 5 + index, :] = gup[dim : dim + 1, index * dim : (index + 1) * dim]


def out_kernel(seqs, place, hid, act, wd0, wd1, bdown, out_o, whole_o, wd_t, vec):
    units = wd0.shape[0]

    @pl.when(pl.program_id(0) == 0)
    def _():
        wd_t[:, :units] = turned(wd0[...])
        wd_t[:, units:] = turned(wd1[...])
        vec[...] = as_column(bdown[...])

    for s in range(seqs):
        rows = slice(s * SEQ, (s + 1) * SEQ)
        out = hid[s].astype(F32) + dot(wd_t[...], act[s]) + wide(vec[...], SEQ)
        made = out.T.astype(BF)
        out_o[rows, :] = made
        whole_o[rows, :] = made


def ff_unpack_kernel(total, up_o, down_o):
    dim, units = up_o.shape
    for start in range(0, units, dim):
        up_o[:, start : start + dim] = total[start : start + dim, :].astype(F32)
    down_o[...] = total[units:, :].astype(F32)


def at_unpack_kernel(here, b0, b1, b2, b3, v0, v1, v2, v3, *refs):
    outs, hold = refs[:-1], refs[-1]
    size = b0.shape[0]
    for m, block in enumerate((b0, b1, b2, b3)):
        hold[here[m]] = block[...]

    def get(start, count):
        parts = []
        while count > 0:
            k, inner = divmod(start, size)
            taken = min(count, size - inner)
            parts.append(hold[k, inner : inner + taken, :].astype(F32))
            start, count = start + taken, count - taken
        return parts[0] if len(parts) == 1 else jnp.concatenate(parts, axis=0)

    dim = outs[0].shape[0]
    for g in range(2):
        base = g * 4 * dim
        for index in range(3):
            outs[index][:, g * LANES : (g + 1) * LANES] = get(base + index * dim, dim)
        for index in range(dim // LANES):
            outs[3][g * LANES : (g + 1) * LANES, index * LANES : (index + 1) * LANES] = get(
                base + 3 * dim + index * LANES, LANES
            )
    used = sum(out.shape[1] for out in outs[4:]) // LANES
    used = -(-used // 16) * 16
    vector = sum(v[:used, :].astype(F32) for v in (v0, v1, v2, v3))
    at = 0
    for out in outs[4:]:
        for start in range(0, out.shape[1], LANES):
            out[:, start : start + LANES] = vector[at : at + 1, :]
            at += 1


def grad_kernel(seqs, place, *refs):
    (hid, cot, dup, first_i) = refs[:4]
    (query_i, keys_i, values_i, mixed_i, signed_i, slope_i, norm_i) = refs[4:11]
    wo0, wo1, wu0, wu1, gain2 = refs[11:16]
    outs = refs[16:22]
    low_o, own_o, other_o, gvec_o, hvec_o = refs[22:27]
    gqkv, gout, gb, hvec, vec = refs[27:32]
    dim = hid.shape[1]
    units = wu0.shape[1]
    part = 2 * LANES
    step = pl.program_id(0)
    scale = 1.0 / math.sqrt(HEAD_DIM)

    @pl.when(step == 0)
    def _():
        gqkv[...] = jnp.zeros_like(gqkv)
        gout[...] = jnp.zeros_like(gout)
        gb[...] = jnp.zeros_like(gb)
        hvec[...] = jnp.zeros_like(hvec)
        vec[...] = as_column(gain2[...])

    def hidden_grad(s):
        dnorm = dot(wu0[...], dup[s, :units, :]) + dot(wu1[...], dup[s, units:, :])
        plain, factor = norm_plain(hid[s].astype(F32))
        grad_out = cot[s * SEQ : (s + 1) * SEQ, :].astype(F32).T
        dhidden = grad_out + norm_back(dnorm, plain, factor, wide(vec[...], SEQ))
        hvec[0:dim, :] += lane_fold(dnorm * plain)
        hvec[dim : 2 * dim, :] += lane_fold(dnorm)
        hvec[2 * dim :, :] += lane_fold(dhidden)
        low = dhidden.astype(BF)
        low_o[s] = low
        dmixed = []
        for c, wo in enumerate((wo0, wo1)):
            spread = [
                jnp.broadcast_to(norm_i[s, c, g, e : e + 1, :], (HEAD_DIM, SEQ))
                for g in range(2)
                for e in range(2)
            ]
            dmixed.append((dot(wo[...], low) * jnp.concatenate(spread, axis=0)).astype(BF))
        return low, dmixed

    def inner(s, g, c, dmixed):
        dm = dmixed[c][g * LANES : (g + 1) * LANES]
        v_nat = turned(values_i[s, c, g])
        near_m, far_m = pair_near_far(dm)
        return dot(v_nat[:HALF], near_m), dot(v_nat, far_m), near_m, far_m

    def outer(s, g, c, near_s, far_s, near_m, far_m):
        q, k = query_i[s, c, g], keys_i[s, c, g]
        near_q, far_q = pair_near_far(q)
        low_pair = []
        for index, dsigned in enumerate((near_s, far_s)):
            block = slice(0, HALF) if index == 0 else slice(HALF, HALF + SEQ)
            lanes = slice(index * HALF, (index + 1) * HALF)
            signed = signed_i[s, c, g, block].astype(F32)
            row_dot = jnp.sum(signed * dsigned, axis=0, keepdims=True)
            row_dot = row_dot * jnp.concatenate(
                [norm_i[s, c, g, e : e + 1, lanes] for e in range(2)], axis=1
            )
            dscores = slope_i[s, c, g, block].astype(F32) * dsigned - signed * row_dot
            low_pair.append(dscores.astype(BF))
        near, far = low_pair
        near_p, far_p = dot(k[:, :HALF], near), dot(k, far)
        dq = jnp.concatenate(
            [
                jnp.concatenate([near_p[:HEAD_DIM, :HALF], far_p[:HEAD_DIM, :HALF]], axis=1),
                jnp.concatenate([near_p[HEAD_DIM:, HALF:], far_p[HEAD_DIM:, HALF:]], axis=1),
            ],
            axis=0,
        )
        near_p, far_p = tail_dot(near, near_q), tail_dot(far, far_q)
        dk = jnp.concatenate([far_p[:HALF] + near_p, far_p[HALF:]], axis=0)
        near_p = tail_dot(signed_i[s, c, g, :HALF], near_m)
        far_p = tail_dot(signed_i[s, c, g, HALF:], far_m)
        dv = jnp.concatenate([far_p[:HALF] + near_p, far_p[HALF:]], axis=0)
        dq, dk, dv = (dq * scale).astype(BF), dk.astype(BF), dv.astype(BF)
        dq_o, dk_o, dv_o = outs[3 * g : 3 * g + 3]
        rows = slice(c * LANES, (c + 1) * LANES)
        dq_o[s, rows, :], dk_o[s, :, rows], dv_o[s, :, rows] = dq, dk, dv
        base = g * 4 * LANES
        gb[base + c * LANES : base + (c + 1) * LANES, :] += lane_fold(dq.astype(F32))
        for index, block in ((2, dk), (3, dv)):
            at = base + index * LANES + 8 * c
            gb[at : at + 8, :] += jnp.sum(block.astype(F32).reshape(-1, 8, LANES), axis=0)

    def weight_grads(s, low, g):
        first = first_i[s]
        mixed = jnp.concatenate([mixed_i[s, 0, g], mixed_i[s, 1, g]], axis=0)
        gout[g * part : (g + 1) * part, :] += tail_dot(mixed, low)
        dq_o, dk_o, dv_o = outs[3 * g : 3 * g + 3]
        at = 3 * g * part
        gqkv[:, at : at + part] += tail_dot(first, dq_o[s])
        gqkv[:, at + part : at + 2 * part] += dot(first, dk_o[s])
        gqkv[:, at + 2 * part : at + 3 * part] += dot(first, dv_o[s])

    order = [(s, g, c) for s in range(seqs) for g in range(2) for c in range(2)]
    lows, mixes = {}, {}
    lows[0], mixes[0] = hidden_grad(0)
    ready = inner(*order[0], mixes[0])
    for n, (s, g, c) in enumerate(order):
        current = ready
        if n + 1 < len(order):
            following = order[n + 1]
            ready = inner(*following, mixes[following[0]])
        outer(s, g, c, *current)
        if c == 1 and n >= 3:
            back = order[n - 2]
            weight_grads(back[0], lows[back[0]], back[1])
        if (g, c) == (0, 1) and s + 1 < seqs:
            lows[s + 1], mixes[s + 1] = hidden_grad(s + 1)
    weight_grads(seqs - 1, lows[seqs - 1], 1)

    @pl.when(step == pl.num_programs(0) - 1)
    def _():
        for index in range(3):
            hvec_o[index : index + 1, :] = as_row(hvec[index * dim : (index + 1) * dim, :])
        for g in range(2):
            base = g * 4 * LANES
            tall = g * 4 * dim
            for c, grad_o in enumerate((own_o, other_o)):
                for index in range(3):
                    start = 3 * g * part + index * part + c * LANES
                    grad_o[tall + index * dim : tall + (index + 1) * dim, :] = gqkv[
                        :, start : start + LANES
                    ].astype(BF)
                for index in range(dim // LANES):
                    start = tall + 3 * dim + index * LANES
                    grad_o[start : start + LANES, :] = gout[
                        g * part + c * LANES : g * part + (c + 1) * LANES,
                        index * LANES : (index + 1) * LANES,
                    ].astype(BF)
                gvec_o[8 * g + c : 8 * g + c + 1, :] = as_row(
                    gb[base + c * LANES : base + (c + 1) * LANES, :]
                )
                for index in (2, 3):
                    rows = slice(base + index * LANES + 8 * c, base + index * LANES + 8 * c + 8)
                    at = 8 * g + 2 * index - 2 + c
                    gvec_o[at : at + 1, :] = jnp.sum(gb[rows, :], axis=0, keepdims=True)


def input_kernel(seqs, place, *refs):
    tok, dhid, dq0, dk0, dv0, dq1, dk1, dv1 = refs[:8]
    wq0, wq1, wk0, wk1, wv0, wv1, gain1 = refs[8:15]
    vec_ff, vec_hid, vec_at = refs[15:18]
    tgrad_o, whole_o, gvec_o, own_o, other_o = refs[18:23]
    gvec, vec, pack = refs[23:26]
    dim = tok.shape[1]

    @pl.when(pl.program_id(0) == 0)
    def _():
        gvec[...] = jnp.zeros_like(gvec)
        vec[...] = as_column(gain1[...])

    gain = wide(vec[...], SEQ)
    for s in range(seqs):
        rows = slice(s * SEQ, (s + 1) * SEQ)
        dnorm = None
        for c, (wq, wk, wv) in enumerate(((wq0, wk0, wv0), (wq1, wk1, wv1))):
            lanes = slice(c * LANES, (c + 1) * LANES)
            dq = jnp.concatenate([dq0[s, lanes, :], dq1[s, lanes, :]], axis=0)
            dk = jnp.concatenate([dk0[s, :, lanes], dk1[s, :, lanes]], axis=1)
            dv = jnp.concatenate([dv0[s, :, lanes], dv1[s, :, lanes]], axis=1)
            made = dot(wq[...], dq) + tail_dot(wk[...], dk) + tail_dot(wv[...], dv)
            dnorm = made if dnorm is None else dnorm + made
        plain, factor = norm_plain(tok[rows, :].astype(F32).T)
        gvec[0:dim, :] += lane_fold(dnorm * plain)
        gvec[dim : 2 * dim, :] += lane_fold(dnorm)
        tgrad = dhid[s].astype(F32) + norm_back(dnorm, plain, factor, gain)
        made = tgrad.T.astype(BF)
        tgrad_o[rows, :] = made
        whole_o[rows, :] = made

    @pl.when(pl.program_id(0) == pl.num_programs(0) - 1)
    def _():
        for index in range(2):
            gvec_o[index : index + 1, :] = as_row(gvec[index * dim : (index + 1) * dim, :])
        same = [(vec_hid, 0), (vec_hid, 1), (vec_ff, 0), (vec_hid, 2), (gvec_o, 0), (gvec_o, 1)]
        units = 2 * dim
        pack[...] = jnp.zeros_like(pack)
        for c, out in enumerate((own_o, other_o)):
            rows = [ref[r : r + 1, k : k + LANES] for ref, r in same for k in range(0, dim, LANES)]
            rows += [vec_at[r : r + 1, :] for i in range(3) for r in (2 * i + c, 8 + 2 * i + c)]
            rows += [
                vec_ff[4 + r : 5 + r, k : k + LANES]
                for r in range(c * units // dim, (c + 1) * units // dim)
                for k in range(0, dim, LANES)
            ]
            for index, row in enumerate(rows):
                pack[index : index + 1, :] = row
            out[...] = pack[...].astype(BF)


def whole_vmem():
    return pl.BlockSpec(memory_space=pltpu.VMEM)


def seq_block(seqs, *dims):
    return pl.BlockSpec((seqs,) + dims, lambda i: (i,) + (0,) * len(dims))


def params():
    return pltpu.CompilerParams(
        dimension_semantics=("arbitrary",), vmem_limit_bytes=VMEM_LIMIT
    )


def prefetch(grid, in_specs, out_specs, scratch=()):
    return pltpu.PrefetchScalarGridSpec(
        num_scalar_prefetch=1, grid=grid, in_specs=in_specs, out_specs=out_specs, scratch_shapes=scratch
    )


def row_block(seqs, dim, steps):
    return pl.BlockSpec((seqs * SEQ, dim), lambda i, place: (place[0] * steps + i, 0))


def placed_seq_block(seqs, *dims):
    return pl.BlockSpec((seqs,) + dims, lambda i, place: (i,) + (0,) * len(dims))


def attn_call(place, tokens, own, weights, vectors, seqs):
    dim = tokens.shape[1]
    count = own // SEQ
    steps = count // seqs
    feat = (2, 2, LANES, SEQ)
    wide_block = (2, 2, HALF + SEQ, SEQ)
    shape = jax.ShapeDtypeStruct
    return pl.pallas_call(
        functools.partial(attn_kernel, seqs),
        grid_spec=prefetch(
            (steps,),
            [row_block(seqs, dim, steps)] + [whole_vmem()] * 13,
            [placed_seq_block(seqs, *feat)] * 4
            + [placed_seq_block(seqs, *wide_block)] * 2
            + [placed_seq_block(seqs, 2, 2, 8, SEQ)]
            + [placed_seq_block(seqs, dim, SEQ)] * 2,
            [
                pltpu.VMEM((3 * dim, dim), BF),
                pltpu.VMEM((dim, dim), BF),
                pltpu.VMEM((6 * dim, LANES), F32),
            ],
        ),
        out_shape=[shape((count,) + feat, BF)] * 4
        + [shape((count,) + wide_block, BF)] * 2
        + [shape((count, 2, 2, 8, SEQ), F32)]
        + [shape((count, dim, SEQ), BF)] * 2,
        compiler_params=params(),
        cost_estimate=pl.CostEstimate(flops=1, bytes_accessed=1, transcendentals=0),
        name="attn_forward",
    )(place, tokens, *weights, *vectors)


def grad_call(place, hidden, cotangent, dup, first, saved, weights, seqs):
    count, dim = hidden.shape[:2]
    steps = count // seqs
    units = dup.shape[1]
    every = lambda *dims: placed_seq_block(seqs, 2, 2, *dims)
    shape = jax.ShapeDtypeStruct
    part = 2 * LANES
    trio = [
        placed_seq_block(seqs, part, SEQ),
        placed_seq_block(seqs, SEQ, part),
        placed_seq_block(seqs, SEQ, part),
    ]
    return pl.pallas_call(
        functools.partial(grad_kernel, seqs),
        grid_spec=prefetch(
            (steps,),
            [
                placed_seq_block(seqs, dim, SEQ),
                row_block(seqs, dim, steps),
                placed_seq_block(seqs, units, SEQ),
                placed_seq_block(seqs, dim, SEQ),
            ]
            + [every(LANES, SEQ)] * 4
            + [every(HALF + SEQ, SEQ)] * 2
            + [every(8, SEQ)]
            + [whole_vmem()] * 5,
            trio * 2 + [placed_seq_block(seqs, dim, SEQ)] + [whole_vmem()] * 4,
            [
                pltpu.VMEM((dim, 6 * part), F32),
                pltpu.VMEM((2 * part, dim), F32),
                pltpu.VMEM((8 * LANES, LANES), F32),
                pltpu.VMEM((3 * dim, LANES), F32),
                pltpu.VMEM((dim, LANES), F32),
            ],
        ),
        out_shape=[
            shape((count, part, SEQ), BF),
            shape((count, SEQ, part), BF),
            shape((count, SEQ, part), BF),
        ]
        * 2
        + [
            shape((count, dim, SEQ), BF),
            shape((8 * dim, LANES), BF),
            shape((8 * dim, LANES), BF),
            shape((16, LANES), F32),
            shape((8, dim), F32),
        ],
        compiler_params=params(),
        cost_estimate=pl.CostEstimate(flops=1, bytes_accessed=1, transcendentals=0),
        name="attn_backward",
    )(place, hidden, cotangent, dup, first, *saved, *weights)


def input_call(place, tokens, dhidden, pieces, weights, gain1, vectors, grow, seqs):
    dim = tokens.shape[1]
    count = dhidden.shape[0]
    steps = count // seqs
    part = 2 * LANES
    trio = [
        placed_seq_block(seqs, part, SEQ),
        placed_seq_block(seqs, SEQ, part),
        placed_seq_block(seqs, SEQ, part),
    ]
    return pl.pallas_call(
        functools.partial(input_kernel, seqs),
        grid_spec=prefetch(
            (steps,),
            [row_block(seqs, dim, steps), placed_seq_block(seqs, dim, SEQ)]
            + trio * 2
            + [whole_vmem()] * 10,
            [
                pl.BlockSpec((seqs * SEQ, dim), lambda i, place: (i, 0)),
                row_block(seqs, dim, steps),
            ]
            + [whole_vmem()] * 3,
            [
                pltpu.VMEM((2 * dim, LANES), F32),
                pltpu.VMEM((dim, LANES), F32),
                pltpu.VMEM((grow, LANES), F32),
            ],
        ),
        out_shape=[
            jax.ShapeDtypeStruct((count * SEQ, dim), BF),
            jax.ShapeDtypeStruct(tokens.shape, BF),
            jax.ShapeDtypeStruct((8, dim), F32),
            jax.ShapeDtypeStruct((grow, LANES), BF),
            jax.ShapeDtypeStruct((grow, LANES), BF),
        ],
        compiler_params=params(),
        cost_estimate=pl.CostEstimate(flops=1, bytes_accessed=1, transcendentals=0),
        name="input_grad",
    )(place, tokens, dhidden, *pieces, *weights, gain1, *vectors)


def mlp_call(place, hidden, cotangent, weights, vectors, seqs, block):
    count, dim = hidden.shape[:2]
    steps = count // seqs
    units = weights[0].shape[1]
    shape = jax.ShapeDtypeStruct
    return pl.pallas_call(
        functools.partial(mlp_kernel, seqs, block),
        grid_spec=prefetch(
            (steps,),
            [placed_seq_block(seqs, dim, SEQ), row_block(seqs, dim, steps)] + [whole_vmem()] * 8,
            [placed_seq_block(seqs, 2 * units, SEQ)] * 2 + [whole_vmem()] * 3,
            [
                pltpu.VMEM((2 * units, dim), BF),
                pltpu.VMEM((dim + 16, 2 * units), F32),
                pltpu.VMEM((2 * units + 16, dim), F32),
                pltpu.VMEM((2 * dim, LANES), F32),
                pltpu.VMEM((2 * units, LANES), F32),
            ],
        ),
        out_shape=[
            shape((count, 2 * units, SEQ), BF),
            shape((count, 2 * units, SEQ), BF),
            shape((2 * units, dim), BF),
            shape((2 * units, dim), BF),
            shape((8, dim), F32),
        ],
        compiler_params=params(),
        cost_estimate=pl.CostEstimate(flops=1, bytes_accessed=1, transcendentals=0),
        name="feed_forward",
    )(place, hidden, cotangent, *weights, *vectors)


def out_call(place, hidden, act, weights, bdown, rows, seqs):
    count, dim = hidden.shape[:2]
    units = act.shape[1]
    steps = count // seqs
    return pl.pallas_call(
        functools.partial(out_kernel, seqs),
        grid_spec=prefetch(
            (steps,),
            [placed_seq_block(seqs, dim, SEQ), placed_seq_block(seqs, units, SEQ)] + [whole_vmem()] * 3,
            [
                pl.BlockSpec((seqs * SEQ, dim), lambda i, place: (i, 0)),
                row_block(seqs, dim, steps),
            ],
            [pltpu.VMEM((dim, units), BF), pltpu.VMEM((dim, LANES), F32)],
        ),
        out_shape=[
            jax.ShapeDtypeStruct((count * SEQ, dim), BF),
            jax.ShapeDtypeStruct((rows, dim), BF),
        ],
        compiler_params=params(),
        cost_estimate=pl.CostEstimate(flops=1, bytes_accessed=1, transcendentals=0),
        name="layer_out",
    )(place, hidden, act, *weights, bdown)


def ff_unpack_call(total, units):
    dim = total.shape[1]
    return pl.pallas_call(
        ff_unpack_kernel,
        in_specs=[whole_vmem()],
        out_specs=[whole_vmem()] * 2,
        out_shape=[
            jax.ShapeDtypeStruct((dim, units), F32),
            jax.ShapeDtypeStruct((units, dim), F32),
        ],
        compiler_params=pltpu.CompilerParams(vmem_limit_bytes=VMEM_LIMIT),
        name="ff_unpack",
    )(total)


def at_unpack_call(here, blocks, vecs, dim, local, sizes):
    shape = jax.ShapeDtypeStruct
    outs = [shape((dim, local), F32)] * 3 + [shape((local, dim), F32)]
    outs += [shape((1, n), F32) for n in sizes]
    return pl.pallas_call(
        at_unpack_kernel,
        in_specs=[pl.BlockSpec(memory_space=pltpu.SMEM)] + [whole_vmem()] * 8,
        out_specs=[whole_vmem()] * len(outs),
        out_shape=outs,
        scratch_shapes=[pltpu.VMEM((4,) + blocks[0].shape, BF)],
        compiler_params=pltpu.CompilerParams(vmem_limit_bytes=VMEM_LIMIT),
        name="at_unpack",
    )(here, *blocks, *vecs)


def shifted(value, axis, count, shift):
    return lax.ppermute(value, axis, [(i, (i + shift) % count) for i in range(count)])


def gathered(value, count, axis):
    blocks = [value] + [shifted(value, "mp", count, -r) for r in range(1, count)]
    half = count // 2
    return [
        blocks[g * half] if half == 1 else jnp.concatenate(blocks[g * half : (g + 1) * half], axis)
        for g in range(2)
    ]


def total_of(blocks):
    total = blocks[0].astype(F32)
    for block in blocks[1:]:
        total = total + block.astype(F32)
    return total.astype(BF)


class DpSum:
    def __init__(self, count):
        self.count = count
        self.groups = []
        bit = 1
        while bit < count:
            size = min(4, count // bit)
            self.groups.append((bit, size))
            bit *= size

    def swap(self, value, distance):
        return lax.ppermute(value, "dp", [(i, i ^ distance) for i in range(self.count)])

    def place(self, bit, size):
        return (lax.axis_index("dp") // bit) % size

    def scatter(self, value, stage):
        bit, size = self.groups[stage]
        here = self.place(bit, size)
        parts = value.reshape(size, value.shape[0] // size, value.shape[1])
        pick = lambda m: lax.dynamic_index_in_dim(parts, here ^ m, 0, keepdims=False)
        return [pick(0)] + [self.swap(pick(m), m * bit) for m in range(1, size)]

    def gather(self, value, stage):
        bit, size = self.groups[stage]
        return [value] + [self.swap(value, m * bit) for m in range(1, size)]

    def join(self, blocks, stage):
        bit, size = self.groups[stage]
        here = self.place(bit, size)
        whole = jnp.zeros((size,) + blocks[0].shape, blocks[0].dtype)
        for m, block in enumerate(blocks):
            whole = lax.dynamic_update_index_in_dim(whole, block, here ^ m, 0)
        return whole.reshape(-1, blocks[0].shape[1])


def body(mp, dp, *args):
    (tokens, gain1, shift1, wq, bq, wk, bk, wv, bv, wo, bo) = args[:11]
    (gain2, shift2, wu, bu, wd, bd, cotangent) = args[11:]
    rows, dim = tokens.shape
    local = wq.shape[1]
    units = wu.shape[1]
    own = rows // mp
    per = mp // 2
    me = lax.axis_index("mp")
    place = me.astype(jnp.int32).reshape(1)
    tie = lax.optimization_barrier
    dp_sum = DpSum(dp)

    weights = []
    for w in (wq, wk, wv):
        weights += gathered(w, mp, 1)
    weights += gathered(wo, mp, 0)
    small = jnp.concatenate([bq, bk, bv, bu]).reshape(1, -1)
    smalls = [small] + [shifted(small, "mp", mp, -r) for r in range(1, mp)]
    if per > 1:
        cuts = [0, local, 2 * local, 3 * local, 3 * local + units]
        smalls = [
            jnp.concatenate(
                [
                    block[:, lo:hi]
                    for lo, hi in zip(cuts, cuts[1:])
                    for block in smalls[c * per : (c + 1) * per]
                ],
                axis=1,
            )
            for c in range(2)
        ]
    weights, smalls, wu, wd = tie((weights, smalls, wu, wd))
    mlp_weights = gathered(wu, mp, 1) + gathered(wd, mp, 0)
    gain1, shift1, bo, gain2, shift2, bd = (
        v.reshape(1, -1) for v in (gain1, shift1, bo, gain2, shift2, bd)
    )

    def filled(full, others):
        for r, block in enumerate(others, 1):
            full = lax.dynamic_update_slice_in_dim(full, block, ((me - r) % mp) * own, 0)
        return full

    def spread_out(part):
        return [shifted(part, "mp", mp, r) for r in range(1, mp)]

    def ff_piece(grad, r):
        g, j = divmod(r, per)
        if per == 1:
            return grad[g]
        up = grad[g][: per * units].reshape(-1, dim, dim)
        up = jnp.concatenate(list(up), axis=1)[:, j * units : (j + 1) * units]
        down = grad[g][per * units + j * units : per * units + (j + 1) * units]
        return jnp.concatenate([up.reshape(-1, dim), down], axis=0)

    def at_piece(grads, r):
        g, j = divmod(r, per)
        if per == 1:
            return jnp.concatenate([grad[g] for grad in grads], axis=0)
        parts = []
        for index in range(3):
            block = [grad[g][index * dim : (index + 1) * dim] for grad in grads]
            block = jnp.concatenate(block, axis=1)[:, j * local : (j + 1) * local]
            parts.append(block.reshape(-1, LANES))
        block = [grad[g][3 * dim :].reshape(-1, LANES, LANES) for grad in grads]
        block = jnp.concatenate([jnp.concatenate(list(b), axis=1) for b in block], axis=0)
        parts.append(block[j * local : (j + 1) * local].reshape(-1, LANES))
        return jnp.concatenate(parts, axis=0)

    def mp_send(piece):
        return [piece(0)] + [shifted(piece(r), "mp", mp, r) for r in range(1, mp)]

    *saved, first, hidden = attn_call(
        place, tokens, own, weights, [gain1, shift1, bo] + smalls, SEQS["attn"]
    )
    hidden, mlp_weights = tie((hidden, mlp_weights))
    act, dup, *grad_ff, vec_ff = mlp_call(
        place, hidden, cotangent, mlp_weights, [gain2, shift2] + smalls, SEQS["mlp"], 512
    )
    ff = total_of(mp_send(lambda r: ff_piece(grad_ff, r)))
    dup, ff = tie((dup, ff))
    ff = lax.psum(ff, "dp")
    *pieces, low, grad_own, grad_other, vec_at, vec_hid = grad_call(
        place,
        hidden,
        cotangent,
        dup,
        first,
        saved,
        weights[6:] + mlp_weights[:2] + [gain2],
        SEQS["grad"],
    )
    grad_at = [grad_own, grad_other]

    sizes = [dim] * 6 + [local] * 3 + [units]
    grow = max(-(-sum(sizes) // (16 * LANES)) * 16, -(-(6 * dim + 6 * LANES + 2 * dim) // (16 * LANES)) * 16)

    def input_grads(low):
        return input_call(
            place,
            tokens,
            low,
            pieces,
            weights[:6],
            gain1,
            [vec_ff, vec_hid, vec_at],
            grow,
            SEQS["input"],
        )

    def layer_outs(act):
        return out_call(place, hidden, act, mlp_weights[2:], bd, rows, SEQS["out"])

    def finish(low, act, grad_at):
        at = dp_sum.scatter(total_of(mp_send(lambda r: grad_at[r])), 0)
        low, at[0] = tie((low, at[0]))
        tgrad, tgrad_full, _, *vec_low = input_grads(low)
        at, tgrad = tie((at, tgrad))
        at = dp_sum.scatter(total_of(at), 1)
        vecs = mp_send(lambda r: vec_low[r])
        tgrads = spread_out(tgrad)
        act, at[0], vecs[0], tgrad = tie((act, at[0], vecs[0], tgrad))
        out, out_full = layer_outs(act)
        at, vecs, out, tgrads = tie((at, vecs, out, tgrads))
        at = dp_sum.gather(total_of(at), 1)
        vecs = dp_sum.gather(total_of(vecs), 0)
        outs = spread_out(out)
        at = dp_sum.gather(dp_sum.join(at, 1), 0)
        vecs = dp_sum.gather(total_of(vecs), 1)
        tgrad_full, tgrads, at[0] = tie((tgrad_full, tgrads, at[0]))
        tgrad_full = filled(tgrad_full, tgrads)
        out_full = filled(out_full, outs)
        at, vecs, out_full, tgrad_full = tie((at, vecs, out_full, tgrad_full))
        here = dp_sum.place(*dp_sum.groups[0]).astype(jnp.int32) ^ jnp.arange(4, dtype=jnp.int32)
        made = at_unpack_call(here, at, vecs, dim, local, sizes)
        flat = [v.reshape(-1) for v in made[4:]]
        return (out_full, tgrad_full, flat[:6], made[:3], flat[6:9], made[3], flat[9])

    def finish_any(low, act, grad_at):
        tgrad, tgrad_full, vec_in, *_ = input_grads(low)
        out, out_full = layer_outs(act)
        same = [vec_hid[:2], vec_ff[:1], vec_hid[2:3], vec_in[:2]]
        same = jnp.concatenate([v.reshape(-1) for v in same])
        vec_at0, vec_at1 = vec_at[:8], vec_at[8:]
        grads = [[v[: 4 * dim] for v in grad_at], [v[4 * dim :] for v in grad_at]]
        gbup = vec_ff[4:].reshape(-1)
        bias = [
            jnp.concatenate([v[2 * i + c] for c in range(2) for v in (vec_at0, vec_at1)])
            for i in range(3)
        ]

        def all_piece(r):
            vector = jnp.concatenate(
                [same]
                + [b[r * local : (r + 1) * local] for b in bias]
                + [gbup[r * units : (r + 1) * units]]
            )
            size = -(-vector.shape[0] // (16 * dp * LANES)) * (16 * dp * LANES)
            vector = jnp.pad(vector, (0, size - vector.shape[0])).reshape(-1, LANES).astype(BF)
            return jnp.concatenate([at_piece(grads, r), vector], axis=0)

        at = total_of(mp_send(all_piece))
        stages = len(dp_sum.groups)
        for stage in range(stages):
            at = total_of(dp_sum.scatter(at, stage))
        for stage in reversed(range(stages)):
            at = dp_sum.join(dp_sum.gather(at, stage), stage)
        at = at.astype(F32)
        each = dim * local // LANES
        if per == 1:
            halves = [at[: 4 * dim], at[4 * dim : 8 * dim]]
            g_qkv = [
                jnp.concatenate([h[i * dim : (i + 1) * dim] for h in halves], axis=1)
                for i in range(3)
            ]
            g_out = [h[3 * dim :].reshape(-1, LANES, LANES) for h in halves]
            g_out = jnp.concatenate([jnp.concatenate(list(h), axis=1) for h in g_out], axis=0)
        else:
            g_qkv = [at[i * each : (i + 1) * each].reshape(dim, local) for i in range(3)]
            g_out = at[3 * each : 4 * each].reshape(local, dim)
        vector = at[4 * each :].reshape(-1)
        parts = []
        for size in sizes:
            parts.append(vector[:size])
            vector = vector[size:]
        return (
            filled(out_full, spread_out(out)),
            filled(tgrad_full, spread_out(tgrad)),
            parts[:6],
            g_qkv,
            parts[6:9],
            g_out,
            parts[9],
        )

    if per != 1 or [size for _, size in dp_sum.groups] != [4, 4]:
        finish = finish_any
    blank = jax.eval_shape(finish, low, act, grad_at)
    out_full, tgrad_full, g_same, g_qkv, g_bias, g_out, g_bup = lax.cond(
        lax.axis_index("dp") != dp,
        finish,
        lambda *_: jax.tree.map(lambda v: jnp.zeros(v.shape, v.dtype), blank),
        low,
        act,
        grad_at,
    )
    if per == 1:
        g_up, g_down = ff_unpack_call(ff, units)
    else:
        ff = ff.astype(F32)
        g_up = ff[:units].reshape(dim, units)
        g_down = ff[units:]
    return (
        out_full,
        tgrad_full,
        g_same[4],
        g_same[5],
        g_qkv[0],
        g_bias[0],
        g_qkv[1],
        g_bias[1],
        g_qkv[2],
        g_bias[2],
        g_out,
        g_same[3],
        g_same[0],
        g_same[1],
        g_up,
        g_bup,
        g_down,
        g_same[2],
    )


def solution(mesh):
    split = P("dp", None)
    columns, some, lines = P(None, "mp"), P("mp"), P("mp", None)
    return jax.shard_map(
        functools.partial(body, mesh.shape["mp"], mesh.shape["dp"]),
        mesh=mesh,
        in_specs=(split, P(), P(), columns, some, columns, some, columns, some, lines, P())
        + (P(), P(), columns, some, lines, P(), split),
        out_specs=(split, split, P(), P(), columns, some, columns, some, columns, some, lines)
        + (P(), P(), P(), columns, some, lines, P()),
        check_vma=False,
    )
```

```python
import functools
import math

import jax
import jax.numpy as jnp
from jax import lax
from jax.experimental import pallas as pl
from jax.experimental.pallas import tpu as pltpu
from jax.sharding import PartitionSpec as P

HEAD_DIM = 64
SEQ = 256
HALF = SEQ // 2
LANES = 128
BF = jnp.bfloat16
F32 = jnp.float32
VMEM_LIMIT = 60 * 1024 * 1024
SEQS = {"attn": 4, "mlp": 2, "grad": 2, "input": 4, "out": 4}


def dot(left, right):
    return jnp.dot(left, right, preferred_element_type=F32)


def tail_dot(left, right):
    return lax.dot_general(left, right, (((1,), (1,)), ((), ())), preferred_element_type=F32)


def turned(block):
    return block.astype(F32).T.astype(BF)


def wide(column, lanes):
    return jnp.concatenate([column] * (lanes // LANES), axis=1)


def lane_fold(rows):
    total = rows[:, :LANES]
    for start in range(LANES, rows.shape[1], LANES):
        total = total + rows[:, start : start + LANES]
    return total


def as_column(row):
    return jnp.broadcast_to(row, (LANES, row.shape[1])).T


def as_row(sums):
    return jnp.sum(sums.T, axis=0, keepdims=True)


def norm_plain(x):
    center = x - jnp.mean(x, axis=0, keepdims=True)
    factor = lax.rsqrt(jnp.mean(center * center, axis=0, keepdims=True) + 1e-05)
    return center * factor, factor


def norm_back(grad, plain, factor, gain):
    scaled = grad * gain
    return factor * (
        scaled
        - jnp.mean(scaled, axis=0, keepdims=True)
        - plain * jnp.mean(scaled * plain, axis=0, keepdims=True)
    )


def upper_mask():
    return lax.broadcasted_iota(jnp.int32, (HALF, HALF), 0) <= lax.broadcasted_iota(
        jnp.int32, (HALF, HALF), 1
    )


def smooth(scores):
    square = scores * scores + 1.0
    inverse = lax.rsqrt(square)
    return inverse, square * inverse


def pair_diag(left, right):
    zero = jnp.zeros_like(left)
    return jnp.concatenate(
        [jnp.concatenate([left, zero], axis=1), jnp.concatenate([zero, right], axis=1)], axis=0
    )


def pair_near_far(rows):
    left, right = rows[:HEAD_DIM], rows[HEAD_DIM:]
    return (
        pair_diag(left[:, :HALF], right[:, :HALF]),
        pair_diag(left[:, HALF:], right[:, HALF:]),
    )


def attend(scores, mask):
    inverse, root = smooth(scores)
    if scores.shape[0] > HALF:
        diagonal = jnp.where(mask, root[HALF:], -1e30)
        magnitude = jnp.concatenate([root[:HALF], diagonal], axis=0)
    else:
        magnitude = jnp.where(mask, root, -1e30)
    top = jnp.max(magnitude, axis=0, keepdims=True)
    expo = jnp.exp(magnitude - top)
    norm = 1.0 / jnp.sum(expo, axis=0, keepdims=True)
    low_expo, sign, low = expo.astype(BF), (scores * inverse).astype(BF), inverse.astype(BF)
    return sign * low_expo, (low * low * low + sign * sign) * low_expo, norm


def attn_kernel(seqs, place, *refs):
    (tok, wq0, wq1, wk0, wk1, wv0, wv1, wo0, wo1) = refs[:9]
    gain1, shift1, bout, small0, small1 = refs[9:14]
    (query_o, keys_o, values_o, mixed_o, signed_o, slope_o, norm_o, first_o, hidden_o) = refs[14:23]
    wqkv_t, wo_t, vec = refs[23:26]
    dim = tok.shape[1]
    lanes = seqs * SEQ

    @pl.when(pl.program_id(0) == 0)
    def _():
        part = dim // 2
        for index, ref in enumerate((wq0, wq1, wk0, wk1, wv0, wv1)):
            wqkv_t[index * part : (index + 1) * part, :] = turned(ref[...])
        wo_t[:, :part] = turned(wo0[...])
        wo_t[:, part:] = turned(wo1[...])
        for index, ref in ((0, gain1), (1, shift1), (5, bout)):
            vec[index * dim : (index + 1) * dim, :] = as_column(ref[...])
        for index in range(3):
            for c, ref in enumerate((small0, small1)):
                start = (2 + index) * dim + c * part
                vec[start : start + part, :] = as_column(ref[:, index * part : (index + 1) * part])

    half = lax.broadcasted_iota(jnp.int32, (HALF, SEQ), 1)
    mask = lax.broadcasted_iota(jnp.int32, (HALF, SEQ), 0) <= jnp.where(half < HALF, half, half - HALF)
    pairs = dim // LANES
    scale = jnp.asarray(1.0 / math.sqrt(HEAD_DIM), BF)

    def prepare(s):
        x = tok[s * SEQ : (s + 1) * SEQ, :].astype(F32).T
        plain, _ = norm_plain(x)
        first = (plain * wide(vec[0:dim, :], SEQ) + wide(vec[dim : 2 * dim, :], SEQ)).astype(BF)
        first_o[s] = first
        return first

    def project(s, p, first):
        c, g = divmod(p, 2)
        made = []
        for index in range(3):
            rows = slice(index * dim + p * LANES, index * dim + (p + 1) * LANES)
            bias = slice(2 * dim + rows.start, 2 * dim + rows.stop)
            made.append((dot(wqkv_t[rows, :], first) + wide(vec[bias, :], SEQ)).astype(BF))
        query, keys, values = made[0] * scale, made[1], made[2]
        query_o[s, c, g], keys_o[s, c, g], values_o[s, c, g] = query, keys, values
        near_q, far_q = pair_near_far(query)
        kp = turned(keys)
        return dot(kp[:HALF], near_q), dot(kp, far_q), values

    def mix(s, p, near_s, far_s, values):
        c, g = divmod(p, 2)
        near, near_g, near_n = attend(near_s, mask)
        far, far_g, far_n = attend(far_s, mask)
        norms = [
            jnp.concatenate([near_n[:, lanes], far_n[:, lanes]], axis=1)
            for lanes in (slice(0, HALF), slice(HALF, SEQ))
        ]
        signed_o[s, c, g, :HALF], signed_o[s, c, g, HALF:] = near, far
        slope_o[s, c, g, :HALF], slope_o[s, c, g, HALF:] = near_g, far_g
        near_m, far_m = dot(values[:, :HALF], near), dot(values, far)
        made = jnp.concatenate(
            [
                jnp.concatenate([near_m[:HEAD_DIM, :HALF], far_m[:HEAD_DIM, :HALF]], axis=1) * norms[0],
                jnp.concatenate([near_m[HEAD_DIM:, HALF:], far_m[HEAD_DIM:, HALF:]], axis=1) * norms[1],
            ],
            axis=0,
        ).astype(BF)
        mixed_o[s, c, g] = made
        for e in range(2):
            norm_o[s, c, g, e : e + 1, :] = norms[e]
        return made

    def finish(s, mixed):
        x = tok[s * SEQ : (s + 1) * SEQ, :].astype(F32).T
        made = x + dot(wo_t[...], jnp.concatenate(mixed, axis=0)) + wide(vec[5 * dim : 6 * dim, :], SEQ)
        hidden_o[s] = made.astype(BF)

    first = prepare(0)
    ready = project(0, 0, first)
    mixed = []
    for s in range(seqs):
        done, mixed = mixed, []
        for p in range(pairs):
            current = ready
            if p == pairs // 2 and s + 1 < seqs:
                following = prepare(s + 1)
            if p + 1 < pairs:
                ready = project(s, p + 1, first)
            elif s + 1 < seqs:
                first = following
                ready = project(s + 1, 0, first)
            mixed.append(mix(s, p, *current))
            if p == 0 and s > 0:
                finish(s - 1, done)
    finish(seqs - 1, mixed)


def mlp_kernel(seqs, block, place, *refs):
    (hid, cot, wu0, wu1, wd0, wd1, gain2, shift2, small0, small1) = refs[:10]
    (act_o, low_o, own_o, other_o, gvec_o) = refs[10:15]
    wu_t, gup, gdown, gvec, vec, bup = refs[15:21]
    dim = hid.shape[1]
    units = wu0.shape[1]
    lanes = seqs * SEQ
    step = pl.program_id(0)

    @pl.when(step == 0)
    def _():
        for index, (up, small) in enumerate(((wu0, small0), (wu1, small1))):
            rows = slice(index * units, (index + 1) * units)
            wu_t[rows, :] = turned(up[...])
            bup[rows, :] = as_column(small[:, small.shape[1] - units :])
        for index, ref in enumerate((gain2, shift2)):
            vec[index * dim : (index + 1) * dim, :] = as_column(ref[...])
        gup[...] = jnp.zeros_like(gup)
        gdown[...] = jnp.zeros_like(gdown)
        gvec[...] = jnp.zeros_like(gvec)

    hidden = jnp.concatenate([hid[s] for s in range(seqs)], axis=1).astype(F32)
    grad_out = cot[...].astype(F32).T
    grad_low = grad_out.astype(BF)
    gain = wide(vec[0:dim, :], lanes)
    plain, factor = norm_plain(hidden)
    second = (plain * gain + wide(vec[dim : 2 * dim, :], lanes)).astype(BF)
    ones = jnp.ones((16, lanes), BF)
    second_ones = jnp.concatenate([second, ones], axis=0)
    dnorm = None
    for start in range(0, 2 * units, block):
        span = slice(start, start + block)
        half, inner = divmod(start, units)
        up_ref, down_ref = ((wu0, wd0), (wu1, wd1))[half]
        inner = slice(inner, inner + block)
        upper = dot(wu_t[span, :], second) + wide(bup[span, :], lanes)
        dact = dot(down_ref[inner, :], grad_low)
        part = upper * (1.0 / math.sqrt(2.0))
        cdf = 0.5 * lax.erf(part) + 0.5
        density = jnp.exp2((part * part) * (-1.0 / math.log(2.0)))
        act = (upper * cdf).astype(BF)
        dup = (dact * (cdf + part * density * (1.0 / math.sqrt(math.pi)))).astype(BF)
        for s in range(seqs):
            act_o[s, span, :] = act[:, s * SEQ : (s + 1) * SEQ]
        dn_part = dot(up_ref[:, inner], dup)
        dnorm = dn_part if dnorm is None else dnorm + dn_part
        gup[:, span] += tail_dot(second_ones, dup)
        if start == 0:
            act = jnp.concatenate([ones, act], axis=0)
            gdown[: 16 + block, :] += tail_dot(act, grad_low)
        else:
            gdown[16 + start : 16 + start + block, :] += tail_dot(act, grad_low)
    gvec[0:dim, :] += lane_fold(dnorm * plain)
    gvec[dim : 2 * dim, :] += lane_fold(dnorm)
    dhidden = grad_out + norm_back(dnorm, plain, factor, gain)
    gvec[2 * dim :, :] += lane_fold(dhidden)
    for s in range(seqs):
        low_o[s] = dhidden[:, s * SEQ : (s + 1) * SEQ].astype(BF)

    @pl.when(step == pl.num_programs(0) - 1)
    def _():
        for half, grad_o in enumerate((own_o, other_o)):
            for index in range(units // dim):
                start = half * units + index * dim
                grad_o[index * dim : (index + 1) * dim, :] = gup[:dim, start : start + dim].astype(BF)
            grad_o[units:, :] = gdown[16 + half * units : 16 + (half + 1) * units, :].astype(BF)
        for index, row in ((0, 0), (1, 1), (2, 3)):
            gvec_o[row : row + 1, :] = as_row(gvec[index * dim : (index + 1) * dim, :])
        gvec_o[2:3, :] = gdown[:1, :]
        for index in range(2 * units // dim):
            gvec_o[4 + index : 5 + index, :] = gup[dim : dim + 1, index * dim : (index + 1) * dim]


def out_kernel(seqs, place, hid, act, wd0, wd1, bdown, out_o, whole_o, wd_t, vec):
    units = wd0.shape[0]

    @pl.when(pl.program_id(0) == 0)
    def _():
        wd_t[:, :units] = turned(wd0[...])
        wd_t[:, units:] = turned(wd1[...])
        vec[...] = as_column(bdown[...])

    for s in range(seqs):
        rows = slice(s * SEQ, (s + 1) * SEQ)
        out = hid[s].astype(F32) + dot(wd_t[...], act[s]) + wide(vec[...], SEQ)
        made = out.T.astype(BF)
        out_o[rows, :] = made
        whole_o[rows, :] = made


def ff_unpack_kernel(total, up_o, down_o):
    dim, units = up_o.shape
    for start in range(0, units, dim):
        up_o[:, start : start + dim] = total[start : start + dim, :].astype(F32)
    down_o[...] = total[units:, :].astype(F32)


def at_unpack_kernel(here, b0, b1, b2, b3, *refs):
    outs, hold = refs[:-1], refs[-1]
    size = b0.shape[0]
    for m, block in enumerate((b0, b1, b2, b3)):
        hold[here[m]] = block[...]
    rows = lambda start, count: [
        hold[k, max(start - k * size, 0) : min(start + count - k * size, size), :].astype(F32)
        for k in range(4)
        if start < (k + 1) * size and start + count > k * size
    ]
    get = lambda start, count: jnp.concatenate(rows(start, count), axis=0)
    dim = outs[0].shape[0]
    for g in range(2):
        base = g * 4 * dim
        for index in range(3):
            outs[index][:, g * LANES : (g + 1) * LANES] = get(base + index * dim, dim)
        for index in range(dim // LANES):
            outs[3][g * LANES : (g + 1) * LANES, index * LANES : (index + 1) * LANES] = get(
                base + 3 * dim + index * LANES, LANES
            )
    at = 8 * dim
    for out in outs[4:]:
        for start in range(0, out.shape[1], LANES):
            out[:, start : start + LANES] = get(at // 16 * 16, 16)[at % 16 : at % 16 + 1]
            at += 1


def grad_kernel(seqs, *refs):
    (low_i, first_i, query_i, keys_i, values_i, mixed_i, signed_i, slope_i, norm_i) = refs[:9]
    wo0, wo1 = refs[9:11]
    outs = refs[11:17]
    own_o, other_o, gvec_o = refs[17:20]
    gqkv, gout, gb = refs[20:23]
    dim = low_i.shape[1]
    part = 2 * LANES
    step = pl.program_id(0)
    scale = 1.0 / math.sqrt(HEAD_DIM)

    @pl.when(step == 0)
    def _():
        gqkv[...] = jnp.zeros_like(gqkv)
        gout[...] = jnp.zeros_like(gout)
        gb[...] = jnp.zeros_like(gb)

    first = jnp.concatenate([first_i[s] for s in range(seqs)], axis=1)
    low = jnp.concatenate([low_i[s] for s in range(seqs)], axis=1)

    def mix_grad(s, g):
        place = slice(g * LANES, (g + 1) * LANES)
        spread = lambda c, e: jnp.broadcast_to(norm_i[s, c, g, e : e + 1, :], (HEAD_DIM, SEQ))
        return [
            (
                dot(wo[place, :], low_i[s])
                * jnp.concatenate([spread(c, e) for e in range(2)], axis=0)
            ).astype(BF)
            for c, wo in enumerate((wo0, wo1))
        ]

    def inner(s, g, c, dmixed):
        dm = dmixed[c]
        v_nat = turned(values_i[s, c, g])
        near_m, far_m = pair_near_far(dm)
        return dot(v_nat[:HALF], near_m), dot(v_nat, far_m), near_m, far_m

    def outer(s, g, c, near_s, far_s, near_m, far_m):
        q, k = query_i[s, c, g], keys_i[s, c, g]
        near_q, far_q = pair_near_far(q)
        low_pair = []
        for index, dsigned in enumerate((near_s, far_s)):
            block = slice(0, HALF) if index == 0 else slice(HALF, HALF + SEQ)
            lanes = slice(index * HALF, (index + 1) * HALF)
            signed = signed_i[s, c, g, block].astype(F32)
            row_dot = jnp.sum(signed * dsigned, axis=0, keepdims=True)
            row_dot = row_dot * jnp.concatenate(
                [norm_i[s, c, g, e : e + 1, lanes] for e in range(2)], axis=1
            )
            dscores = slope_i[s, c, g, block].astype(F32) * dsigned - signed * row_dot
            low_pair.append(dscores.astype(BF))
        near, far = low_pair
        near_p, far_p = dot(k[:, :HALF], near), dot(k, far)
        dq = jnp.concatenate(
            [
                jnp.concatenate([near_p[:HEAD_DIM, :HALF], far_p[:HEAD_DIM, :HALF]], axis=1),
                jnp.concatenate([near_p[HEAD_DIM:, HALF:], far_p[HEAD_DIM:, HALF:]], axis=1),
            ],
            axis=0,
        )
        near_p, far_p = tail_dot(near, near_q), tail_dot(far, far_q)
        dk = jnp.concatenate([far_p[:HALF] + near_p, far_p[HALF:]], axis=0)
        near_p = tail_dot(signed_i[s, c, g, :HALF], near_m)
        far_p = tail_dot(signed_i[s, c, g, HALF:], far_m)
        dv = jnp.concatenate([far_p[:HALF] + near_p, far_p[HALF:]], axis=0)
        dq, dk, dv = (dq * scale).astype(BF), dk.astype(BF), dv.astype(BF)
        dq_o, dk_o, dv_o = outs[3 * g : 3 * g + 3]
        rows = slice(c * LANES, (c + 1) * LANES)
        dq_o[s, rows, :], dk_o[s, :, rows], dv_o[s, :, rows] = dq, dk, dv
        base = g * 4 * LANES
        gb[base + c * LANES : base + (c + 1) * LANES, :] += lane_fold(dq.astype(F32))
        for index, block in ((2, dk), (3, dv)):
            at = base + index * LANES + 8 * c
            gb[at : at + 8, :] += jnp.sum(block.astype(F32).reshape(-1, 8, LANES), axis=0)

    def weight_grads(g):
        mixed = jnp.concatenate(
            [jnp.concatenate([mixed_i[s, 0, g], mixed_i[s, 1, g]], axis=0) for s in range(seqs)], axis=1
        )
        gout[g * part : (g + 1) * part, :] += tail_dot(mixed, low)
        dq_o, dk_o, dv_o = outs[3 * g : 3 * g + 3]
        dq = jnp.concatenate([dq_o[s] for s in range(seqs)], axis=1)
        dk, dv = (jnp.concatenate([ref[s] for s in range(seqs)], axis=0) for ref in (dk_o, dv_o))
        at = 3 * g * part
        gqkv[:, at : at + part] += tail_dot(first, dq)
        gqkv[:, at + part : at + 2 * part] += dot(first, dk)
        gqkv[:, at + 2 * part : at + 3 * part] += dot(first, dv)

    order = [(s, g, c) for g in range(2) for s in range(seqs) for c in range(2)]
    made = mix_grad(0, 0)
    ready = inner(*order[0], made)
    for n, (s, g, c) in enumerate(order):
        current = ready
        if n + 1 < len(order):
            following = order[n + 1]
            if following[2] == 0:
                made = mix_grad(*following[:2])
            ready = inner(*following, made)
        outer(s, g, c, *current)
        if n == 2 * seqs:
            weight_grads(0)
    weight_grads(1)

    @pl.when(step == pl.num_programs(0) - 1)
    def _():
        for g in range(2):
            base = g * 4 * LANES
            tall = g * 4 * dim
            for c, grad_o in enumerate((own_o, other_o)):
                for index in range(3):
                    start = 3 * g * part + index * part + c * LANES
                    grad_o[tall + index * dim : tall + (index + 1) * dim, :] = gqkv[
                        :, start : start + LANES
                    ].astype(BF)
                for index in range(dim // LANES):
                    start = tall + 3 * dim + index * LANES
                    grad_o[start : start + LANES, :] = gout[
                        g * part + c * LANES : g * part + (c + 1) * LANES,
                        index * LANES : (index + 1) * LANES,
                    ].astype(BF)
                gvec_o[8 * g + c : 8 * g + c + 1, :] = as_row(
                    gb[base + c * LANES : base + (c + 1) * LANES, :]
                )
                for index in (2, 3):
                    rows = slice(base + index * LANES + 8 * c, base + index * LANES + 8 * c + 8)
                    at = 8 * g + 2 * index - 2 + c
                    gvec_o[at : at + 1, :] = jnp.sum(gb[rows, :], axis=0, keepdims=True)


def input_kernel(seqs, place, *refs):
    tok, dhid, dq0, dk0, dv0, dq1, dk1, dv1 = refs[:8]
    wq0, wq1, wk0, wk1, wv0, wv1, gain1 = refs[8:15]
    vec_ff, vec_at = refs[15:17]
    tgrad_o, whole_o, gvec_o, own_o, other_o = refs[17:22]
    gvec, vec, pack = refs[22:25]
    dim = tok.shape[1]

    @pl.when(pl.program_id(0) == 0)
    def _():
        gvec[...] = jnp.zeros_like(gvec)
        vec[...] = as_column(gain1[...])

    gain = wide(vec[...], SEQ)
    for s in range(seqs):
        rows = slice(s * SEQ, (s + 1) * SEQ)
        dnorm = None
        for c, (wq, wk, wv) in enumerate(((wq0, wk0, wv0), (wq1, wk1, wv1))):
            lanes = slice(c * LANES, (c + 1) * LANES)
            dq = jnp.concatenate([dq0[s, lanes, :], dq1[s, lanes, :]], axis=0)
            dk = jnp.concatenate([dk0[s, :, lanes], dk1[s, :, lanes]], axis=1)
            dv = jnp.concatenate([dv0[s, :, lanes], dv1[s, :, lanes]], axis=1)
            made = dot(wq[...], dq) + tail_dot(wk[...], dk) + tail_dot(wv[...], dv)
            dnorm = made if dnorm is None else dnorm + made
        plain, factor = norm_plain(tok[rows, :].astype(F32).T)
        gvec[0:dim, :] += lane_fold(dnorm * plain)
        gvec[dim : 2 * dim, :] += lane_fold(dnorm)
        tgrad = dhid[s].astype(F32) + norm_back(dnorm, plain, factor, gain)
        made = tgrad.T.astype(BF)
        tgrad_o[rows, :] = made
        whole_o[rows, :] = made

    @pl.when(pl.program_id(0) == pl.num_programs(0) - 1)
    def _():
        for index in range(2):
            gvec_o[index : index + 1, :] = as_row(gvec[index * dim : (index + 1) * dim, :])
        same = [(vec_ff, r) for r in range(4)] + [(gvec_o, 0), (gvec_o, 1)]
        units = 2 * dim
        pack[...] = jnp.zeros_like(pack)
        for c, out in enumerate((own_o, other_o)):
            rows = [ref[r : r + 1, k : k + LANES] for ref, r in same for k in range(0, dim, LANES)]
            rows += [vec_at[r : r + 1, :] for i in range(3) for r in (2 * i + c, 8 + 2 * i + c)]
            rows += [
                vec_ff[4 + r : 5 + r, k : k + LANES]
                for r in range(c * units // dim, (c + 1) * units // dim)
                for k in range(0, dim, LANES)
            ]
            for index, row in enumerate(rows):
                pack[index : index + 1, :] = row
            out[...] = pack[...].astype(BF)


def whole_vmem():
    return pl.BlockSpec(memory_space=pltpu.VMEM)


def seq_block(seqs, *dims):
    return pl.BlockSpec((seqs,) + dims, lambda i: (i,) + (0,) * len(dims))


def params():
    return pltpu.CompilerParams(
        dimension_semantics=("arbitrary",), vmem_limit_bytes=VMEM_LIMIT
    )


def prefetch(grid, in_specs, out_specs, scratch=()):
    return pltpu.PrefetchScalarGridSpec(
        num_scalar_prefetch=1, grid=grid, in_specs=in_specs, out_specs=out_specs, scratch_shapes=scratch
    )


def row_block(seqs, dim, steps):
    return pl.BlockSpec((seqs * SEQ, dim), lambda i, place: (place[0] * steps + i, 0))


def placed_seq_block(seqs, *dims):
    return pl.BlockSpec((seqs,) + dims, lambda i, place: (i,) + (0,) * len(dims))


def attn_call(place, tokens, own, weights, vectors, seqs):
    dim = tokens.shape[1]
    count = own // SEQ
    steps = count // seqs
    feat = (2, 2, LANES, SEQ)
    wide_block = (2, 2, HALF + SEQ, SEQ)
    shape = jax.ShapeDtypeStruct
    return pl.pallas_call(
        functools.partial(attn_kernel, seqs),
        grid_spec=prefetch(
            (steps,),
            [row_block(seqs, dim, steps)] + [whole_vmem()] * 13,
            [placed_seq_block(seqs, *feat)] * 4
            + [placed_seq_block(seqs, *wide_block)] * 2
            + [placed_seq_block(seqs, 2, 2, 8, SEQ)]
            + [placed_seq_block(seqs, dim, SEQ)] * 2,
            [
                pltpu.VMEM((3 * dim, dim), BF),
                pltpu.VMEM((dim, dim), BF),
                pltpu.VMEM((6 * dim, LANES), F32),
            ],
        ),
        out_shape=[shape((count,) + feat, BF)] * 4
        + [shape((count,) + wide_block, BF)] * 2
        + [shape((count, 2, 2, 8, SEQ), F32)]
        + [shape((count, dim, SEQ), BF)] * 2,
        compiler_params=params(),
        cost_estimate=pl.CostEstimate(flops=1, bytes_accessed=1, transcendentals=0),
        name="attn_forward",
    )(place, tokens, *weights, *vectors)


def grad_call(low, first, saved, weights, seqs):
    count, dim = low.shape[:2]
    steps = count // seqs
    every = lambda *dims: seq_block(seqs, 2, 2, *dims)
    shape = jax.ShapeDtypeStruct
    part = 2 * LANES
    trio = [seq_block(seqs, part, SEQ), seq_block(seqs, SEQ, part), seq_block(seqs, SEQ, part)]
    return pl.pallas_call(
        functools.partial(grad_kernel, seqs),
        grid=(steps,),
        in_specs=[seq_block(seqs, dim, SEQ)] * 2
        + [every(LANES, SEQ)] * 4
        + [every(HALF + SEQ, SEQ)] * 2
        + [every(8, SEQ)]
        + [whole_vmem()] * 2,
        out_specs=trio * 2 + [whole_vmem()] * 3,
        out_shape=[
            shape((count, part, SEQ), BF),
            shape((count, SEQ, part), BF),
            shape((count, SEQ, part), BF),
        ]
        * 2
        + [
            shape((8 * dim, LANES), BF),
            shape((8 * dim, LANES), BF),
            shape((16, LANES), F32),
        ],
        scratch_shapes=[
            pltpu.VMEM((dim, 6 * part), F32),
            pltpu.VMEM((2 * part, dim), F32),
            pltpu.VMEM((8 * LANES, LANES), F32),
        ],
        compiler_params=params(),
        cost_estimate=pl.CostEstimate(flops=1, bytes_accessed=1, transcendentals=0),
        name="attn_backward",
    )(low, first, *saved, *weights)


def input_call(place, tokens, dhidden, pieces, weights, gain1, vectors, grow, seqs):
    dim = tokens.shape[1]
    count = dhidden.shape[0]
    steps = count // seqs
    part = 2 * LANES
    trio = [
        placed_seq_block(seqs, part, SEQ),
        placed_seq_block(seqs, SEQ, part),
        placed_seq_block(seqs, SEQ, part),
    ]
    return pl.pallas_call(
        functools.partial(input_kernel, seqs),
        grid_spec=prefetch(
            (steps,),
            [row_block(seqs, dim, steps), placed_seq_block(seqs, dim, SEQ)]
            + trio * 2
            + [whole_vmem()] * 9,
            [
                pl.BlockSpec((seqs * SEQ, dim), lambda i, place: (i, 0)),
                row_block(seqs, dim, steps),
            ]
            + [whole_vmem()] * 3,
            [
                pltpu.VMEM((2 * dim, LANES), F32),
                pltpu.VMEM((dim, LANES), F32),
                pltpu.VMEM((grow, LANES), F32),
            ],
        ),
        out_shape=[
            jax.ShapeDtypeStruct((count * SEQ, dim), BF),
            jax.ShapeDtypeStruct(tokens.shape, BF),
            jax.ShapeDtypeStruct((8, dim), F32),
            jax.ShapeDtypeStruct((grow, LANES), BF),
            jax.ShapeDtypeStruct((grow, LANES), BF),
        ],
        compiler_params=params(),
        cost_estimate=pl.CostEstimate(flops=1, bytes_accessed=1, transcendentals=0),
        name="input_grad",
    )(place, tokens, dhidden, *pieces, *weights, gain1, *vectors)


def mlp_call(place, hidden, cotangent, weights, vectors, seqs, block):
    count, dim = hidden.shape[:2]
    steps = count // seqs
    units = weights[0].shape[1]
    shape = jax.ShapeDtypeStruct
    return pl.pallas_call(
        functools.partial(mlp_kernel, seqs, block),
        grid_spec=prefetch(
            (steps,),
            [placed_seq_block(seqs, dim, SEQ), row_block(seqs, dim, steps)] + [whole_vmem()] * 8,
            [placed_seq_block(seqs, 2 * units, SEQ), placed_seq_block(seqs, dim, SEQ)]
            + [whole_vmem()] * 3,
            [
                pltpu.VMEM((2 * units, dim), BF),
                pltpu.VMEM((dim + 16, 2 * units), F32),
                pltpu.VMEM((2 * units + 16, dim), F32),
                pltpu.VMEM((3 * dim, LANES), F32),
                pltpu.VMEM((2 * dim, LANES), F32),
                pltpu.VMEM((2 * units, LANES), F32),
            ],
        ),
        out_shape=[
            shape((count, 2 * units, SEQ), BF),
            shape((count, dim, SEQ), BF),
            shape((2 * units, dim), BF),
            shape((2 * units, dim), BF),
            shape((8, dim), F32),
        ],
        compiler_params=params(),
        cost_estimate=pl.CostEstimate(flops=1, bytes_accessed=1, transcendentals=0),
        name="feed_forward",
    )(place, hidden, cotangent, *weights, *vectors)


def out_call(place, hidden, act, weights, bdown, rows, seqs):
    count, dim = hidden.shape[:2]
    units = act.shape[1]
    steps = count // seqs
    return pl.pallas_call(
        functools.partial(out_kernel, seqs),
        grid_spec=prefetch(
            (steps,),
            [placed_seq_block(seqs, dim, SEQ), placed_seq_block(seqs, units, SEQ)] + [whole_vmem()] * 3,
            [
                pl.BlockSpec((seqs * SEQ, dim), lambda i, place: (i, 0)),
                row_block(seqs, dim, steps),
            ],
            [pltpu.VMEM((dim, units), BF), pltpu.VMEM((dim, LANES), F32)],
        ),
        out_shape=[
            jax.ShapeDtypeStruct((count * SEQ, dim), BF),
            jax.ShapeDtypeStruct((rows, dim), BF),
        ],
        compiler_params=params(),
        cost_estimate=pl.CostEstimate(flops=1, bytes_accessed=1, transcendentals=0),
        name="layer_out",
    )(place, hidden, act, *weights, bdown)


def ff_unpack_call(total, units):
    dim = total.shape[1]
    return pl.pallas_call(
        ff_unpack_kernel,
        in_specs=[whole_vmem()],
        out_specs=[whole_vmem()] * 2,
        out_shape=[
            jax.ShapeDtypeStruct((dim, units), F32),
            jax.ShapeDtypeStruct((units, dim), F32),
        ],
        compiler_params=pltpu.CompilerParams(vmem_limit_bytes=VMEM_LIMIT),
        name="ff_unpack",
    )(total)


def at_unpack_call(here, blocks, dim, local, sizes):
    shape = jax.ShapeDtypeStruct
    outs = [shape((dim, local), F32)] * 3 + [shape((local, dim), F32)]
    outs += [shape((1, n), F32) for n in sizes]
    return pl.pallas_call(
        at_unpack_kernel,
        in_specs=[pl.BlockSpec(memory_space=pltpu.SMEM)] + [whole_vmem()] * 4,
        out_specs=[whole_vmem()] * len(outs),
        out_shape=outs,
        scratch_shapes=[pltpu.VMEM((4,) + blocks[0].shape, BF)],
        compiler_params=pltpu.CompilerParams(vmem_limit_bytes=VMEM_LIMIT),
        name="at_unpack",
    )(here, *blocks)


def shifted(value, axis, count, shift):
    return lax.ppermute(value, axis, [(i, (i + shift) % count) for i in range(count)])


def gathered(value, count, axis):
    blocks = [value] + [shifted(value, "mp", count, -r) for r in range(1, count)]
    half = count // 2
    return [
        blocks[g * half] if half == 1 else jnp.concatenate(blocks[g * half : (g + 1) * half], axis)
        for g in range(2)
    ]


def total_of(blocks):
    total = blocks[0].astype(F32)
    for block in blocks[1:]:
        total = total + block.astype(F32)
    return total.astype(BF)


class DpSum:
    def __init__(self, count):
        self.count = count
        self.groups = []
        bit = 1
        while bit < count:
            size = min(4, count // bit)
            self.groups.append((bit, size))
            bit *= size

    def swap(self, value, distance):
        return lax.ppermute(value, "dp", [(i, i ^ distance) for i in range(self.count)])

    def place(self, bit, size):
        return (lax.axis_index("dp") // bit) % size

    def scatter(self, value, stage):
        bit, size = self.groups[stage]
        here = self.place(bit, size)
        parts = value.reshape(size, value.shape[0] // size, value.shape[1])
        pick = lambda m: lax.dynamic_index_in_dim(parts, here ^ m, 0, keepdims=False)
        return [pick(0)] + [self.swap(pick(m), m * bit) for m in range(1, size)]

    def gather(self, value, stage):
        bit, size = self.groups[stage]
        return [value] + [self.swap(value, m * bit) for m in range(1, size)]

    def join(self, blocks, stage):
        bit, size = self.groups[stage]
        here = self.place(bit, size)
        whole = jnp.zeros((size,) + blocks[0].shape, blocks[0].dtype)
        for m, block in enumerate(blocks):
            whole = lax.dynamic_update_index_in_dim(whole, block, here ^ m, 0)
        return whole.reshape(-1, blocks[0].shape[1])


def body(mp, dp, *args):
    (tokens, gain1, shift1, wq, bq, wk, bk, wv, bv, wo, bo) = args[:11]
    (gain2, shift2, wu, bu, wd, bd, cotangent) = args[11:]
    rows, dim = tokens.shape
    local = wq.shape[1]
    units = wu.shape[1]
    own = rows // mp
    per = mp // 2
    me = lax.axis_index("mp")
    place = me.astype(jnp.int32).reshape(1)
    tie = lax.optimization_barrier
    dp_sum = DpSum(dp)

    weights = []
    for w in (wq, wk, wv):
        weights += gathered(w, mp, 1)
    weights += gathered(wo, mp, 0)
    small = jnp.concatenate([bq, bk, bv, bu]).reshape(1, -1)
    smalls = [small] + [shifted(small, "mp", mp, -r) for r in range(1, mp)]
    if per > 1:
        cuts = [0, local, 2 * local, 3 * local, 3 * local + units]
        smalls = [
            jnp.concatenate(
                [
                    block[:, lo:hi]
                    for lo, hi in zip(cuts, cuts[1:])
                    for block in smalls[c * per : (c + 1) * per]
                ],
                axis=1,
            )
            for c in range(2)
        ]
    weights, smalls, wu, wd = tie((weights, smalls, wu, wd))
    mlp_weights = gathered(wu, mp, 1) + gathered(wd, mp, 0)
    gain1, shift1, bo, gain2, shift2, bd = (
        v.reshape(1, -1) for v in (gain1, shift1, bo, gain2, shift2, bd)
    )

    def filled(full, others):
        for r, block in enumerate(others, 1):
            full = lax.dynamic_update_slice_in_dim(full, block, ((me - r) % mp) * own, 0)
        return full

    def spread_out(part):
        return [shifted(part, "mp", mp, r) for r in range(1, mp)]

    def ff_piece(grad, r):
        g, j = divmod(r, per)
        if per == 1:
            return grad[g]
        up = grad[g][: per * units].reshape(-1, dim, dim)
        up = jnp.concatenate(list(up), axis=1)[:, j * units : (j + 1) * units]
        down = grad[g][per * units + j * units : per * units + (j + 1) * units]
        return jnp.concatenate([up.reshape(-1, dim), down], axis=0)

    def at_piece(grads, r):
        g, j = divmod(r, per)
        if per == 1:
            return jnp.concatenate([grad[g] for grad in grads], axis=0)
        parts = []
        for index in range(3):
            block = [grad[g][index * dim : (index + 1) * dim] for grad in grads]
            block = jnp.concatenate(block, axis=1)[:, j * local : (j + 1) * local]
            parts.append(block.reshape(-1, LANES))
        block = [grad[g][3 * dim :].reshape(-1, LANES, LANES) for grad in grads]
        block = jnp.concatenate([jnp.concatenate(list(b), axis=1) for b in block], axis=0)
        parts.append(block[j * local : (j + 1) * local].reshape(-1, LANES))
        return jnp.concatenate(parts, axis=0)

    def mp_send(piece):
        return [piece(0)] + [shifted(piece(r), "mp", mp, r) for r in range(1, mp)]

    *saved, first, hidden = attn_call(
        place, tokens, own, weights, [gain1, shift1, bo] + smalls, SEQS["attn"]
    )
    hidden, mlp_weights = tie((hidden, mlp_weights))
    act, low, *grad_ff, vec_ff = mlp_call(
        place, hidden, cotangent, mlp_weights, [gain2, shift2] + smalls, SEQS["mlp"], 512
    )
    ff = total_of(mp_send(lambda r: ff_piece(grad_ff, r)))
    low, ff = tie((low, ff))
    ff = lax.psum(ff, "dp")
    *pieces, grad_own, grad_other, vec_at = grad_call(low, first, saved, weights[6:], SEQS["grad"])
    grad_at = [grad_own, grad_other]

    def finish(low, act, grad_at):
        at = mp_send(lambda r: grad_at[r]) if per == 1 else []
        grow = -(-(6 * dim + 3 * local + units) // (16 * dp * LANES)) * 16 * dp
        tgrad, tgrad_full, vec_in, *vec_low = input_call(
            place,
            tokens,
            low,
            pieces,
            weights[:6],
            gain1,
            [vec_ff, vec_at],
            max(grow, -(-(6 * dim + 6 * LANES + 2 * dim) // LANES)),
            SEQS["input"],
        )
        at, tgrad = tie((at, tgrad))

        if per == 1:
            at = jnp.concatenate([total_of(at), total_of(mp_send(lambda r: vec_low[r]))], axis=0)
        else:
            same = jnp.concatenate([vec_ff[:4].reshape(-1), vec_in[:2].reshape(-1)])
            vec_at0, vec_at1 = vec_at[:8], vec_at[8:]
            grads = [[v[: 4 * dim] for v in grad_at], [v[4 * dim :] for v in grad_at]]
            gbup = vec_ff[4:].reshape(-1)
            bias = [
                jnp.concatenate([v[2 * i + c] for c in range(2) for v in (vec_at0, vec_at1)])
                for i in range(3)
            ]

            def all_piece(r):
                vector = jnp.concatenate(
                    [same]
                    + [b[r * local : (r + 1) * local] for b in bias]
                    + [gbup[r * units : (r + 1) * units]]
                )
                size = -(-vector.shape[0] // (16 * dp * LANES)) * (16 * dp * LANES)
                vector = jnp.pad(vector, (0, size - vector.shape[0])).reshape(-1, LANES).astype(BF)
                return jnp.concatenate([at_piece(grads, r), vector], axis=0)

            at = total_of(mp_send(all_piece))
        at = dp_sum.scatter(at, 0)
        tgrads = spread_out(tgrad)
        act, at[0], tgrad = tie((act, at[0], tgrad))
        out, out_full = out_call(
            place, hidden, act, mlp_weights[2:], bd, rows, SEQS["out"]
        )
        at, out, tgrads = tie((at, out, tgrads))
        at = total_of(at)
        stages = len(dp_sum.groups)
        for stage in range(1, stages):
            at = total_of(dp_sum.scatter(at, stage))
        outs = spread_out(out)
        tgrad_full = filled(tgrad_full, tgrads)
        at, tgrad_full = tie((at, tgrad_full))
        for stage in reversed(range(1, stages)):
            at = dp_sum.join(dp_sum.gather(at, stage), stage)
        at = dp_sum.gather(at, 0)
        out_full = filled(out_full, outs)
        at, out_full = tie((at, out_full))

        sizes = [dim] * 6 + [local] * 3 + [units]
        if per == 1 and len(at) == 4:
            here = dp_sum.place(*dp_sum.groups[0]).astype(jnp.int32) ^ jnp.arange(4, dtype=jnp.int32)
            *g_at, g0, g1, g2, g3, g4, g5, q0, q1, q2, g_bup = at_unpack_call(
                here, at, dim, local, sizes
            )
            g_qkv, g_out = g_at[:3], g_at[3]
            g_same = [v.reshape(-1) for v in (g0, g1, g2, g3, g4, g5)]
            g_bias = [v.reshape(-1) for v in (q0, q1, q2)]
            g_bup = g_bup.reshape(-1)
        else:
            at = dp_sum.join(at, 0).astype(F32)
            each = dim * local // LANES
            g_qkv = [at[i * each : (i + 1) * each].reshape(dim, local) for i in range(3)]
            g_out = at[3 * each : 4 * each].reshape(local, dim)
            vector = at[4 * each :].reshape(-1)
            parts = []
            for size in sizes:
                parts.append(vector[:size])
                vector = vector[size:]
            g_same, g_bias, g_bup = parts[:6], parts[6:9], parts[9]
        return (out_full, tgrad_full, list(g_same), list(g_qkv), list(g_bias), g_out, g_bup)

    blank = jax.eval_shape(finish, low, act, grad_at)
    out_full, tgrad_full, g_same, g_qkv, g_bias, g_out, g_bup = lax.cond(
        lax.axis_index("dp") != dp,
        finish,
        lambda *_: jax.tree.map(lambda v: jnp.zeros(v.shape, v.dtype), blank),
        low,
        act,
        grad_at,
    )
    if per == 1:
        g_up, g_down = ff_unpack_call(ff, units)
    else:
        ff = ff.astype(F32)
        g_up = ff[:units].reshape(dim, units)
        g_down = ff[units:]
    return (
        out_full,
        tgrad_full,
        g_same[4],
        g_same[5],
        g_qkv[0],
        g_bias[0],
        g_qkv[1],
        g_bias[1],
        g_qkv[2],
        g_bias[2],
        g_out,
        g_same[3],
        g_same[0],
        g_same[1],
        g_up,
        g_bup,
        g_down,
        g_same[2],
    )


def solution(mesh):
    split = P("dp", None)
    columns, some, lines = P(None, "mp"), P("mp"), P("mp", None)
    return jax.shard_map(
        functools.partial(body, mesh.shape["mp"], mesh.shape["dp"]),
        mesh=mesh,
        in_specs=(split, P(), P(), columns, some, columns, some, columns, some, lines, P())
        + (P(), P(), columns, some, lines, P(), split),
        out_specs=(split, split, P(), P(), columns, some, columns, some, columns, some, lines)
        + (P(), P(), P(), columns, some, lines, P()),
        check_vma=False,
    )
```

```python
import functools
import math

import jax
import jax.numpy as jnp
from jax import lax
from jax.experimental import pallas as pl
from jax.experimental.pallas import tpu as pltpu
from jax.sharding import PartitionSpec as P

HEAD_DIM = 64
SEQ = 256
HALF = SEQ // 2
LANES = 128
BF = jnp.bfloat16
F32 = jnp.float32
VMEM_LIMIT = 60 * 1024 * 1024
SEQS = {"attn": 4, "mlp": 2, "grad": 2, "input": 4, "out": 4}


def dot(left, right):
    return jnp.dot(left, right, preferred_element_type=F32)


def tail_dot(left, right):
    return lax.dot_general(left, right, (((1,), (1,)), ((), ())), preferred_element_type=F32)


def turned(block):
    return block.astype(F32).T.astype(BF)


def wide(column, lanes):
    return jnp.concatenate([column] * (lanes // LANES), axis=1)


def lane_fold(rows):
    total = rows[:, :LANES]
    for start in range(LANES, rows.shape[1], LANES):
        total = total + rows[:, start : start + LANES]
    return total


def as_column(row):
    return jnp.broadcast_to(row, (LANES, row.shape[1])).T


def as_row(sums):
    return jnp.sum(sums.T, axis=0, keepdims=True)


def norm_plain(x):
    center = x - jnp.mean(x, axis=0, keepdims=True)
    factor = lax.rsqrt(jnp.mean(center * center, axis=0, keepdims=True) + 1e-05)
    return center * factor, factor


def norm_back(grad, plain, factor, gain):
    scaled = grad * gain
    return factor * (
        scaled
        - jnp.mean(scaled, axis=0, keepdims=True)
        - plain * jnp.mean(scaled * plain, axis=0, keepdims=True)
    )


def upper_mask():
    return lax.broadcasted_iota(jnp.int32, (HALF, HALF), 0) <= lax.broadcasted_iota(
        jnp.int32, (HALF, HALF), 1
    )


def smooth(scores):
    square = scores * scores + 1.0
    inverse = lax.rsqrt(square)
    return inverse, square * inverse


def pair_diag(left, right):
    zero = jnp.zeros_like(left)
    return jnp.concatenate(
        [jnp.concatenate([left, zero], axis=1), jnp.concatenate([zero, right], axis=1)], axis=0
    )


def pair_near_far(rows):
    left, right = rows[:HEAD_DIM], rows[HEAD_DIM:]
    return (
        pair_diag(left[:, :HALF], right[:, :HALF]),
        pair_diag(left[:, HALF:], right[:, HALF:]),
    )


def attend(scores, mask):
    inverse, root = smooth(scores)
    if scores.shape[0] > HALF:
        diagonal = jnp.where(mask, root[HALF:], -1e30)
        magnitude = jnp.concatenate([root[:HALF], diagonal], axis=0)
    else:
        magnitude = jnp.where(mask, root, -1e30)
    top = jnp.max(magnitude, axis=0, keepdims=True)
    expo = jnp.exp(magnitude - top)
    norm = 1.0 / jnp.sum(expo, axis=0, keepdims=True)
    return (scores * inverse).astype(BF), expo.astype(BF), norm


def attn_kernel(seqs, place, *refs):
    (tok, wq0, wq1, wk0, wk1, wv0, wv1, wo0, wo1) = refs[:9]
    gain1, shift1, bout, small0, small1 = refs[9:14]
    (query_o, keys_o, values_o, mixed_o, sign_o, expo_o, norm_o, first_o, hidden_o) = refs[14:23]
    wqkv_t, wo_t, vec = refs[23:26]
    dim = tok.shape[1]
    lanes = seqs * SEQ

    @pl.when(pl.program_id(0) == 0)
    def _():
        part = dim // 2
        for index, ref in enumerate((wq0, wq1, wk0, wk1, wv0, wv1)):
            wqkv_t[index * part : (index + 1) * part, :] = turned(ref[...])
        wo_t[:, :part] = turned(wo0[...])
        wo_t[:, part:] = turned(wo1[...])
        for index, ref in ((0, gain1), (1, shift1), (5, bout)):
            vec[index * dim : (index + 1) * dim, :] = as_column(ref[...])
        for index in range(3):
            for c, ref in enumerate((small0, small1)):
                start = (2 + index) * dim + c * part
                vec[start : start + part, :] = as_column(ref[:, index * part : (index + 1) * part])

    half = lax.broadcasted_iota(jnp.int32, (HALF, SEQ), 1)
    mask = lax.broadcasted_iota(jnp.int32, (HALF, SEQ), 0) <= jnp.where(half < HALF, half, half - HALF)
    pairs = dim // LANES
    scale = jnp.asarray(1.0 / math.sqrt(HEAD_DIM), BF)

    def prepare(s):
        x = tok[s * SEQ : (s + 1) * SEQ, :].astype(F32).T
        plain, _ = norm_plain(x)
        first = (plain * wide(vec[0:dim, :], SEQ) + wide(vec[dim : 2 * dim, :], SEQ)).astype(BF)
        first_o[s] = first
        return first

    def project(s, p, first):
        c, g = divmod(p, 2)
        made = []
        for index in range(3):
            rows = slice(index * dim + p * LANES, index * dim + (p + 1) * LANES)
            bias = slice(2 * dim + rows.start, 2 * dim + rows.stop)
            made.append((dot(wqkv_t[rows, :], first) + wide(vec[bias, :], SEQ)).astype(BF))
        query, keys, values = made[0] * scale, made[1], made[2]
        query_o[s, c, g], keys_o[s, c, g], values_o[s, c, g] = query, keys, values
        near_q, far_q = pair_near_far(query)
        kp = turned(keys)
        return dot(kp[:HALF], near_q), dot(kp, far_q), values

    def mix(s, p, near_s, far_s, values):
        c, g = divmod(p, 2)
        near_t, near_e, near_n = attend(near_s, mask)
        far_t, far_e, far_n = attend(far_s, mask)
        near, far = near_t * near_e, far_t * far_e
        norms = [
            jnp.concatenate([near_n[:, lanes], far_n[:, lanes]], axis=1)
            for lanes in (slice(0, HALF), slice(HALF, SEQ))
        ]
        sign_o[s, c, g, :HALF], sign_o[s, c, g, HALF:] = near_t, far_t
        expo_o[s, c, g, :HALF], expo_o[s, c, g, HALF:] = near_e, far_e
        near_m, far_m = dot(values[:, :HALF], near), dot(values, far)
        made = jnp.concatenate(
            [
                jnp.concatenate([near_m[:HEAD_DIM, :HALF], far_m[:HEAD_DIM, :HALF]], axis=1) * norms[0],
                jnp.concatenate([near_m[HEAD_DIM:, HALF:], far_m[HEAD_DIM:, HALF:]], axis=1) * norms[1],
            ],
            axis=0,
        ).astype(BF)
        mixed_o[s, c, g] = made
        for e in range(2):
            norm_o[s, c, g, e : e + 1, :] = norms[e]
        return made

    def finish(s, mixed):
        x = tok[s * SEQ : (s + 1) * SEQ, :].astype(F32).T
        made = x + dot(wo_t[...], jnp.concatenate(mixed, axis=0)) + wide(vec[5 * dim : 6 * dim, :], SEQ)
        hidden_o[s] = made.astype(BF)

    first = prepare(0)
    ready = project(0, 0, first)
    mixed = []
    for s in range(seqs):
        done, mixed = mixed, []
        for p in range(pairs):
            current = ready
            if p == pairs // 2 and s + 1 < seqs:
                following = prepare(s + 1)
            if p + 1 < pairs:
                ready = project(s, p + 1, first)
            elif s + 1 < seqs:
                first = following
                ready = project(s + 1, 0, first)
            mixed.append(mix(s, p, *current))
            if p == 0 and s > 0:
                finish(s - 1, done)
    finish(seqs - 1, mixed)


def mlp_kernel(seqs, block, place, *refs):
    (hid, cot, wu0, wu1, wd0, wd1, gain2, shift2, small0, small1) = refs[:10]
    (act_o, low_o, own_up, own_down, other_up, other_down, gvec_o) = refs[10:17]
    wu_t, gup, gdown, gvec, vec, bup = refs[17:23]
    dim = hid.shape[1]
    units = wu0.shape[1]
    lanes = seqs * SEQ
    step = pl.program_id(0)

    @pl.when(step == 0)
    def _():
        for index, (up, small) in enumerate(((wu0, small0), (wu1, small1))):
            rows = slice(index * units, (index + 1) * units)
            wu_t[rows, :] = turned(up[...])
            bup[rows, :] = as_column(small[:, small.shape[1] - units :])
        for index, ref in enumerate((gain2, shift2)):
            vec[index * dim : (index + 1) * dim, :] = as_column(ref[...])
        gup[...] = jnp.zeros_like(gup)
        gdown[...] = jnp.zeros_like(gdown)
        gvec[...] = jnp.zeros_like(gvec)

    hidden = jnp.concatenate([hid[s] for s in range(seqs)], axis=1).astype(F32)
    grad_out = cot[...].astype(F32).T
    grad_low = grad_out.astype(BF)
    gain = wide(vec[0:dim, :], lanes)
    plain, factor = norm_plain(hidden)
    second = (plain * gain + wide(vec[dim : 2 * dim, :], lanes)).astype(BF)
    ones = jnp.ones((16, lanes), BF)
    second_ones = jnp.concatenate([second, ones], axis=0)
    dnorm = None
    for start in range(0, 2 * units, block):
        span = slice(start, start + block)
        half, inner = divmod(start, units)
        up_ref, down_ref = ((wu0, wd0), (wu1, wd1))[half]
        inner = slice(inner, inner + block)
        upper = dot(wu_t[span, :], second) + wide(bup[span, :], lanes)
        dact = dot(down_ref[inner, :], grad_low)
        part = upper * (1.0 / math.sqrt(2.0))
        cdf = 0.5 * lax.erf(part) + 0.5
        density = jnp.exp2((part * part) * (-1.0 / math.log(2.0)))
        act = (upper * cdf).astype(BF)
        dup = (dact * (cdf + part * density * (1.0 / math.sqrt(math.pi)))).astype(BF)
        for s in range(seqs):
            act_o[s, span, :] = act[:, s * SEQ : (s + 1) * SEQ]
        dn_part = dot(up_ref[:, inner], dup)
        dnorm = dn_part if dnorm is None else dnorm + dn_part
        gup[:, span] += tail_dot(second_ones, dup)
        if start == 0:
            act = jnp.concatenate([ones, act], axis=0)
            gdown[: 16 + block, :] += tail_dot(act, grad_low)
        else:
            gdown[16 + start : 16 + start + block, :] += tail_dot(act, grad_low)
    gvec[0:dim, :] += lane_fold(dnorm * plain)
    gvec[dim : 2 * dim, :] += lane_fold(dnorm)
    dhidden = grad_out + norm_back(dnorm, plain, factor, gain)
    gvec[2 * dim :, :] += lane_fold(dhidden)
    for s in range(seqs):
        low_o[s] = dhidden[:, s * SEQ : (s + 1) * SEQ].astype(BF)

    @pl.when(step == pl.num_programs(0) - 1)
    def _():
        for half, (up_o, down_o) in enumerate(((own_up, own_down), (other_up, other_down))):
            for index in range(units // dim):
                start = half * units + index * dim
                up_o[index * dim : (index + 1) * dim, :] = gup[:dim, start : start + dim].astype(BF)
            down_o[...] = gdown[16 + half * units : 16 + (half + 1) * units, :].astype(BF)
        for index, row in ((0, 0), (1, 1), (2, 3)):
            gvec_o[row : row + 1, :] = as_row(gvec[index * dim : (index + 1) * dim, :])
        gvec_o[2:3, :] = gdown[:1, :]
        for index in range(2 * units // dim):
            gvec_o[4 + index : 5 + index, :] = gup[dim : dim + 1, index * dim : (index + 1) * dim]


def out_kernel(seqs, place, hid, act, wd0, wd1, bdown, out_o, whole_o, wd_t, vec):
    units = wd0.shape[0]

    @pl.when(pl.program_id(0) == 0)
    def _():
        wd_t[:, :units] = turned(wd0[...])
        wd_t[:, units:] = turned(wd1[...])
        vec[...] = as_column(bdown[...])

    for s in range(seqs):
        rows = slice(s * SEQ, (s + 1) * SEQ)
        out = hid[s].astype(F32) + dot(wd_t[...], act[s]) + wide(vec[...], SEQ)
        made = out.T.astype(BF)
        out_o[rows, :] = made
        whole_o[rows, :] = made


def ff_unpack_kernel(up, down, up_o, down_o):
    dim, units = up_o.shape
    for start in range(0, units, dim):
        up_o[:, start : start + dim] = up[start : start + dim, :].astype(F32)
    down_o[...] = down[...].astype(F32)


def at_unpack_kernel(here, b0, b1, b2, b3, *refs):
    outs, hold = refs[:-1], refs[-1]
    size = b0.shape[0]
    for m, block in enumerate((b0, b1, b2, b3)):
        hold[here[m]] = block[...]
    rows = lambda start, count: [
        hold[k, max(start - k * size, 0) : min(start + count - k * size, size), :].astype(F32)
        for k in range(4)
        if start < (k + 1) * size and start + count > k * size
    ]
    get = lambda start, count: jnp.concatenate(rows(start, count), axis=0)
    dim = outs[0].shape[0]
    for g in range(2):
        base = g * 4 * dim
        for index in range(3):
            outs[index][:, g * LANES : (g + 1) * LANES] = get(base + index * dim, dim)
        for index in range(dim // LANES):
            outs[3][g * LANES : (g + 1) * LANES, index * LANES : (index + 1) * LANES] = get(
                base + 3 * dim + index * LANES, LANES
            )
    at = 8 * dim
    for out in outs[4:]:
        for start in range(0, out.shape[1], LANES):
            out[:, start : start + LANES] = get(at // 16 * 16, 16)[at % 16 : at % 16 + 1]
            at += 1


def grad_kernel(seqs, *refs):
    (low_i, first_i, query_i, keys_i, values_i, mixed_i, sign_i, expo_i, norm_i) = refs[:9]
    wo0, wo1 = refs[9:11]
    outs = refs[11:17]
    own_o, other_o, gvec_o = refs[17:20]
    gqkv, gout, gb = refs[20:23]
    dim = low_i.shape[1]
    part = 2 * LANES
    step = pl.program_id(0)
    scale = 1.0 / math.sqrt(HEAD_DIM)

    @pl.when(step == 0)
    def _():
        gqkv[...] = jnp.zeros_like(gqkv)
        gout[...] = jnp.zeros_like(gout)
        gb[...] = jnp.zeros_like(gb)

    first = jnp.concatenate([first_i[s] for s in range(seqs)], axis=1)
    low = jnp.concatenate([low_i[s] for s in range(seqs)], axis=1)

    def mix_grad(s, g):
        place = slice(g * LANES, (g + 1) * LANES)
        spread = lambda c, e: jnp.broadcast_to(norm_i[s, c, g, e : e + 1, :], (HEAD_DIM, SEQ))
        return [
            (
                dot(wo[place, :], low_i[s])
                * jnp.concatenate([spread(c, e) for e in range(2)], axis=0)
            ).astype(BF)
            for c, wo in enumerate((wo0, wo1))
        ]

    def inner(s, g, c, dmixed):
        dm = dmixed[c]
        v_nat = turned(values_i[s, c, g])
        near_m, far_m = pair_near_far(dm)
        return dot(v_nat[:HALF], near_m), dot(v_nat, far_m), near_m, far_m

    def outer(s, g, c, near_s, far_s, near_m, far_m):
        q, k = query_i[s, c, g], keys_i[s, c, g]
        near_q, far_q = pair_near_far(q)
        low_pair, signed_pair = [], []
        for index, dsigned in enumerate((near_s, far_s)):
            block = slice(0, HALF) if index == 0 else slice(HALF, HALF + SEQ)
            lanes = slice(index * HALF, (index + 1) * HALF)
            sign, expo = sign_i[s, c, g, block], expo_i[s, c, g, block]
            signed_pair.append(sign * expo)
            signed = signed_pair[index].astype(F32)
            square = sign * sign
            rest = jnp.maximum(1.0 - square, 1e-6)
            slope = (rest * rest * lax.rsqrt(rest) + square) * expo
            row_dot = jnp.sum(signed * dsigned, axis=0, keepdims=True)
            row_dot = row_dot * jnp.concatenate(
                [norm_i[s, c, g, e : e + 1, lanes] for e in range(2)], axis=1
            )
            dscores = slope.astype(F32) * dsigned - signed * row_dot
            low_pair.append(dscores.astype(BF))
        near, far = low_pair
        near_p, far_p = dot(k[:, :HALF], near), dot(k, far)
        dq = jnp.concatenate(
            [
                jnp.concatenate([near_p[:HEAD_DIM, :HALF], far_p[:HEAD_DIM, :HALF]], axis=1),
                jnp.concatenate([near_p[HEAD_DIM:, HALF:], far_p[HEAD_DIM:, HALF:]], axis=1),
            ],
            axis=0,
        )
        near_p, far_p = tail_dot(near, near_q), tail_dot(far, far_q)
        dk = jnp.concatenate([far_p[:HALF] + near_p, far_p[HALF:]], axis=0)
        near_p, far_p = tail_dot(signed_pair[0], near_m), tail_dot(signed_pair[1], far_m)
        dv = jnp.concatenate([far_p[:HALF] + near_p, far_p[HALF:]], axis=0)
        dq, dk, dv = (dq * scale).astype(BF), dk.astype(BF), dv.astype(BF)
        dq_o, dk_o, dv_o = outs[3 * g : 3 * g + 3]
        rows = slice(c * LANES, (c + 1) * LANES)
        dq_o[s, rows, :], dk_o[s, :, rows], dv_o[s, :, rows] = dq, dk, dv
        base = g * 4 * LANES
        gb[base + c * LANES : base + (c + 1) * LANES, :] += lane_fold(dq.astype(F32))
        for index, block in ((2, dk), (3, dv)):
            at = base + index * LANES + 8 * c
            gb[at : at + 8, :] += jnp.sum(block.astype(F32).reshape(-1, 8, LANES), axis=0)

    def weight_grads(g):
        mixed = jnp.concatenate(
            [jnp.concatenate([mixed_i[s, 0, g], mixed_i[s, 1, g]], axis=0) for s in range(seqs)], axis=1
        )
        gout[g * part : (g + 1) * part, :] += tail_dot(mixed, low)
        dq_o, dk_o, dv_o = outs[3 * g : 3 * g + 3]
        dq = jnp.concatenate([dq_o[s] for s in range(seqs)], axis=1)
        dk, dv = (jnp.concatenate([ref[s] for s in range(seqs)], axis=0) for ref in (dk_o, dv_o))
        at = 3 * g * part
        gqkv[:, at : at + part] += tail_dot(first, dq)
        gqkv[:, at + part : at + 2 * part] += dot(first, dk)
        gqkv[:, at + 2 * part : at + 3 * part] += dot(first, dv)

    order = [(s, g, c) for g in range(2) for s in range(seqs) for c in range(2)]
    made = mix_grad(0, 0)
    ready = inner(*order[0], made)
    for n, (s, g, c) in enumerate(order):
        current = ready
        if n + 1 < len(order):
            following = order[n + 1]
            if following[2] == 0:
                made = mix_grad(*following[:2])
            ready = inner(*following, made)
        outer(s, g, c, *current)
        if n == 2 * seqs:
            weight_grads(0)
    weight_grads(1)

    @pl.when(step == pl.num_programs(0) - 1)
    def _():
        for g in range(2):
            base = g * 4 * LANES
            tall = g * 4 * dim
            for c, grad_o in enumerate((own_o, other_o)):
                for index in range(3):
                    start = 3 * g * part + index * part + c * LANES
                    grad_o[tall + index * dim : tall + (index + 1) * dim, :] = gqkv[
                        :, start : start + LANES
                    ].astype(BF)
                for index in range(dim // LANES):
                    start = tall + 3 * dim + index * LANES
                    grad_o[start : start + LANES, :] = gout[
                        g * part + c * LANES : g * part + (c + 1) * LANES,
                        index * LANES : (index + 1) * LANES,
                    ].astype(BF)
                gvec_o[8 * g + c : 8 * g + c + 1, :] = as_row(
                    gb[base + c * LANES : base + (c + 1) * LANES, :]
                )
                for index in (2, 3):
                    rows = slice(base + index * LANES + 8 * c, base + index * LANES + 8 * c + 8)
                    at = 8 * g + 2 * index - 2 + c
                    gvec_o[at : at + 1, :] = jnp.sum(gb[rows, :], axis=0, keepdims=True)


def input_kernel(seqs, place, *refs):
    tok, dhid, dq0, dk0, dv0, dq1, dk1, dv1 = refs[:8]
    wq0, wq1, wk0, wk1, wv0, wv1, gain1 = refs[8:15]
    vec_ff, vec_at = refs[15:17]
    tgrad_o, whole_o, gvec_o, own_o, other_o = refs[17:22]
    gvec, vec, pack = refs[22:25]
    dim = tok.shape[1]

    @pl.when(pl.program_id(0) == 0)
    def _():
        gvec[...] = jnp.zeros_like(gvec)
        vec[...] = as_column(gain1[...])

    gain = wide(vec[...], SEQ)
    for s in range(seqs):
        rows = slice(s * SEQ, (s + 1) * SEQ)
        dnorm = None
        for c, (wq, wk, wv) in enumerate(((wq0, wk0, wv0), (wq1, wk1, wv1))):
            lanes = slice(c * LANES, (c + 1) * LANES)
            dq = jnp.concatenate([dq0[s, lanes, :], dq1[s, lanes, :]], axis=0)
            dk = jnp.concatenate([dk0[s, :, lanes], dk1[s, :, lanes]], axis=1)
            dv = jnp.concatenate([dv0[s, :, lanes], dv1[s, :, lanes]], axis=1)
            made = dot(wq[...], dq) + tail_dot(wk[...], dk) + tail_dot(wv[...], dv)
            dnorm = made if dnorm is None else dnorm + made
        plain, factor = norm_plain(tok[rows, :].astype(F32).T)
        gvec[0:dim, :] += lane_fold(dnorm * plain)
        gvec[dim : 2 * dim, :] += lane_fold(dnorm)
        tgrad = dhid[s].astype(F32) + norm_back(dnorm, plain, factor, gain)
        made = tgrad.T.astype(BF)
        tgrad_o[rows, :] = made
        whole_o[rows, :] = made

    @pl.when(pl.program_id(0) == pl.num_programs(0) - 1)
    def _():
        for index in range(2):
            gvec_o[index : index + 1, :] = as_row(gvec[index * dim : (index + 1) * dim, :])
        same = [(vec_ff, r) for r in range(4)] + [(gvec_o, 0), (gvec_o, 1)]
        units = 2 * dim
        pack[...] = jnp.zeros_like(pack)
        for c, out in enumerate((own_o, other_o)):
            rows = [ref[r : r + 1, k : k + LANES] for ref, r in same for k in range(0, dim, LANES)]
            rows += [vec_at[r : r + 1, :] for i in range(3) for r in (2 * i + c, 8 + 2 * i + c)]
            rows += [
                vec_ff[4 + r : 5 + r, k : k + LANES]
                for r in range(c * units // dim, (c + 1) * units // dim)
                for k in range(0, dim, LANES)
            ]
            for index, row in enumerate(rows):
                pack[index : index + 1, :] = row
            out[...] = pack[...].astype(BF)


def whole_vmem():
    return pl.BlockSpec(memory_space=pltpu.VMEM)


def seq_block(seqs, *dims):
    return pl.BlockSpec((seqs,) + dims, lambda i: (i,) + (0,) * len(dims))


def params():
    return pltpu.CompilerParams(
        dimension_semantics=("arbitrary",), vmem_limit_bytes=VMEM_LIMIT
    )


def prefetch(grid, in_specs, out_specs, scratch=()):
    return pltpu.PrefetchScalarGridSpec(
        num_scalar_prefetch=1, grid=grid, in_specs=in_specs, out_specs=out_specs, scratch_shapes=scratch
    )


def row_block(seqs, dim, steps):
    return pl.BlockSpec((seqs * SEQ, dim), lambda i, place: (place[0] * steps + i, 0))


def placed_seq_block(seqs, *dims):
    return pl.BlockSpec((seqs,) + dims, lambda i, place: (i,) + (0,) * len(dims))


def attn_call(place, tokens, own, weights, vectors, seqs):
    dim = tokens.shape[1]
    count = own // SEQ
    steps = count // seqs
    feat = (2, 2, LANES, SEQ)
    wide_block = (2, 2, HALF + SEQ, SEQ)
    shape = jax.ShapeDtypeStruct
    return pl.pallas_call(
        functools.partial(attn_kernel, seqs),
        grid_spec=prefetch(
            (steps,),
            [row_block(seqs, dim, steps)] + [whole_vmem()] * 13,
            [placed_seq_block(seqs, *feat)] * 4
            + [placed_seq_block(seqs, *wide_block)] * 2
            + [placed_seq_block(seqs, 2, 2, 8, SEQ)]
            + [placed_seq_block(seqs, dim, SEQ)] * 2,
            [
                pltpu.VMEM((3 * dim, dim), BF),
                pltpu.VMEM((dim, dim), BF),
                pltpu.VMEM((6 * dim, LANES), F32),
            ],
        ),
        out_shape=[shape((count,) + feat, BF)] * 4
        + [shape((count,) + wide_block, BF)] * 2
        + [shape((count, 2, 2, 8, SEQ), F32)]
        + [shape((count, dim, SEQ), BF)] * 2,
        compiler_params=params(),
        cost_estimate=pl.CostEstimate(flops=1, bytes_accessed=1, transcendentals=0),
        name="attn_forward",
    )(place, tokens, *weights, *vectors)


def grad_call(low, first, saved, weights, seqs):
    count, dim = low.shape[:2]
    steps = count // seqs
    every = lambda *dims: seq_block(seqs, 2, 2, *dims)
    shape = jax.ShapeDtypeStruct
    part = 2 * LANES
    trio = [seq_block(seqs, part, SEQ), seq_block(seqs, SEQ, part), seq_block(seqs, SEQ, part)]
    return pl.pallas_call(
        functools.partial(grad_kernel, seqs),
        grid=(steps,),
        in_specs=[seq_block(seqs, dim, SEQ)] * 2
        + [every(LANES, SEQ)] * 4
        + [every(HALF + SEQ, SEQ)] * 2
        + [every(8, SEQ)]
        + [whole_vmem()] * 2,
        out_specs=trio * 2 + [whole_vmem()] * 3,
        out_shape=[
            shape((count, part, SEQ), BF),
            shape((count, SEQ, part), BF),
            shape((count, SEQ, part), BF),
        ]
        * 2
        + [
            shape((8 * dim, LANES), BF),
            shape((8 * dim, LANES), BF),
            shape((16, LANES), F32),
        ],
        scratch_shapes=[
            pltpu.VMEM((dim, 6 * part), F32),
            pltpu.VMEM((2 * part, dim), F32),
            pltpu.VMEM((8 * LANES, LANES), F32),
        ],
        compiler_params=params(),
        cost_estimate=pl.CostEstimate(flops=1, bytes_accessed=1, transcendentals=0),
        name="attn_backward",
    )(low, first, *saved, *weights)


def input_call(place, tokens, dhidden, pieces, weights, gain1, vectors, grow, seqs):
    dim = tokens.shape[1]
    count = dhidden.shape[0]
    steps = count // seqs
    part = 2 * LANES
    trio = [
        placed_seq_block(seqs, part, SEQ),
        placed_seq_block(seqs, SEQ, part),
        placed_seq_block(seqs, SEQ, part),
    ]
    return pl.pallas_call(
        functools.partial(input_kernel, seqs),
        grid_spec=prefetch(
            (steps,),
            [row_block(seqs, dim, steps), placed_seq_block(seqs, dim, SEQ)]
            + trio * 2
            + [whole_vmem()] * 9,
            [
                pl.BlockSpec((seqs * SEQ, dim), lambda i, place: (i, 0)),
                row_block(seqs, dim, steps),
            ]
            + [whole_vmem()] * 3,
            [
                pltpu.VMEM((2 * dim, LANES), F32),
                pltpu.VMEM((dim, LANES), F32),
                pltpu.VMEM((grow, LANES), F32),
            ],
        ),
        out_shape=[
            jax.ShapeDtypeStruct((count * SEQ, dim), BF),
            jax.ShapeDtypeStruct(tokens.shape, BF),
            jax.ShapeDtypeStruct((8, dim), F32),
            jax.ShapeDtypeStruct((grow, LANES), BF),
            jax.ShapeDtypeStruct((grow, LANES), BF),
        ],
        compiler_params=params(),
        cost_estimate=pl.CostEstimate(flops=1, bytes_accessed=1, transcendentals=0),
        name="input_grad",
    )(place, tokens, dhidden, *pieces, *weights, gain1, *vectors)


def mlp_call(place, hidden, cotangent, weights, vectors, seqs, block):
    count, dim = hidden.shape[:2]
    steps = count // seqs
    units = weights[0].shape[1]
    shape = jax.ShapeDtypeStruct
    return pl.pallas_call(
        functools.partial(mlp_kernel, seqs, block),
        grid_spec=prefetch(
            (steps,),
            [placed_seq_block(seqs, dim, SEQ), row_block(seqs, dim, steps)] + [whole_vmem()] * 8,
            [placed_seq_block(seqs, 2 * units, SEQ), placed_seq_block(seqs, dim, SEQ)]
            + [whole_vmem()] * 5,
            [
                pltpu.VMEM((2 * units, dim), BF),
                pltpu.VMEM((dim + 16, 2 * units), F32),
                pltpu.VMEM((2 * units + 16, dim), F32),
                pltpu.VMEM((3 * dim, LANES), F32),
                pltpu.VMEM((2 * dim, LANES), F32),
                pltpu.VMEM((2 * units, LANES), F32),
            ],
        ),
        out_shape=[
            shape((count, 2 * units, SEQ), BF),
            shape((count, dim, SEQ), BF),
            shape((units, dim), BF),
            shape((units, dim), BF),
            shape((units, dim), BF),
            shape((units, dim), BF),
            shape((8, dim), F32),
        ],
        compiler_params=params(),
        cost_estimate=pl.CostEstimate(flops=1, bytes_accessed=1, transcendentals=0),
        name="feed_forward",
    )(place, hidden, cotangent, *weights, *vectors)


def out_call(place, hidden, act, weights, bdown, rows, seqs):
    count, dim = hidden.shape[:2]
    units = act.shape[1]
    steps = count // seqs
    return pl.pallas_call(
        functools.partial(out_kernel, seqs),
        grid_spec=prefetch(
            (steps,),
            [placed_seq_block(seqs, dim, SEQ), placed_seq_block(seqs, units, SEQ)] + [whole_vmem()] * 3,
            [
                pl.BlockSpec((seqs * SEQ, dim), lambda i, place: (i, 0)),
                row_block(seqs, dim, steps),
            ],
            [pltpu.VMEM((dim, units), BF), pltpu.VMEM((dim, LANES), F32)],
        ),
        out_shape=[
            jax.ShapeDtypeStruct((count * SEQ, dim), BF),
            jax.ShapeDtypeStruct((rows, dim), BF),
        ],
        compiler_params=params(),
        cost_estimate=pl.CostEstimate(flops=1, bytes_accessed=1, transcendentals=0),
        name="layer_out",
    )(place, hidden, act, *weights, bdown)


def ff_unpack_call(up, down):
    units, dim = up.shape
    return pl.pallas_call(
        ff_unpack_kernel,
        in_specs=[whole_vmem()] * 2,
        out_specs=[whole_vmem()] * 2,
        out_shape=[
            jax.ShapeDtypeStruct((dim, units), F32),
            jax.ShapeDtypeStruct((units, dim), F32),
        ],
        compiler_params=pltpu.CompilerParams(vmem_limit_bytes=VMEM_LIMIT),
        name="ff_unpack",
    )(up, down)


def at_unpack_call(here, blocks, dim, local, sizes):
    shape = jax.ShapeDtypeStruct
    outs = [shape((dim, local), F32)] * 3 + [shape((local, dim), F32)]
    outs += [shape((1, n), F32) for n in sizes]
    return pl.pallas_call(
        at_unpack_kernel,
        in_specs=[pl.BlockSpec(memory_space=pltpu.SMEM)] + [whole_vmem()] * 4,
        out_specs=[whole_vmem()] * len(outs),
        out_shape=outs,
        scratch_shapes=[pltpu.VMEM((4,) + blocks[0].shape, BF)],
        compiler_params=pltpu.CompilerParams(vmem_limit_bytes=VMEM_LIMIT),
        name="at_unpack",
    )(here, *blocks)


def shifted(value, axis, count, shift):
    return lax.ppermute(value, axis, [(i, (i + shift) % count) for i in range(count)])


def gathered(value, count, axis):
    blocks = [value] + [shifted(value, "mp", count, -r) for r in range(1, count)]
    half = count // 2
    return [
        blocks[g * half] if half == 1 else jnp.concatenate(blocks[g * half : (g + 1) * half], axis)
        for g in range(2)
    ]


def total_of(blocks):
    total = blocks[0].astype(F32)
    for block in blocks[1:]:
        total = total + block.astype(F32)
    return total.astype(BF)


class DpSum:
    def __init__(self, count):
        self.count = count
        self.groups = []
        bit = 1
        while bit < count:
            size = min(4, count // bit)
            self.groups.append((bit, size))
            bit *= size

    def swap(self, value, distance):
        return lax.ppermute(value, "dp", [(i, i ^ distance) for i in range(self.count)])

    def place(self, bit, size):
        return (lax.axis_index("dp") // bit) % size

    def scatter(self, value, stage):
        bit, size = self.groups[stage]
        here = self.place(bit, size)
        parts = value.reshape(size, value.shape[0] // size, value.shape[1])
        pick = lambda m: lax.dynamic_index_in_dim(parts, here ^ m, 0, keepdims=False)
        return [pick(0)] + [self.swap(pick(m), m * bit) for m in range(1, size)]

    def gather(self, value, stage):
        bit, size = self.groups[stage]
        return [value] + [self.swap(value, m * bit) for m in range(1, size)]

    def join(self, blocks, stage):
        bit, size = self.groups[stage]
        here = self.place(bit, size)
        whole = jnp.zeros((size,) + blocks[0].shape, blocks[0].dtype)
        for m, block in enumerate(blocks):
            whole = lax.dynamic_update_index_in_dim(whole, block, here ^ m, 0)
        return whole.reshape(-1, blocks[0].shape[1])


def body(mp, dp, *args):
    (tokens, gain1, shift1, wq, bq, wk, bk, wv, bv, wo, bo) = args[:11]
    (gain2, shift2, wu, bu, wd, bd, cotangent) = args[11:]
    rows, dim = tokens.shape
    local = wq.shape[1]
    units = wu.shape[1]
    own = rows // mp
    per = mp // 2
    me = lax.axis_index("mp")
    place = me.astype(jnp.int32).reshape(1)
    tie = lax.optimization_barrier
    dp_sum = DpSum(dp)

    weights = []
    for w in (wq, wk, wv):
        weights += gathered(w, mp, 1)
    weights += gathered(wo, mp, 0)
    small = jnp.concatenate([bq, bk, bv, bu]).reshape(1, -1)
    smalls = [small] + [shifted(small, "mp", mp, -r) for r in range(1, mp)]
    if per > 1:
        cuts = [0, local, 2 * local, 3 * local, 3 * local + units]
        smalls = [
            jnp.concatenate(
                [
                    block[:, lo:hi]
                    for lo, hi in zip(cuts, cuts[1:])
                    for block in smalls[c * per : (c + 1) * per]
                ],
                axis=1,
            )
            for c in range(2)
        ]
    weights, smalls, wu, wd = tie((weights, smalls, wu, wd))
    mlp_weights = gathered(wu, mp, 1) + gathered(wd, mp, 0)
    gain1, shift1, bo, gain2, shift2, bd = (
        v.reshape(1, -1) for v in (gain1, shift1, bo, gain2, shift2, bd)
    )

    def filled(full, others):
        for r, block in enumerate(others, 1):
            full = lax.dynamic_update_slice_in_dim(full, block, ((me - r) % mp) * own, 0)
        return full

    def spread_out(part):
        return [shifted(part, "mp", mp, r) for r in range(1, mp)]

    def ff_piece(grad, r):
        g, j = divmod(r, per)
        if per == 1:
            return grad[g]
        up = grad[g][: per * units].reshape(-1, dim, dim)
        up = jnp.concatenate(list(up), axis=1)[:, j * units : (j + 1) * units]
        down = grad[g][per * units + j * units : per * units + (j + 1) * units]
        return jnp.concatenate([up.reshape(-1, dim), down], axis=0)

    def at_piece(grads, r):
        g, j = divmod(r, per)
        if per == 1:
            return jnp.concatenate([grad[g] for grad in grads], axis=0)
        parts = []
        for index in range(3):
            block = [grad[g][index * dim : (index + 1) * dim] for grad in grads]
            block = jnp.concatenate(block, axis=1)[:, j * local : (j + 1) * local]
            parts.append(block.reshape(-1, LANES))
        block = [grad[g][3 * dim :].reshape(-1, LANES, LANES) for grad in grads]
        block = jnp.concatenate([jnp.concatenate(list(b), axis=1) for b in block], axis=0)
        parts.append(block[j * local : (j + 1) * local].reshape(-1, LANES))
        return jnp.concatenate(parts, axis=0)

    def mp_send(piece):
        return [piece(0)] + [shifted(piece(r), "mp", mp, r) for r in range(1, mp)]

    *saved, first, hidden = attn_call(
        place, tokens, own, weights, [gain1, shift1, bo] + smalls, SEQS["attn"]
    )
    hidden, mlp_weights = tie((hidden, mlp_weights))
    act, low, *grad_ff, vec_ff = mlp_call(
        place, hidden, cotangent, mlp_weights, [gain2, shift2] + smalls, SEQS["mlp"], 512
    )
    if per == 1:
        ff = [total_of(mp_send(lambda r: grad_ff[2 * r + k])) for k in range(2)]
    else:
        grad_ff = [jnp.concatenate(grad_ff[2 * c : 2 * c + 2], axis=0) for c in range(2)]
        ff = [total_of(mp_send(lambda r: ff_piece(grad_ff, r)))]
    low, ff = tie((low, ff))
    ff = lax.psum(ff, "dp")
    *pieces, grad_own, grad_other, vec_at = grad_call(low, first, saved, weights[6:], SEQS["grad"])
    grad_at = [grad_own, grad_other]

    def finish(low, act, grad_at):
        at = mp_send(lambda r: grad_at[r]) if per == 1 else []
        grow = -(-(6 * dim + 3 * local + units) // (16 * dp * LANES)) * 16 * dp
        tgrad, tgrad_full, vec_in, *vec_low = input_call(
            place,
            tokens,
            low,
            pieces,
            weights[:6],
            gain1,
            [vec_ff, vec_at],
            max(grow, -(-(6 * dim + 6 * LANES + 2 * dim) // LANES)),
            SEQS["input"],
        )
        at, tgrad = tie((at, tgrad))

        if per == 1:
            at = jnp.concatenate([total_of(at), total_of(mp_send(lambda r: vec_low[r]))], axis=0)
        else:
            same = jnp.concatenate([vec_ff[:4].reshape(-1), vec_in[:2].reshape(-1)])
            vec_at0, vec_at1 = vec_at[:8], vec_at[8:]
            grads = [[v[: 4 * dim] for v in grad_at], [v[4 * dim :] for v in grad_at]]
            gbup = vec_ff[4:].reshape(-1)
            bias = [
                jnp.concatenate([v[2 * i + c] for c in range(2) for v in (vec_at0, vec_at1)])
                for i in range(3)
            ]

            def all_piece(r):
                vector = jnp.concatenate(
                    [same]
                    + [b[r * local : (r + 1) * local] for b in bias]
                    + [gbup[r * units : (r + 1) * units]]
                )
                size = -(-vector.shape[0] // (16 * dp * LANES)) * (16 * dp * LANES)
                vector = jnp.pad(vector, (0, size - vector.shape[0])).reshape(-1, LANES).astype(BF)
                return jnp.concatenate([at_piece(grads, r), vector], axis=0)

            at = total_of(mp_send(all_piece))
        at = dp_sum.scatter(at, 0)
        tgrads = spread_out(tgrad)
        act, at[0], tgrad = tie((act, at[0], tgrad))
        out, out_full = out_call(
            place, hidden, act, mlp_weights[2:], bd, rows, SEQS["out"]
        )
        at, out, tgrads = tie((at, out, tgrads))
        at = total_of(at)
        stages = len(dp_sum.groups)
        for stage in range(1, stages):
            at = total_of(dp_sum.scatter(at, stage))
        outs = spread_out(out)
        tgrad_full = filled(tgrad_full, tgrads)
        at, tgrad_full = tie((at, tgrad_full))
        for stage in reversed(range(1, stages)):
            at = dp_sum.join(dp_sum.gather(at, stage), stage)
        at = dp_sum.gather(at, 0)
        out_full = filled(out_full, outs)
        at, out_full = tie((at, out_full))

        sizes = [dim] * 6 + [local] * 3 + [units]
        if per == 1 and len(at) == 4:
            here = dp_sum.place(*dp_sum.groups[0]).astype(jnp.int32) ^ jnp.arange(4, dtype=jnp.int32)
            *g_at, g0, g1, g2, g3, g4, g5, q0, q1, q2, g_bup = at_unpack_call(
                here, at, dim, local, sizes
            )
            g_qkv, g_out = g_at[:3], g_at[3]
            g_same = [v.reshape(-1) for v in (g0, g1, g2, g3, g4, g5)]
            g_bias = [v.reshape(-1) for v in (q0, q1, q2)]
            g_bup = g_bup.reshape(-1)
        else:
            at = dp_sum.join(at, 0).astype(F32)
            each = dim * local // LANES
            g_qkv = [at[i * each : (i + 1) * each].reshape(dim, local) for i in range(3)]
            g_out = at[3 * each : 4 * each].reshape(local, dim)
            vector = at[4 * each :].reshape(-1)
            parts = []
            for size in sizes:
                parts.append(vector[:size])
                vector = vector[size:]
            g_same, g_bias, g_bup = parts[:6], parts[6:9], parts[9]
        return (out_full, tgrad_full, list(g_same), list(g_qkv), list(g_bias), g_out, g_bup)

    blank = jax.eval_shape(finish, low, act, grad_at)
    out_full, tgrad_full, g_same, g_qkv, g_bias, g_out, g_bup = lax.cond(
        lax.axis_index("dp") != dp,
        finish,
        lambda *_: jax.tree.map(lambda v: jnp.zeros(v.shape, v.dtype), blank),
        low,
        act,
        grad_at,
    )
    if per == 1:
        g_up, g_down = ff_unpack_call(*ff)
    else:
        ff = ff[0].astype(F32)
        g_up = ff[:units].reshape(dim, units)
        g_down = ff[units:]
    return (
        out_full,
        tgrad_full,
        g_same[4],
        g_same[5],
        g_qkv[0],
        g_bias[0],
        g_qkv[1],
        g_bias[1],
        g_qkv[2],
        g_bias[2],
        g_out,
        g_same[3],
        g_same[0],
        g_same[1],
        g_up,
        g_bup,
        g_down,
        g_same[2],
    )


def solution(mesh):
    split = P("dp", None)
    columns, some, lines = P(None, "mp"), P("mp"), P("mp", None)
    return jax.shard_map(
        functools.partial(body, mesh.shape["mp"], mesh.shape["dp"]),
        mesh=mesh,
        in_specs=(split, P(), P(), columns, some, columns, some, columns, some, lines, P())
        + (P(), P(), columns, some, lines, P(), split),
        out_specs=(split, split, P(), P(), columns, some, columns, some, columns, some, lines)
        + (P(), P(), P(), columns, some, lines, P()),
        check_vma=False,
    )
```

```python
import functools
import math

import jax
import jax.numpy as jnp
from jax import lax
from jax.experimental import pallas as pl
from jax.experimental.pallas import tpu as pltpu
from jax.sharding import PartitionSpec as P

HEAD_DIM = 64
SEQ = 256
HALF = SEQ // 2
LANES = 128
BF = jnp.bfloat16
F32 = jnp.float32
VMEM_LIMIT = 60 * 1024 * 1024
SEQS = {"attn": 4, "mlp": 2, "grad": 2, "input": 4, "out": 4}


def dot(left, right):
    return jnp.dot(left, right, preferred_element_type=F32)


def tail_dot(left, right):
    return lax.dot_general(left, right, (((1,), (1,)), ((), ())), preferred_element_type=F32)


def turned(block):
    return block.astype(F32).T.astype(BF)


def wide(column, lanes):
    return jnp.concatenate([column] * (lanes // LANES), axis=1)


def lane_fold(rows):
    total = rows[:, :LANES]
    for start in range(LANES, rows.shape[1], LANES):
        total = total + rows[:, start : start + LANES]
    return total


def as_column(row):
    return jnp.broadcast_to(row, (LANES, row.shape[1])).T


def as_row(sums):
    return jnp.sum(sums.T, axis=0, keepdims=True)


def norm_plain(x):
    center = x - jnp.mean(x, axis=0, keepdims=True)
    factor = lax.rsqrt(jnp.mean(center * center, axis=0, keepdims=True) + 1e-05)
    return center * factor, factor


def norm_back(grad, plain, factor, gain):
    scaled = grad * gain
    return factor * (
        scaled
        - jnp.mean(scaled, axis=0, keepdims=True)
        - plain * jnp.mean(scaled * plain, axis=0, keepdims=True)
    )


def upper_mask():
    return lax.broadcasted_iota(jnp.int32, (HALF, HALF), 0) <= lax.broadcasted_iota(
        jnp.int32, (HALF, HALF), 1
    )


def smooth(scores):
    square = scores * scores + 1.0
    inverse = lax.rsqrt(square)
    return inverse, square * inverse


def pair_diag(left, right):
    zero = jnp.zeros_like(left)
    return jnp.concatenate(
        [jnp.concatenate([left, zero], axis=1), jnp.concatenate([zero, right], axis=1)], axis=0
    )


def pair_near_far(rows):
    left, right = rows[:HEAD_DIM], rows[HEAD_DIM:]
    return (
        pair_diag(left[:, :HALF], right[:, :HALF]),
        pair_diag(left[:, HALF:], right[:, HALF:]),
    )


def attend(scores, mask):
    inverse, root = smooth(scores)
    if scores.shape[0] > HALF:
        diagonal = jnp.where(mask, root[HALF:], -1e30)
        magnitude = jnp.concatenate([root[:HALF], diagonal], axis=0)
    else:
        magnitude = jnp.where(mask, root, -1e30)
    top = jnp.max(magnitude, axis=0, keepdims=True)
    expo = jnp.exp(magnitude - top)
    norm = 1.0 / jnp.sum(expo, axis=0, keepdims=True)
    return (scores * inverse).astype(BF), expo.astype(BF), norm


def attn_kernel(seqs, place, *refs):
    (tok, wq0, wq1, wk0, wk1, wv0, wv1, wo0, wo1) = refs[:9]
    gain1, shift1, bout, small0, small1 = refs[9:14]
    (query_o, keys_o, values_o, mixed_o, sign_o, expo_o, norm_o, first_o, hidden_o) = refs[14:23]
    wqkv_t, wo_t, vec = refs[23:26]
    dim = tok.shape[1]
    lanes = seqs * SEQ

    @pl.when(pl.program_id(0) == 0)
    def _():
        part = dim // 2
        for index, ref in enumerate((wq0, wq1, wk0, wk1, wv0, wv1)):
            wqkv_t[index * part : (index + 1) * part, :] = turned(ref[...])
        wo_t[:, :part] = turned(wo0[...])
        wo_t[:, part:] = turned(wo1[...])
        for index, ref in ((0, gain1), (1, shift1), (5, bout)):
            vec[index * dim : (index + 1) * dim, :] = as_column(ref[...])
        for index in range(3):
            for c, ref in enumerate((small0, small1)):
                start = (2 + index) * dim + c * part
                vec[start : start + part, :] = as_column(ref[:, index * part : (index + 1) * part])

    half = lax.broadcasted_iota(jnp.int32, (HALF, SEQ), 1)
    mask = lax.broadcasted_iota(jnp.int32, (HALF, SEQ), 0) <= jnp.where(half < HALF, half, half - HALF)
    pairs = dim // LANES
    scale = jnp.asarray(1.0 / math.sqrt(HEAD_DIM), BF)

    def prepare(s):
        x = tok[s * SEQ : (s + 1) * SEQ, :].astype(F32).T
        plain, _ = norm_plain(x)
        first = (plain * wide(vec[0:dim, :], SEQ) + wide(vec[dim : 2 * dim, :], SEQ)).astype(BF)
        first_o[s] = first
        return first

    def project(s, p, first):
        c, g = divmod(p, 2)
        made = []
        for index in range(3):
            rows = slice(index * dim + p * LANES, index * dim + (p + 1) * LANES)
            bias = slice(2 * dim + rows.start, 2 * dim + rows.stop)
            made.append((dot(wqkv_t[rows, :], first) + wide(vec[bias, :], SEQ)).astype(BF))
        query, keys, values = made[0] * scale, made[1], made[2]
        query_o[s, c, g], keys_o[s, c, g], values_o[s, c, g] = query, keys, values
        near_q, far_q = pair_near_far(query)
        kp = turned(keys)
        return dot(kp[:HALF], near_q), dot(kp, far_q), values

    def mix(s, p, near_s, far_s, values):
        c, g = divmod(p, 2)
        near_t, near_e, near_n = attend(near_s, mask)
        far_t, far_e, far_n = attend(far_s, mask)
        near, far = near_t * near_e, far_t * far_e
        norms = [
            jnp.concatenate([near_n[:, lanes], far_n[:, lanes]], axis=1)
            for lanes in (slice(0, HALF), slice(HALF, SEQ))
        ]
        sign_o[s, c, g, :HALF], sign_o[s, c, g, HALF:] = near_t, far_t
        expo_o[s, c, g, :HALF], expo_o[s, c, g, HALF:] = near_e, far_e
        near_m, far_m = dot(values[:, :HALF], near), dot(values, far)
        made = jnp.concatenate(
            [
                jnp.concatenate([near_m[:HEAD_DIM, :HALF], far_m[:HEAD_DIM, :HALF]], axis=1) * norms[0],
                jnp.concatenate([near_m[HEAD_DIM:, HALF:], far_m[HEAD_DIM:, HALF:]], axis=1) * norms[1],
            ],
            axis=0,
        ).astype(BF)
        mixed_o[s, c, g] = made
        for e in range(2):
            norm_o[s, c, g, e : e + 1, :] = norms[e]
        return made

    def finish(s, mixed):
        x = tok[s * SEQ : (s + 1) * SEQ, :].astype(F32).T
        made = x + dot(wo_t[...], jnp.concatenate(mixed, axis=0)) + wide(vec[5 * dim : 6 * dim, :], SEQ)
        hidden_o[s] = made.astype(BF)

    first = prepare(0)
    ready = project(0, 0, first)
    mixed = []
    for s in range(seqs):
        done, mixed = mixed, []
        for p in range(pairs):
            current = ready
            if p == pairs // 2 and s + 1 < seqs:
                following = prepare(s + 1)
            if p + 1 < pairs:
                ready = project(s, p + 1, first)
            elif s + 1 < seqs:
                first = following
                ready = project(s + 1, 0, first)
            mixed.append(mix(s, p, *current))
            if p == 0 and s > 0:
                finish(s - 1, done)
    finish(seqs - 1, mixed)


def mlp_kernel(seqs, block, place, *refs):
    (hid, cot, wu0, wu1, wd0, wd1, gain2, shift2, small0, small1) = refs[:10]
    (act_o, low_o, own_up, own_down, other_up, other_down, gvec_o) = refs[10:17]
    wu_t, gup, gdown, gvec, vec, bup = refs[17:23]
    dim = hid.shape[1]
    units = wu0.shape[1]
    lanes = seqs * SEQ
    step = pl.program_id(0)

    @pl.when(step == 0)
    def _():
        for index, (up, small) in enumerate(((wu0, small0), (wu1, small1))):
            rows = slice(index * units, (index + 1) * units)
            wu_t[rows, :] = turned(up[...])
            bup[rows, :] = as_column(small[:, small.shape[1] - units :])
        for index, ref in enumerate((gain2, shift2)):
            vec[index * dim : (index + 1) * dim, :] = as_column(ref[...])
        gup[...] = jnp.zeros_like(gup)
        gdown[...] = jnp.zeros_like(gdown)
        gvec[...] = jnp.zeros_like(gvec)

    hidden = jnp.concatenate([hid[s] for s in range(seqs)], axis=1).astype(F32)
    grad_out = cot[...].astype(F32).T
    grad_low = grad_out.astype(BF)
    gain = wide(vec[0:dim, :], lanes)
    plain, factor = norm_plain(hidden)
    second = (plain * gain + wide(vec[dim : 2 * dim, :], lanes)).astype(BF)
    ones = jnp.ones((16, lanes), BF)
    second_ones = jnp.concatenate([second, ones], axis=0)
    dnorm = None
    for start in range(0, 2 * units, block):
        span = slice(start, start + block)
        half, inner = divmod(start, units)
        up_ref, down_ref = ((wu0, wd0), (wu1, wd1))[half]
        inner = slice(inner, inner + block)
        upper = dot(wu_t[span, :], second) + wide(bup[span, :], lanes)
        dact = dot(down_ref[inner, :], grad_low)
        part = upper * (1.0 / math.sqrt(2.0))
        cdf = 0.5 * lax.erf(part) + 0.5
        density = jnp.exp2((part * part) * (-1.0 / math.log(2.0)))
        act = (upper * cdf).astype(BF)
        dup = (dact * (cdf + part * density * (1.0 / math.sqrt(math.pi)))).astype(BF)
        for s in range(seqs):
            act_o[s, span, :] = act[:, s * SEQ : (s + 1) * SEQ]
        dn_part = dot(up_ref[:, inner], dup)
        dnorm = dn_part if dnorm is None else dnorm + dn_part
        gup[:, span] += tail_dot(second_ones, dup)
        if start == 0:
            act = jnp.concatenate([ones, act], axis=0)
            gdown[: 16 + block, :] += tail_dot(act, grad_low)
        else:
            gdown[16 + start : 16 + start + block, :] += tail_dot(act, grad_low)
    gvec[0:dim, :] += lane_fold(dnorm * plain)
    gvec[dim : 2 * dim, :] += lane_fold(dnorm)
    dhidden = grad_out + norm_back(dnorm, plain, factor, gain)
    gvec[2 * dim :, :] += lane_fold(dhidden)
    for s in range(seqs):
        low_o[s] = dhidden[:, s * SEQ : (s + 1) * SEQ].astype(BF)

    @pl.when(step == pl.num_programs(0) - 1)
    def _():
        for half, (up_o, down_o) in enumerate(((own_up, own_down), (other_up, other_down))):
            for index in range(units // dim):
                start = half * units + index * dim
                up_o[index * dim : (index + 1) * dim, :] = gup[:dim, start : start + dim].astype(BF)
            down_o[...] = gdown[16 + half * units : 16 + (half + 1) * units, :].astype(BF)
        for index, row in ((0, 0), (1, 1), (2, 3)):
            gvec_o[row : row + 1, :] = as_row(gvec[index * dim : (index + 1) * dim, :])
        gvec_o[2:3, :] = gdown[:1, :]
        for index in range(2 * units // dim):
            gvec_o[4 + index : 5 + index, :] = gup[dim : dim + 1, index * dim : (index + 1) * dim]


def out_kernel(seqs, place, hid, act, wd0, wd1, bdown, out_o, whole_o, wd_t, vec):
    units = wd0.shape[0]

    @pl.when(pl.program_id(0) == 0)
    def _():
        wd_t[:, :units] = turned(wd0[...])
        wd_t[:, units:] = turned(wd1[...])
        vec[...] = as_column(bdown[...])

    for s in range(seqs):
        rows = slice(s * SEQ, (s + 1) * SEQ)
        out = hid[s].astype(F32) + dot(wd_t[...], act[s]) + wide(vec[...], SEQ)
        made = out.T.astype(BF)
        out_o[rows, :] = made
        whole_o[rows, :] = made


def ff_unpack_kernel(up, down, up_o, down_o):
    up_o[...] = up[...].astype(F32)
    down_o[...] = down[...].astype(F32)


def at_unpack_kernel(here, b0, b1, b2, b3, *refs):
    outs, hold = refs[:-1], refs[-1]
    size = b0.shape[0]
    for m, block in enumerate((b0, b1, b2, b3)):
        hold[here[m]] = block[...]
    rows = lambda start, count: [
        hold[k, max(start - k * size, 0) : min(start + count - k * size, size), :].astype(F32)
        for k in range(4)
        if start < (k + 1) * size and start + count > k * size
    ]
    get = lambda start, count: jnp.concatenate(rows(start, count), axis=0)
    dim = outs[0].shape[0]
    for g in range(2):
        base = g * 4 * dim
        for index in range(3):
            outs[index][:, g * LANES : (g + 1) * LANES] = get(base + index * dim, dim)
        for index in range(dim // LANES):
            outs[3][g * LANES : (g + 1) * LANES, index * LANES : (index + 1) * LANES] = get(
                base + 3 * dim + index * LANES, LANES
            )
    at = 8 * dim
    for out in outs[4:]:
        for start in range(0, out.shape[1], LANES):
            out[:, start : start + LANES] = get(at // 16 * 16, 16)[at % 16 : at % 16 + 1]
            at += 1


def grad_kernel(seqs, *refs):
    (low_i, first_i, query_i, keys_i, values_i, mixed_i, sign_i, expo_i, norm_i) = refs[:9]
    wo0, wo1 = refs[9:11]
    outs = refs[11:17]
    own_o, other_o, gvec_o = refs[17:20]
    gqkv, gout, gb = refs[20:23]
    dim = low_i.shape[1]
    part = 2 * LANES
    step = pl.program_id(0)
    scale = 1.0 / math.sqrt(HEAD_DIM)

    @pl.when(step == 0)
    def _():
        gqkv[...] = jnp.zeros_like(gqkv)
        gout[...] = jnp.zeros_like(gout)
        gb[...] = jnp.zeros_like(gb)

    first = jnp.concatenate([first_i[s] for s in range(seqs)], axis=1)
    low = jnp.concatenate([low_i[s] for s in range(seqs)], axis=1)

    def mix_grad(s, g):
        place = slice(g * LANES, (g + 1) * LANES)
        spread = lambda c, e: jnp.broadcast_to(norm_i[s, c, g, e : e + 1, :], (HEAD_DIM, SEQ))
        return [
            (
                dot(wo[place, :], low_i[s])
                * jnp.concatenate([spread(c, e) for e in range(2)], axis=0)
            ).astype(BF)
            for c, wo in enumerate((wo0, wo1))
        ]

    def inner(s, g, c, dmixed):
        dm = dmixed[c]
        v_nat = turned(values_i[s, c, g])
        near_m, far_m = pair_near_far(dm)
        return dot(v_nat[:HALF], near_m), dot(v_nat, far_m), near_m, far_m

    def outer(s, g, c, near_s, far_s, near_m, far_m):
        q, k = query_i[s, c, g], keys_i[s, c, g]
        near_q, far_q = pair_near_far(q)
        low_pair, signed_pair = [], []
        for index, dsigned in enumerate((near_s, far_s)):
            block = slice(0, HALF) if index == 0 else slice(HALF, HALF + SEQ)
            lanes = slice(index * HALF, (index + 1) * HALF)
            sign, expo = sign_i[s, c, g, block], expo_i[s, c, g, block]
            signed_pair.append(sign * expo)
            signed = signed_pair[index].astype(F32)
            square = sign * sign
            rest = jnp.maximum(1.0 - square, 1e-6)
            slope = (rest * rest * lax.rsqrt(rest) + square) * expo
            row_dot = jnp.sum(signed * dsigned, axis=0, keepdims=True)
            row_dot = row_dot * jnp.concatenate(
                [norm_i[s, c, g, e : e + 1, lanes] for e in range(2)], axis=1
            )
            dscores = slope.astype(F32) * dsigned - signed * row_dot
            low_pair.append(dscores.astype(BF))
        near, far = low_pair
        near_p, far_p = dot(k[:, :HALF], near), dot(k, far)
        dq = jnp.concatenate(
            [
                jnp.concatenate([near_p[:HEAD_DIM, :HALF], far_p[:HEAD_DIM, :HALF]], axis=1),
                jnp.concatenate([near_p[HEAD_DIM:, HALF:], far_p[HEAD_DIM:, HALF:]], axis=1),
            ],
            axis=0,
        )
        near_p, far_p = tail_dot(near, near_q), tail_dot(far, far_q)
        dk = jnp.concatenate([far_p[:HALF] + near_p, far_p[HALF:]], axis=0)
        near_p, far_p = tail_dot(signed_pair[0], near_m), tail_dot(signed_pair[1], far_m)
        dv = jnp.concatenate([far_p[:HALF] + near_p, far_p[HALF:]], axis=0)
        dq, dk, dv = (dq * scale).astype(BF), dk.astype(BF), dv.astype(BF)
        dq_o, dk_o, dv_o = outs[3 * g : 3 * g + 3]
        rows = slice(c * LANES, (c + 1) * LANES)
        dq_o[s, rows, :], dk_o[s, :, rows], dv_o[s, :, rows] = dq, dk, dv
        base = g * 4 * LANES
        gb[base + c * LANES : base + (c + 1) * LANES, :] += lane_fold(dq.astype(F32))
        for index, block in ((2, dk), (3, dv)):
            at = base + index * LANES + 8 * c
            gb[at : at + 8, :] += jnp.sum(block.astype(F32).reshape(-1, 8, LANES), axis=0)

    def weight_grads(g):
        mixed = jnp.concatenate(
            [jnp.concatenate([mixed_i[s, 0, g], mixed_i[s, 1, g]], axis=0) for s in range(seqs)], axis=1
        )
        gout[g * part : (g + 1) * part, :] += tail_dot(mixed, low)
        dq_o, dk_o, dv_o = outs[3 * g : 3 * g + 3]
        dq = jnp.concatenate([dq_o[s] for s in range(seqs)], axis=1)
        dk, dv = (jnp.concatenate([ref[s] for s in range(seqs)], axis=0) for ref in (dk_o, dv_o))
        at = 3 * g * part
        gqkv[:, at : at + part] += tail_dot(first, dq)
        gqkv[:, at + part : at + 2 * part] += dot(first, dk)
        gqkv[:, at + 2 * part : at + 3 * part] += dot(first, dv)

    order = [(s, g, c) for g in range(2) for s in range(seqs) for c in range(2)]
    made = mix_grad(0, 0)
    ready = inner(*order[0], made)
    for n, (s, g, c) in enumerate(order):
        current = ready
        if n + 1 < len(order):
            following = order[n + 1]
            if following[2] == 0:
                made = mix_grad(*following[:2])
            ready = inner(*following, made)
        outer(s, g, c, *current)
        if n == 2 * seqs:
            weight_grads(0)
    weight_grads(1)

    @pl.when(step == pl.num_programs(0) - 1)
    def _():
        for g in range(2):
            base = g * 4 * LANES
            tall = g * 4 * dim
            for c, grad_o in enumerate((own_o, other_o)):
                for index in range(3):
                    start = 3 * g * part + index * part + c * LANES
                    grad_o[tall + index * dim : tall + (index + 1) * dim, :] = gqkv[
                        :, start : start + LANES
                    ].astype(BF)
                for index in range(dim // LANES):
                    start = tall + 3 * dim + index * LANES
                    grad_o[start : start + LANES, :] = gout[
                        g * part + c * LANES : g * part + (c + 1) * LANES,
                        index * LANES : (index + 1) * LANES,
                    ].astype(BF)
                gvec_o[8 * g + c : 8 * g + c + 1, :] = as_row(
                    gb[base + c * LANES : base + (c + 1) * LANES, :]
                )
                for index in (2, 3):
                    rows = slice(base + index * LANES + 8 * c, base + index * LANES + 8 * c + 8)
                    at = 8 * g + 2 * index - 2 + c
                    gvec_o[at : at + 1, :] = jnp.sum(gb[rows, :], axis=0, keepdims=True)


def input_kernel(seqs, place, *refs):
    tok, dhid, dq0, dk0, dv0, dq1, dk1, dv1 = refs[:8]
    wq0, wq1, wk0, wk1, wv0, wv1, gain1 = refs[8:15]
    vec_ff, vec_at = refs[15:17]
    tgrad_o, whole_o, gvec_o, own_o, other_o = refs[17:22]
    gvec, vec, pack = refs[22:25]
    dim = tok.shape[1]

    @pl.when(pl.program_id(0) == 0)
    def _():
        gvec[...] = jnp.zeros_like(gvec)
        vec[...] = as_column(gain1[...])

    gain = wide(vec[...], SEQ)
    for s in range(seqs):
        rows = slice(s * SEQ, (s + 1) * SEQ)
        dnorm = None
        for c, (wq, wk, wv) in enumerate(((wq0, wk0, wv0), (wq1, wk1, wv1))):
            lanes = slice(c * LANES, (c + 1) * LANES)
            dq = jnp.concatenate([dq0[s, lanes, :], dq1[s, lanes, :]], axis=0)
            dk = jnp.concatenate([dk0[s, :, lanes], dk1[s, :, lanes]], axis=1)
            dv = jnp.concatenate([dv0[s, :, lanes], dv1[s, :, lanes]], axis=1)
            made = dot(wq[...], dq) + tail_dot(wk[...], dk) + tail_dot(wv[...], dv)
            dnorm = made if dnorm is None else dnorm + made
        plain, factor = norm_plain(tok[rows, :].astype(F32).T)
        gvec[0:dim, :] += lane_fold(dnorm * plain)
        gvec[dim : 2 * dim, :] += lane_fold(dnorm)
        tgrad = dhid[s].astype(F32) + norm_back(dnorm, plain, factor, gain)
        made = tgrad.T.astype(BF)
        tgrad_o[rows, :] = made
        whole_o[rows, :] = made

    @pl.when(pl.program_id(0) == pl.num_programs(0) - 1)
    def _():
        for index in range(2):
            gvec_o[index : index + 1, :] = as_row(gvec[index * dim : (index + 1) * dim, :])
        same = [(vec_ff, r) for r in range(4)] + [(gvec_o, 0), (gvec_o, 1)]
        units = 2 * dim
        pack[...] = jnp.zeros_like(pack)
        for c, out in enumerate((own_o, other_o)):
            rows = [ref[r : r + 1, k : k + LANES] for ref, r in same for k in range(0, dim, LANES)]
            rows += [vec_at[r : r + 1, :] for i in range(3) for r in (2 * i + c, 8 + 2 * i + c)]
            rows += [
                vec_ff[4 + r : 5 + r, k : k + LANES]
                for r in range(c * units // dim, (c + 1) * units // dim)
                for k in range(0, dim, LANES)
            ]
            for index, row in enumerate(rows):
                pack[index : index + 1, :] = row
            out[...] = pack[...].astype(BF)


def whole_vmem():
    return pl.BlockSpec(memory_space=pltpu.VMEM)


def seq_block(seqs, *dims):
    return pl.BlockSpec((seqs,) + dims, lambda i: (i,) + (0,) * len(dims))


def params():
    return pltpu.CompilerParams(
        dimension_semantics=("arbitrary",), vmem_limit_bytes=VMEM_LIMIT
    )


def prefetch(grid, in_specs, out_specs, scratch=()):
    return pltpu.PrefetchScalarGridSpec(
        num_scalar_prefetch=1, grid=grid, in_specs=in_specs, out_specs=out_specs, scratch_shapes=scratch
    )


def row_block(seqs, dim, steps):
    return pl.BlockSpec((seqs * SEQ, dim), lambda i, place: (place[0] * steps + i, 0))


def placed_seq_block(seqs, *dims):
    return pl.BlockSpec((seqs,) + dims, lambda i, place: (i,) + (0,) * len(dims))


def attn_call(place, tokens, own, weights, vectors, seqs):
    dim = tokens.shape[1]
    count = own // SEQ
    steps = count // seqs
    feat = (2, 2, LANES, SEQ)
    wide_block = (2, 2, HALF + SEQ, SEQ)
    shape = jax.ShapeDtypeStruct
    return pl.pallas_call(
        functools.partial(attn_kernel, seqs),
        grid_spec=prefetch(
            (steps,),
            [row_block(seqs, dim, steps)] + [whole_vmem()] * 13,
            [placed_seq_block(seqs, *feat)] * 4
            + [placed_seq_block(seqs, *wide_block)] * 2
            + [placed_seq_block(seqs, 2, 2, 8, SEQ)]
            + [placed_seq_block(seqs, dim, SEQ)] * 2,
            [
                pltpu.VMEM((3 * dim, dim), BF),
                pltpu.VMEM((dim, dim), BF),
                pltpu.VMEM((6 * dim, LANES), F32),
            ],
        ),
        out_shape=[shape((count,) + feat, BF)] * 4
        + [shape((count,) + wide_block, BF)] * 2
        + [shape((count, 2, 2, 8, SEQ), F32)]
        + [shape((count, dim, SEQ), BF)] * 2,
        compiler_params=params(),
        cost_estimate=pl.CostEstimate(flops=1, bytes_accessed=1, transcendentals=0),
        name="attn_forward",
    )(place, tokens, *weights, *vectors)


def grad_call(low, first, saved, weights, seqs):
    count, dim = low.shape[:2]
    steps = count // seqs
    every = lambda *dims: seq_block(seqs, 2, 2, *dims)
    shape = jax.ShapeDtypeStruct
    part = 2 * LANES
    trio = [seq_block(seqs, part, SEQ), seq_block(seqs, SEQ, part), seq_block(seqs, SEQ, part)]
    return pl.pallas_call(
        functools.partial(grad_kernel, seqs),
        grid=(steps,),
        in_specs=[seq_block(seqs, dim, SEQ)] * 2
        + [every(LANES, SEQ)] * 4
        + [every(HALF + SEQ, SEQ)] * 2
        + [every(8, SEQ)]
        + [whole_vmem()] * 2,
        out_specs=trio * 2 + [whole_vmem()] * 3,
        out_shape=[
            shape((count, part, SEQ), BF),
            shape((count, SEQ, part), BF),
            shape((count, SEQ, part), BF),
        ]
        * 2
        + [
            shape((8 * dim, LANES), BF),
            shape((8 * dim, LANES), BF),
            shape((16, LANES), F32),
        ],
        scratch_shapes=[
            pltpu.VMEM((dim, 6 * part), F32),
            pltpu.VMEM((2 * part, dim), F32),
            pltpu.VMEM((8 * LANES, LANES), F32),
        ],
        compiler_params=params(),
        cost_estimate=pl.CostEstimate(flops=1, bytes_accessed=1, transcendentals=0),
        name="attn_backward",
    )(low, first, *saved, *weights)


def input_call(place, tokens, dhidden, pieces, weights, gain1, vectors, grow, seqs):
    dim = tokens.shape[1]
    count = dhidden.shape[0]
    steps = count // seqs
    part = 2 * LANES
    trio = [
        placed_seq_block(seqs, part, SEQ),
        placed_seq_block(seqs, SEQ, part),
        placed_seq_block(seqs, SEQ, part),
    ]
    return pl.pallas_call(
        functools.partial(input_kernel, seqs),
        grid_spec=prefetch(
            (steps,),
            [row_block(seqs, dim, steps), placed_seq_block(seqs, dim, SEQ)]
            + trio * 2
            + [whole_vmem()] * 9,
            [
                pl.BlockSpec((seqs * SEQ, dim), lambda i, place: (i, 0)),
                row_block(seqs, dim, steps),
            ]
            + [whole_vmem()] * 3,
            [
                pltpu.VMEM((2 * dim, LANES), F32),
                pltpu.VMEM((dim, LANES), F32),
                pltpu.VMEM((grow, LANES), F32),
            ],
        ),
        out_shape=[
            jax.ShapeDtypeStruct((count * SEQ, dim), BF),
            jax.ShapeDtypeStruct(tokens.shape, BF),
            jax.ShapeDtypeStruct((8, dim), F32),
            jax.ShapeDtypeStruct((grow, LANES), BF),
            jax.ShapeDtypeStruct((grow, LANES), BF),
        ],
        compiler_params=params(),
        cost_estimate=pl.CostEstimate(flops=1, bytes_accessed=1, transcendentals=0),
        name="input_grad",
    )(place, tokens, dhidden, *pieces, *weights, gain1, *vectors)


def mlp_call(place, hidden, cotangent, weights, vectors, seqs, block):
    count, dim = hidden.shape[:2]
    steps = count // seqs
    units = weights[0].shape[1]
    shape = jax.ShapeDtypeStruct
    return pl.pallas_call(
        functools.partial(mlp_kernel, seqs, block),
        grid_spec=prefetch(
            (steps,),
            [placed_seq_block(seqs, dim, SEQ), row_block(seqs, dim, steps)] + [whole_vmem()] * 8,
            [placed_seq_block(seqs, 2 * units, SEQ), placed_seq_block(seqs, dim, SEQ)]
            + [whole_vmem()] * 5,
            [
                pltpu.VMEM((2 * units, dim), BF),
                pltpu.VMEM((dim + 16, 2 * units), F32),
                pltpu.VMEM((2 * units + 16, dim), F32),
                pltpu.VMEM((3 * dim, LANES), F32),
                pltpu.VMEM((2 * dim, LANES), F32),
                pltpu.VMEM((2 * units, LANES), F32),
            ],
        ),
        out_shape=[
            shape((count, 2 * units, SEQ), BF),
            shape((count, dim, SEQ), BF),
            shape((units, dim), BF),
            shape((units, dim), BF),
            shape((units, dim), BF),
            shape((units, dim), BF),
            shape((8, dim), F32),
        ],
        compiler_params=params(),
        cost_estimate=pl.CostEstimate(flops=1, bytes_accessed=1, transcendentals=0),
        name="feed_forward",
    )(place, hidden, cotangent, *weights, *vectors)


def out_call(place, hidden, act, weights, bdown, rows, seqs):
    count, dim = hidden.shape[:2]
    units = act.shape[1]
    steps = count // seqs
    return pl.pallas_call(
        functools.partial(out_kernel, seqs),
        grid_spec=prefetch(
            (steps,),
            [placed_seq_block(seqs, dim, SEQ), placed_seq_block(seqs, units, SEQ)] + [whole_vmem()] * 3,
            [
                pl.BlockSpec((seqs * SEQ, dim), lambda i, place: (i, 0)),
                row_block(seqs, dim, steps),
            ],
            [pltpu.VMEM((dim, units), BF), pltpu.VMEM((dim, LANES), F32)],
        ),
        out_shape=[
            jax.ShapeDtypeStruct((count * SEQ, dim), BF),
            jax.ShapeDtypeStruct((rows, dim), BF),
        ],
        compiler_params=params(),
        cost_estimate=pl.CostEstimate(flops=1, bytes_accessed=1, transcendentals=0),
        name="layer_out",
    )(place, hidden, act, *weights, bdown)


def ff_unpack_call(up, down):
    units, dim = up.shape
    tall = dim // SEQ
    block = pl.BlockSpec((SEQ, dim), lambda i: (i, 0))
    return pl.pallas_call(
        ff_unpack_kernel,
        grid=(units // SEQ,),
        in_specs=[block] * 2,
        out_specs=[pl.BlockSpec((SEQ, dim), lambda i: (i % tall, i // tall)), block],
        out_shape=[
            jax.ShapeDtypeStruct((dim, units), F32),
            jax.ShapeDtypeStruct((units, dim), F32),
        ],
        compiler_params=params(),
        name="ff_unpack",
    )(up, down)


def at_unpack_call(here, blocks, dim, local, sizes):
    shape = jax.ShapeDtypeStruct
    outs = [shape((dim, local), F32)] * 3 + [shape((local, dim), F32)]
    outs += [shape((1, n), F32) for n in sizes]
    return pl.pallas_call(
        at_unpack_kernel,
        in_specs=[pl.BlockSpec(memory_space=pltpu.SMEM)] + [whole_vmem()] * 4,
        out_specs=[whole_vmem()] * len(outs),
        out_shape=outs,
        scratch_shapes=[pltpu.VMEM((4,) + blocks[0].shape, BF)],
        compiler_params=pltpu.CompilerParams(vmem_limit_bytes=VMEM_LIMIT),
        name="at_unpack",
    )(here, *blocks)


def shifted(value, axis, count, shift):
    return lax.ppermute(value, axis, [(i, (i + shift) % count) for i in range(count)])


def gathered(value, count, axis):
    blocks = [value] + [shifted(value, "mp", count, -r) for r in range(1, count)]
    half = count // 2
    return [
        blocks[g * half] if half == 1 else jnp.concatenate(blocks[g * half : (g + 1) * half], axis)
        for g in range(2)
    ]


def total_of(blocks):
    total = blocks[0].astype(F32)
    for block in blocks[1:]:
        total = total + block.astype(F32)
    return total.astype(BF)


class DpSum:
    def __init__(self, count):
        self.count = count
        self.groups = []
        bit = 1
        while bit < count:
            size = min(4, count // bit)
            self.groups.append((bit, size))
            bit *= size

    def swap(self, value, distance):
        return lax.ppermute(value, "dp", [(i, i ^ distance) for i in range(self.count)])

    def place(self, bit, size):
        return (lax.axis_index("dp") // bit) % size

    def scatter(self, value, stage):
        bit, size = self.groups[stage]
        here = self.place(bit, size)
        parts = value.reshape(size, value.shape[0] // size, value.shape[1])
        pick = lambda m: lax.dynamic_index_in_dim(parts, here ^ m, 0, keepdims=False)
        return [pick(0)] + [self.swap(pick(m), m * bit) for m in range(1, size)]

    def gather(self, value, stage):
        bit, size = self.groups[stage]
        return [value] + [self.swap(value, m * bit) for m in range(1, size)]

    def join(self, blocks, stage):
        bit, size = self.groups[stage]
        here = self.place(bit, size)
        whole = jnp.zeros((size,) + blocks[0].shape, blocks[0].dtype)
        for m, block in enumerate(blocks):
            whole = lax.dynamic_update_index_in_dim(whole, block, here ^ m, 0)
        return whole.reshape(-1, blocks[0].shape[1])


def body(mp, dp, *args):
    (tokens, gain1, shift1, wq, bq, wk, bk, wv, bv, wo, bo) = args[:11]
    (gain2, shift2, wu, bu, wd, bd, cotangent) = args[11:]
    rows, dim = tokens.shape
    local = wq.shape[1]
    units = wu.shape[1]
    own = rows // mp
    per = mp // 2
    me = lax.axis_index("mp")
    place = me.astype(jnp.int32).reshape(1)
    tie = lax.optimization_barrier
    dp_sum = DpSum(dp)

    weights = []
    for w in (wq, wk, wv):
        weights += gathered(w, mp, 1)
    weights += gathered(wo, mp, 0)
    small = jnp.concatenate([bq, bk, bv, bu]).reshape(1, -1)
    smalls = [small] + [shifted(small, "mp", mp, -r) for r in range(1, mp)]
    if per > 1:
        cuts = [0, local, 2 * local, 3 * local, 3 * local + units]
        smalls = [
            jnp.concatenate(
                [
                    block[:, lo:hi]
                    for lo, hi in zip(cuts, cuts[1:])
                    for block in smalls[c * per : (c + 1) * per]
                ],
                axis=1,
            )
            for c in range(2)
        ]
    weights, smalls, wu, wd = tie((weights, smalls, wu, wd))
    mlp_weights = gathered(wu, mp, 1) + gathered(wd, mp, 0)
    gain1, shift1, bo, gain2, shift2, bd = (
        v.reshape(1, -1) for v in (gain1, shift1, bo, gain2, shift2, bd)
    )

    def filled(full, others):
        for r, block in enumerate(others, 1):
            full = lax.dynamic_update_slice_in_dim(full, block, ((me - r) % mp) * own, 0)
        return full

    def spread_out(part):
        return [shifted(part, "mp", mp, r) for r in range(1, mp)]

    def ff_piece(grad, r):
        g, j = divmod(r, per)
        if per == 1:
            return grad[g]
        up = grad[g][: per * units].reshape(-1, dim, dim)
        up = jnp.concatenate(list(up), axis=1)[:, j * units : (j + 1) * units]
        down = grad[g][per * units + j * units : per * units + (j + 1) * units]
        return jnp.concatenate([up.reshape(-1, dim), down], axis=0)

    def at_piece(grads, r):
        g, j = divmod(r, per)
        if per == 1:
            return jnp.concatenate([grad[g] for grad in grads], axis=0)
        parts = []
        for index in range(3):
            block = [grad[g][index * dim : (index + 1) * dim] for grad in grads]
            block = jnp.concatenate(block, axis=1)[:, j * local : (j + 1) * local]
            parts.append(block.reshape(-1, LANES))
        block = [grad[g][3 * dim :].reshape(-1, LANES, LANES) for grad in grads]
        block = jnp.concatenate([jnp.concatenate(list(b), axis=1) for b in block], axis=0)
        parts.append(block[j * local : (j + 1) * local].reshape(-1, LANES))
        return jnp.concatenate(parts, axis=0)

    def mp_send(piece):
        return [piece(0)] + [shifted(piece(r), "mp", mp, r) for r in range(1, mp)]

    *saved, first, hidden = attn_call(
        place, tokens, own, weights, [gain1, shift1, bo] + smalls, SEQS["attn"]
    )
    hidden, mlp_weights = tie((hidden, mlp_weights))
    act, low, *grad_ff, vec_ff = mlp_call(
        place, hidden, cotangent, mlp_weights, [gain2, shift2] + smalls, SEQS["mlp"], 512
    )
    if per == 1:
        ff = [total_of(mp_send(lambda r: grad_ff[2 * r + k])) for k in range(2)]
    else:
        grad_ff = [jnp.concatenate(grad_ff[2 * c : 2 * c + 2], axis=0) for c in range(2)]
        ff = [total_of(mp_send(lambda r: ff_piece(grad_ff, r)))]
    low, ff = tie((low, ff))
    ff = lax.psum(ff, "dp")
    *pieces, grad_own, grad_other, vec_at = grad_call(low, first, saved, weights[6:], SEQS["grad"])
    grad_at = [grad_own, grad_other]

    def finish(low, act, grad_at):
        at = mp_send(lambda r: grad_at[r]) if per == 1 else []
        grow = -(-(6 * dim + 3 * local + units) // (16 * dp * LANES)) * 16 * dp
        tgrad, tgrad_full, vec_in, *vec_low = input_call(
            place,
            tokens,
            low,
            pieces,
            weights[:6],
            gain1,
            [vec_ff, vec_at],
            max(grow, -(-(6 * dim + 6 * LANES + 2 * dim) // LANES)),
            SEQS["input"],
        )
        at, tgrad = tie((at, tgrad))

        if per == 1:
            at = jnp.concatenate([total_of(at), total_of(mp_send(lambda r: vec_low[r]))], axis=0)
        else:
            same = jnp.concatenate([vec_ff[:4].reshape(-1), vec_in[:2].reshape(-1)])
            vec_at0, vec_at1 = vec_at[:8], vec_at[8:]
            grads = [[v[: 4 * dim] for v in grad_at], [v[4 * dim :] for v in grad_at]]
            gbup = vec_ff[4:].reshape(-1)
            bias = [
                jnp.concatenate([v[2 * i + c] for c in range(2) for v in (vec_at0, vec_at1)])
                for i in range(3)
            ]

            def all_piece(r):
                vector = jnp.concatenate(
                    [same]
                    + [b[r * local : (r + 1) * local] for b in bias]
                    + [gbup[r * units : (r + 1) * units]]
                )
                size = -(-vector.shape[0] // (16 * dp * LANES)) * (16 * dp * LANES)
                vector = jnp.pad(vector, (0, size - vector.shape[0])).reshape(-1, LANES).astype(BF)
                return jnp.concatenate([at_piece(grads, r), vector], axis=0)

            at = total_of(mp_send(all_piece))
        at = dp_sum.scatter(at, 0)
        tgrads = spread_out(tgrad)
        act, at[0], tgrad = tie((act, at[0], tgrad))
        out, out_full = out_call(
            place, hidden, act, mlp_weights[2:], bd, rows, SEQS["out"]
        )
        at, out, tgrads = tie((at, out, tgrads))
        at = total_of(at)
        stages = len(dp_sum.groups)
        for stage in range(1, stages):
            at = total_of(dp_sum.scatter(at, stage))
        outs = spread_out(out)
        tgrad_full = filled(tgrad_full, tgrads)
        at, tgrad_full = tie((at, tgrad_full))
        for stage in reversed(range(1, stages)):
            at = dp_sum.join(dp_sum.gather(at, stage), stage)
        at = dp_sum.gather(at, 0)
        out_full = filled(out_full, outs)
        at, out_full = tie((at, out_full))

        sizes = [dim] * 6 + [local] * 3 + [units]
        if per == 1 and len(at) == 4:
            here = dp_sum.place(*dp_sum.groups[0]).astype(jnp.int32) ^ jnp.arange(4, dtype=jnp.int32)
            *g_at, g0, g1, g2, g3, g4, g5, q0, q1, q2, g_bup = at_unpack_call(
                here, at, dim, local, sizes
            )
            g_qkv, g_out = g_at[:3], g_at[3]
            g_same = [v.reshape(-1) for v in (g0, g1, g2, g3, g4, g5)]
            g_bias = [v.reshape(-1) for v in (q0, q1, q2)]
            g_bup = g_bup.reshape(-1)
        else:
            at = dp_sum.join(at, 0).astype(F32)
            each = dim * local // LANES
            g_qkv = [at[i * each : (i + 1) * each].reshape(dim, local) for i in range(3)]
            g_out = at[3 * each : 4 * each].reshape(local, dim)
            vector = at[4 * each :].reshape(-1)
            parts = []
            for size in sizes:
                parts.append(vector[:size])
                vector = vector[size:]
            g_same, g_bias, g_bup = parts[:6], parts[6:9], parts[9]
        return (out_full, tgrad_full, list(g_same), list(g_qkv), list(g_bias), g_out, g_bup)

    blank = jax.eval_shape(finish, low, act, grad_at)
    out_full, tgrad_full, g_same, g_qkv, g_bias, g_out, g_bup = lax.cond(
        lax.axis_index("dp") != dp,
        finish,
        lambda *_: jax.tree.map(lambda v: jnp.zeros(v.shape, v.dtype), blank),
        low,
        act,
        grad_at,
    )
    if per == 1:
        g_up, g_down = ff_unpack_call(*ff)
    else:
        ff = ff[0].astype(F32)
        g_up = ff[:units].reshape(dim, units)
        g_down = ff[units:]
    return (
        out_full,
        tgrad_full,
        g_same[4],
        g_same[5],
        g_qkv[0],
        g_bias[0],
        g_qkv[1],
        g_bias[1],
        g_qkv[2],
        g_bias[2],
        g_out,
        g_same[3],
        g_same[0],
        g_same[1],
        g_up,
        g_bup,
        g_down,
        g_same[2],
    )


def solution(mesh):
    split = P("dp", None)
    columns, some, lines = P(None, "mp"), P("mp"), P("mp", None)
    return jax.shard_map(
        functools.partial(body, mesh.shape["mp"], mesh.shape["dp"]),
        mesh=mesh,
        in_specs=(split, P(), P(), columns, some, columns, some, columns, some, lines, P())
        + (P(), P(), columns, some, lines, P(), split),
        out_specs=(split, split, P(), P(), columns, some, columns, some, columns, some, lines)
        + (P(), P(), P(), columns, some, lines, P()),
        check_vma=False,
    )
```
